32 devices in a mesh: seq: 16 (over z, x, core), blk: 2 (over y).
Axes of the slice: x: 2, y: 2, z: 4, core: 2. Of those that a mesh axis runs over, the one named last changes fastest.
Arguments:
- tokens: bfloat16 [16, 1024, 768], P('seq', 'blk'), may hold values from -6 to 6
- lengths: int32 [16, 4], P('seq'), may hold values from 32 to 768, as said below
- padding: int32 [16, 1024], P('seq', 'blk'), may hold values 0 or 1
- cotangent: bfloat16 [16, 1024, 768], P('seq', 'blk'), may hold values from -6 to 6
- ln1_gain: float32 [768], replicated, may hold values from 0.5 to 1.5
- ln1_bias: float32 [768], replicated, may hold values from -1 to 1
- w_qkv: bfloat16 [768, 2304], replicated, may hold values from -0.21875 to 0.21875
- q_bias: float32 [768], replicated, may hold values from -3 to 3
- v_bias: float32 [768], replicated, may hold values from -3 to 3
- w_out: bfloat16 [768, 768], replicated, may hold values from -6 to 6
- out_bias: float32 [768], replicated, may hold values from -2 to 2
- ln2_gain: float32 [768], replicated, may hold values from 0.5 to 1.5
- ln2_bias: float32 [768], replicated, may hold values from -1 to 1
- w_fc1: bfloat16 [768, 3072], replicated, may hold values from -0.21875 to 0.21875
- fc1_bias: float32 [3072], replicated, may hold values from -3 to 3
- w_fc2: bfloat16 [3072, 768], replicated, may hold values from -0.109375 to 0.109375
- fc2_bias: float32 [768], replicated, may hold values from -2 to 2
Outputs:
- result: bfloat16 [16, 1024, 768], P('seq', 'blk')
- grad_tokens: bfloat16 [16, 1024, 768], P('seq', 'blk')
- grad_ln1_gain: float32 [768], P(('seq', 'blk'))
- grad_ln1_bias: float32 [768], P(('seq', 'blk'))
- grad_w_qkv: float32 [768, 2304], P(('seq', 'blk'))
- grad_q_bias: float32 [768], P(('seq', 'blk'))
- grad_v_bias: float32 [768], P(('seq', 'blk'))
- grad_w_out: float32 [768, 768], P(('seq', 'blk'))
- grad_out_bias: float32 [768], P(('seq', 'blk'))
- grad_ln2_gain: float32 [768], P(('seq', 'blk'))
- grad_ln2_bias: float32 [768], P(('seq', 'blk'))
- grad_w_fc1: float32 [768, 3072], P(('seq', 'blk'))
- grad_fc1_bias: float32 [3072], P(('seq', 'blk'))
- grad_w_fc2: float32 [3072, 768], P(('seq', 'blk'))
- grad_fc2_bias: float32 [768], P(('seq', 'blk'))
The draws below stay inside these ranges and needn't reach their ends.
Inputs may be any that keep to these rules, and one draw needn't show every extreme that they name: In each packed sequence the 4 clip lengths sum to 1024; one clip, a long video whose visible patches fill 1024 - 512 // 2 tokens, stands at a place drawn from the seed, and three short clips share the remaining 512 // 2.
All inputs are finite; a program needn't handle non-finite values. No bound on the sum of `padding` on one device may be relied on, other than what follows from the above.
Results may differ from the reference program's by a relative error of at most 0.014.
Values may be sent and summed in bfloat16 or wider, within the bound.
A program may use at most 256 MiB of HBM per device.

```python
import jax
import jax.numpy as jnp
from jax import lax

D = 768
FF = 3072
HEADS = 12
HEAD_DIM = 64
TOK_DEV = 512
SEQ_LEN = 1024
PACKS = 16
N_BLK = 2


def draw_lengths(key, part):
    key = jax.random.fold_in(key, 7)
    spare = TOK_DEV // 2
    lowest = max(1, spare // 8)
    highest = 3 * spare // 8 + 1

    def one_pack(pack_key):
        first_key, second_key, order_key = jax.random.split(pack_key, 3)
        first_len = jax.random.randint(first_key, (), lowest, highest, dtype=jnp.int32)
        second_len = jax.random.randint(second_key, (), lowest, highest, dtype=jnp.int32)
        third_len = jnp.int32(spare) - first_len - second_len
        row = jnp.stack([jnp.int32(SEQ_LEN - spare), first_len, second_len, third_len]).astype(jnp.int32)
        return row[jax.random.permutation(order_key, 4)]
    return jax.vmap(one_pack)(jax.random.split(key, PACKS))


def touch_ends(entries, own_key, smallest, largest):
    spot = [jax.random.randint(jax.random.fold_in(own_key, axis), (), 0, length) for axis, length in enumerate(entries.shape)]
    main_axis = entries.shape.index(max(entries.shape))
    beside = spot[:main_axis] + [(spot[main_axis] + 1) % entries.shape[main_axis]] + spot[main_axis + 1:]
    return entries.at[tuple(spot)].set(smallest).at[tuple(beside)].set(largest)


def shard_levels(stream_key, dims, cuts, low, largest):
    def one(dim, shards_of):
        heights = jax.random.uniform(jax.random.fold_in(jax.random.fold_in(stream_key, 6), dim), (shards_of,), jnp.float32, low / len(cuts), largest / len(cuts))
        return jnp.repeat(jnp.exp(heights), dims[dim] // shards_of).reshape((-1,) + (1,) * (len(dims) - dim - 1))

    loudness = one(*cuts[0])
    for cut in cuts[1:]:
        loudness = loudness * one(*cut)
    return loudness


def gaussian(stream_key, extent, scale, limit, cuts=(), kind=jnp.bfloat16):
    values = scale * jax.random.normal(stream_key, extent, jnp.float32)
    if cuts:
        values = values * shard_levels(stream_key, extent, cuts, -0.22, 0.18)
    return jnp.clip(values, -limit, limit).astype(kind)


def setup_inputs(seed: int = 0) -> dict:
    key_of = jax.random.split(jax.random.key(seed), 18)
    tokens = gaussian(key_of[0], (PACKS, SEQ_LEN, D), 1.0, 6.0, ((0, 16), (1, 2)))
    lengths = draw_lengths(jax.random.fold_in(key_of[17], 71), 0)
    padding = touch_ends((jax.random.randint(key_of[2], (PACKS, SEQ_LEN), 0, 8) < 1).astype(jnp.int32), jax.random.fold_in(key_of[2], 1), 0, 1)
    cotangent = gaussian(key_of[3], (PACKS, SEQ_LEN, D), 1.0, 6.0, ((0, 16), (1, 2)))
    ln1_gain = jnp.clip(1.0 + 0.1 * jax.random.normal(key_of[4], (D,), jnp.float32), 0.5, 1.5)
    ln1_bias = gaussian(key_of[5], (D,), 0.2, 1.0, (), jnp.float32)
    w_qkv = gaussian(key_of[6], (D, 3 * D), D ** -0.5, 0.21875)
    q_bias = gaussian(key_of[7], (D,), 0.5, 3.0, (), jnp.float32)
    v_bias = gaussian(key_of[8], (D,), 0.5, 3.0, (), jnp.float32)
    w_out = gaussian(key_of[9], (D, D), (max(1, 2 * D // SEQ_LEN)) ** -0.5, 6.0)
    out_bias = gaussian(key_of[10], (D,), 0.3, 2.0, (), jnp.float32)
    ln2_gain = jnp.clip(1.0 + 0.1 * jax.random.normal(key_of[11], (D,), jnp.float32), 0.5, 1.5)
    ln2_bias = gaussian(key_of[12], (D,), 0.2, 1.0, (), jnp.float32)
    w_fc1 = gaussian(key_of[13], (D, FF), D ** -0.5, 0.21875)
    fc1_bias = gaussian(key_of[14], (FF,), 0.5, 3.0, (), jnp.float32)
    w_fc2 = gaussian(key_of[15], (FF, D), FF ** -0.5, 0.109375)
    fc2_bias = gaussian(key_of[16], (D,), 0.3, 2.0, (), jnp.float32)
    return dict(tokens=tokens, lengths=lengths, padding=padding, cotangent=cotangent, ln1_gain=ln1_gain, ln1_bias=ln1_bias, w_qkv=w_qkv, q_bias=q_bias, v_bias=v_bias, w_out=w_out, out_bias=out_bias, ln2_gain=ln2_gain, ln2_bias=ln2_bias, w_fc1=w_fc1, fc1_bias=fc1_bias, w_fc2=w_fc2, fc2_bias=fc2_bias)


@jax.custom_vjp
def low(v):
    return lax.optimization_barrier(v.astype(jnp.bfloat16)).astype(jnp.float32)

@jax.custom_vjp
def low_back(v):
    return v

def low_keep(v):
    return (low(v), None)

def low_pass(kept, grad):
    return (grad,)

def back_keep(v):
    return (v, None)

def back_low(kept, grad):
    return (low(grad),)
low.defvjp(low_keep, low_pass)
low_back.defvjp(back_keep, back_low)
epsilon = 1e-06
score_scale = 0.125
masked_score = -1e+30

def clip_numbers(clip_lengths, positions):
    bounds = jnp.cumsum(clip_lengths).astype(jnp.int32)
    return lax.optimization_barrier(jnp.sum((positions[:, None] >= bounds[None, :]).astype(jnp.int32), axis=1)).astype(jnp.int32)

def normalize(values, scales, offset):
    center = values - lax.optimization_barrier(jnp.mean(values, axis=-1, keepdims=True))
    spread = lax.optimization_barrier(jnp.mean(center * center, axis=-1, keepdims=True))
    return center * lax.rsqrt(spread + epsilon) * scales + offset

def layer_fwd(tokens_f32, clip_ids, key_tags, positions, params):
    ln1_gain, ln1_bias, w_qkv, q_bias, v_bias, w_out, out_bias, ln2_gain, ln2_bias, w_fc1, fc1_bias, w_fc2, fc2_bias = params
    highest = lax.Precision.HIGHEST
    normed_one = low(normalize(tokens_f32, ln1_gain, ln1_bias))
    joint_bias = jnp.concatenate([q_bias, jnp.zeros_like(q_bias), v_bias])
    projected = low(low_back(jnp.dot(normed_one, w_qkv, precision=highest) + joint_bias))
    queries = projected[:, :D].reshape(SEQ_LEN, HEADS, HEAD_DIM)
    keys_all = projected[:, D:2 * D].reshape(SEQ_LEN, HEADS, HEAD_DIM)
    values_all = projected[:, 2 * D:].reshape(SEQ_LEN, HEADS, HEAD_DIM)

    def query_block(block_args):
        block_queries, block_clips, block_pos = block_args
        scores = low_back(jnp.einsum('qhd,khd->qhk', block_queries, keys_all, precision=highest) * score_scale)
        allowed = (key_tags[None, :] == block_clips[:, None]) | (block_pos[:, None] == positions[None, :])
        scores = jnp.where(allowed[:, None, :], scores, masked_score)
        attn_probs = low(jax.nn.softmax(scores, axis=-1))
        return jnp.einsum('qhk,khd->qhd', attn_probs, values_all, precision=highest)
    mixed = lax.map(jax.checkpoint(query_block), (queries.reshape(N_BLK, TOK_DEV, HEADS, HEAD_DIM), clip_ids.reshape(N_BLK, TOK_DEV), positions.reshape(N_BLK, TOK_DEV)))
    mixed = low(low_back(mixed.reshape(SEQ_LEN, D)))
    branch = low_back(jnp.dot(mixed, w_out, precision=highest) + out_bias)
    residual = tokens_f32 + branch
    normed_two = low(normalize(residual, ln2_gain, ln2_bias))
    pre_gelu = low_back(jnp.dot(normed_two, w_fc1, precision=highest) + fc1_bias)
    activated = low(jax.nn.gelu(pre_gelu, approximate=False))
    return residual + jnp.dot(activated, w_fc2, precision=highest) + fc2_bias

def reference(tokens, lengths, padding, cotangent, ln1_gain, ln1_bias, w_qkv, q_bias, v_bias, w_out, out_bias, ln2_gain, ln2_bias, w_fc1, fc1_bias, w_fc2, fc2_bias):
    params = (ln1_gain.astype(jnp.float32), ln1_bias.astype(jnp.float32), w_qkv.astype(jnp.float32), q_bias.astype(jnp.float32), v_bias.astype(jnp.float32), w_out.astype(jnp.float32), out_bias.astype(jnp.float32), ln2_gain.astype(jnp.float32), ln2_bias.astype(jnp.float32), w_fc1.astype(jnp.float32), fc1_bias.astype(jnp.float32), w_fc2.astype(jnp.float32), fc2_bias.astype(jnp.float32))
    positions = jnp.arange(SEQ_LEN, dtype=jnp.int32)

    def one_pack(totals, pack_args):
        pack_tokens, pack_lengths, pack_padding, pack_cot = pack_args
        clip_ids = clip_numbers(pack_lengths, positions)
        key_tags = jnp.where(pack_padding == 1, -1, clip_ids).astype(jnp.int32)

        def forward(tokens_f32, weights):
            return layer_fwd(tokens_f32, clip_ids, key_tags, positions, weights)
        result, pull_back = jax.vjp(forward, pack_tokens.astype(jnp.float32), params)
        grad_input, grad_weights = pull_back(pack_cot.astype(jnp.float32))
        totals = tuple((summed + weight_grad for summed, weight_grad in zip(totals, grad_weights)))
        return (totals, (result.astype(jnp.bfloat16), grad_input.astype(jnp.bfloat16)))
    start_totals = tuple((jnp.zeros_like(weight) for weight in params))
    totals, (result, grad_tokens) = lax.scan(one_pack, start_totals, (tokens, lengths, padding, cotangent))
    return (result, grad_tokens, totals[0], totals[1], totals[2], totals[3], totals[4], totals[5], totals[6], totals[7], totals[8], totals[9], totals[10], totals[11], totals[12])
```

```python
import jax
import jax.numpy as jnp
from jax import lax
from jax.sharding import PartitionSpec as P

D = 768
FF = 3072
HEADS = 12
HEAD_DIM = 64


epsilon = 1e-06
score_scale = 0.125
masked_score = -1e30


def clip_numbers(clip_lengths, positions):
    bounds = jnp.cumsum(clip_lengths)
    return jnp.sum((positions[:, None] >= bounds[None, :]).astype(jnp.int32), axis=1)


def normalize(values, scales, offset):
    center = values - jnp.mean(values, axis=-1, keepdims=True)
    spread = jnp.mean(center * center, axis=-1, keepdims=True)
    inverse = lax.rsqrt(spread + epsilon)
    unit = center * inverse
    return (unit * scales + offset, unit, inverse)


def norm_back(upstream, unit, inverse, scales):
    scaled = upstream * scales
    return inverse * (
        scaled
        - jnp.mean(scaled, axis=-1, keepdims=True)
        - unit * jnp.mean(scaled * unit, axis=-1, keepdims=True)
    )


def gelu_slope(pre_gelu):
    cdf_part = 0.5 * (1.0 + lax.erf(pre_gelu * 0.7071067811865476))
    return cdf_part + pre_gelu * jnp.exp(-0.5 * pre_gelu * pre_gelu) * 0.3989422804014327


def masked_scores(query_heads, key_heads, clip_ids, positions, block_tags, key_pos):
    raw_scores = (
        jnp.einsum("qhd,khd->qhk", query_heads, key_heads, preferred_element_type=jnp.float32)
        * score_scale
    )
    allowed = (block_tags[None, :] == clip_ids[:, None]) | (positions[:, None] == key_pos[None, :])
    return jnp.where(allowed[:, None, :], raw_scores, masked_score)


def score_grads(
    query_heads,
    key_heads,
    value_heads,
    grad_heads,
    log_total,
    row_delta,
    clip_ids,
    positions,
    block_tags,
    key_pos,
):
    scores = masked_scores(query_heads, key_heads, clip_ids, positions, block_tags, key_pos)
    attn_probs = jnp.exp(scores - log_total[..., None])
    grad_probs = jnp.einsum(
        "qhd,khd->qhk", grad_heads, value_heads, preferred_element_type=jnp.float32
    )
    grad_scores = (attn_probs * (grad_probs - row_delta[..., None])).astype(jnp.bfloat16)
    return (attn_probs, grad_scores)


def stage_orders():
    seq_bits = lax.axis_size("seq").bit_length() - 1
    blk_bits = lax.axis_size("blk").bit_length() - 1
    seq_stages = [blk_bits + b for b in range(seq_bits)]
    blk_stages = list(range(blk_bits))
    one = seq_stages[:2] + blk_stages + seq_stages[2:]
    two = seq_stages[:1] + blk_stages + seq_stages[1:]
    return one, two


def scatter_stages(terms, order):
    n_dev = terms.shape[0]
    bits = n_dev.bit_length() - 1
    me = lax.axis_index("seq") * lax.axis_size("blk") + lax.axis_index("blk")
    rest = terms.shape[1:]
    kind = terms.dtype
    held = terms.reshape((2,) * bits + rest)
    for number, bit in enumerate(order):
        axis = bits - 1 - bit
        mine = (me >> bit) & 1
        sent = lax.dynamic_slice_in_dim(held, 1 - mine, 1, axis)
        kept = lax.dynamic_slice_in_dim(held, mine, 1, axis)
        swap = [(i, i ^ (1 << bit)) for i in range(n_dev)]
        came = lax.ppermute(sent, ("seq", "blk"), swap)
        total = kept.astype(jnp.float32) + came.astype(jnp.float32)
        held = total if number == bits - 1 else total.astype(kind)
    return held.reshape((1,) + rest)


def scatter_sum(grad):
    n_dev = lax.axis_size("seq") * lax.axis_size("blk")
    rows, width = grad.shape
    terms = grad.astype(jnp.bfloat16).reshape(n_dev, rows // n_dev, width)
    one, two = stage_orders()
    left = scatter_stages(terms[:, :, : width // 2], one)[0]
    right = scatter_stages(terms[:, :, width // 2 :], two)[0]
    return jnp.concatenate([left, right], axis=1)


def body(
    tokens,
    lengths,
    padding,
    cotangent,
    ln1_gain,
    ln1_bias,
    w_qkv,
    q_bias,
    v_bias,
    w_out,
    out_bias,
    ln2_gain,
    ln2_bias,
    w_fc1,
    fc1_bias,
    w_fc2,
    fc2_bias,
):
    tok_rows = tokens.shape[1]
    group_size = lax.axis_size("blk")
    n_dev = lax.axis_size("seq") * group_size
    positions = lax.axis_index("blk") * tok_rows + jnp.arange(tok_rows, dtype=jnp.int32)
    clip_ids = clip_numbers(lengths[0], positions)
    key_tags = jnp.where(padding[0] == 1, -1, clip_ids)
    tokens_f32 = tokens[0].astype(jnp.float32)
    first_norm, unit_one, inverse_one = normalize(tokens_f32, ln1_gain, ln1_bias)
    normed_one = first_norm.astype(jnp.bfloat16)
    joint_bias = jnp.concatenate([q_bias, jnp.zeros_like(q_bias), v_bias])
    projected = (
        jnp.dot(normed_one, w_qkv, preferred_element_type=jnp.float32) + joint_bias
    ).astype(jnp.bfloat16)
    keys_own = projected[:, D : 2 * D]
    values_own = projected[:, 2 * D :]
    query_heads = projected[:, :D].reshape(tok_rows, HEADS, HEAD_DIM)
    starts = jnp.arange(group_size, dtype=jnp.int32) * tok_rows

    def fold_keys(running, key_block, offset):
        block_keys, block_values, block_tags = key_block
        key_count = block_keys.shape[0]
        key_pos = offset + jnp.arange(key_count, dtype=jnp.int32)
        scores = masked_scores(
            query_heads,
            block_keys.reshape(key_count, HEADS, HEAD_DIM),
            clip_ids,
            positions,
            block_tags,
            key_pos,
        )
        row_max, row_sum, weighted = running
        new_max = jnp.maximum(row_max, jnp.max(scores, axis=-1))
        rescale = jnp.exp(row_max - new_max)
        exp_scores = jnp.exp(scores - new_max[..., None])
        row_sum = row_sum * rescale + jnp.sum(exp_scores, axis=-1)
        weighted = weighted * rescale[..., None] + jnp.einsum(
            "qhk,khd->qhd",
            exp_scores.astype(jnp.bfloat16),
            block_values.reshape(key_count, HEADS, HEAD_DIM),
            preferred_element_type=jnp.float32,
        )
        return (new_max, row_sum, weighted)

    start_state = (
        jnp.full((tok_rows, HEADS), masked_score, jnp.float32),
        jnp.zeros((tok_rows, HEADS), jnp.float32),
        jnp.zeros((tok_rows, HEADS, HEAD_DIM), jnp.float32),
    )
    group_keys, group_values, group_tags = (
        lax.all_gather(keys_own, "blk", axis=0, tiled=True),
        lax.all_gather(values_own, "blk", axis=0, tiled=True),
        lax.all_gather(key_tags, "blk", axis=0, tiled=True),
    )

    def scan_fold(running, scan_args):
        return (fold_keys(running, (scan_args[0], scan_args[1], scan_args[2]), scan_args[3]), None)

    final_state = lax.scan(
        scan_fold,
        start_state,
        (
            group_keys.reshape(group_size, tok_rows, D),
            group_values.reshape(group_size, tok_rows, D),
            group_tags.reshape(group_size, tok_rows),
            starts,
        ),
    )[0]
    row_max, row_sum, weighted = final_state
    mixed_f32 = weighted / row_sum[..., None]
    log_total = row_max + jnp.log(row_sum)
    mixed = mixed_f32.reshape(tok_rows, D).astype(jnp.bfloat16)
    residual = tokens_f32 + jnp.dot(mixed, w_out, preferred_element_type=jnp.float32) + out_bias
    second_norm, unit_two, inverse_two = normalize(residual, ln2_gain, ln2_bias)
    normed_two = second_norm.astype(jnp.bfloat16)
    pre_gelu = jnp.dot(normed_two, w_fc1, preferred_element_type=jnp.float32) + fc1_bias
    activated = jax.nn.gelu(pre_gelu, approximate=False).astype(jnp.bfloat16)
    result = (
        residual + jnp.dot(activated, w_fc2, preferred_element_type=jnp.float32) + fc2_bias
    ).astype(jnp.bfloat16)
    grad_out = cotangent[0]
    grad_fc2_bias = jnp.sum(grad_out, axis=0, dtype=jnp.float32)
    grad_w_fc2 = jnp.einsum("tf,td->fd", activated, grad_out, preferred_element_type=jnp.float32)
    grad_act = jnp.einsum("td,fd->tf", grad_out, w_fc2, preferred_element_type=jnp.float32)
    grad_pre = (grad_act * gelu_slope(pre_gelu)).astype(jnp.bfloat16)
    grad_fc1_bias = jnp.sum(grad_pre, axis=0, dtype=jnp.float32)
    grad_w_fc1 = jnp.einsum("td,tf->df", normed_two, grad_pre, preferred_element_type=jnp.float32)
    grad_norm_two = jnp.einsum("tf,df->td", grad_pre, w_fc1, preferred_element_type=jnp.float32)
    grad_ln2_gain = jnp.sum(grad_norm_two * unit_two, axis=0)
    grad_ln2_bias = jnp.sum(grad_norm_two, axis=0)
    grad_residual = grad_out.astype(jnp.float32) + norm_back(
        grad_norm_two, unit_two, inverse_two, ln2_gain
    )
    grad_branch = grad_residual.astype(jnp.bfloat16)
    grad_out_bias = jnp.sum(grad_branch, axis=0, dtype=jnp.float32)
    grad_w_out = jnp.einsum("td,te->de", mixed, grad_branch, preferred_element_type=jnp.float32)
    grad_mixed = jnp.einsum(
        "te,de->td", grad_branch, w_out, preferred_element_type=jnp.float32
    ).astype(jnp.bfloat16)
    grad_heads = grad_mixed.reshape(tok_rows, HEADS, HEAD_DIM)
    row_delta = jnp.sum(grad_heads * mixed_f32, axis=-1)
    key_stack = (
        group_keys.reshape(group_size, tok_rows, D),
        group_values.reshape(group_size, tok_rows, D),
        group_tags.reshape(group_size, tok_rows),
        starts,
    )

    def back_block(grad_queries, scan_args):
        block_keys, block_values, block_tags, offset = scan_args
        key_pos = offset + jnp.arange(tok_rows, dtype=jnp.int32)
        key_heads = block_keys.reshape(tok_rows, HEADS, HEAD_DIM)
        value_heads = block_values.reshape(tok_rows, HEADS, HEAD_DIM)
        attn_probs, grad_scores = score_grads(
            query_heads,
            key_heads,
            value_heads,
            grad_heads,
            log_total,
            row_delta,
            clip_ids,
            positions,
            block_tags,
            key_pos,
        )
        grad_values = jnp.einsum(
            "qhk,qhd->khd",
            attn_probs.astype(jnp.bfloat16),
            grad_heads,
            preferred_element_type=jnp.float32,
        )
        grad_queries = (
            grad_queries
            + jnp.einsum("qhk,khd->qhd", grad_scores, key_heads, preferred_element_type=jnp.float32)
            * score_scale
        )
        grad_keys = (
            jnp.einsum("qhk,qhd->khd", grad_scores, query_heads, preferred_element_type=jnp.float32)
            * score_scale
        )
        return (
            grad_queries,
            jnp.concatenate(
                [grad_keys.reshape(tok_rows, D), grad_values.reshape(tok_rows, D)], axis=1
            ),
        )

    grad_queries, key_terms = lax.scan(
        back_block, jnp.zeros((tok_rows, HEADS, HEAD_DIM), jnp.float32), key_stack
    )
    key_sums = lax.psum_scatter(
        key_terms.reshape(group_size * tok_rows, 2 * D).astype(jnp.bfloat16),
        "blk",
        scatter_dimension=0,
        tiled=True,
    )
    grad_qkv = jnp.concatenate(
        [grad_queries.reshape(tok_rows, D).astype(jnp.bfloat16), key_sums], axis=1
    )
    grad_q_bias = jnp.sum(grad_qkv[:, :D], axis=0, dtype=jnp.float32)
    grad_v_bias = jnp.sum(grad_qkv[:, 2 * D :], axis=0, dtype=jnp.float32)
    grad_w_qkv = jnp.einsum("td,te->de", normed_one, grad_qkv, preferred_element_type=jnp.float32)
    grad_norm_one = jnp.einsum("te,de->td", grad_qkv, w_qkv, preferred_element_type=jnp.float32)
    grad_ln1_gain = jnp.sum(grad_norm_one * unit_one, axis=0)
    grad_ln1_bias = jnp.sum(grad_norm_one, axis=0)
    grad_tokens = (
        grad_residual + norm_back(grad_norm_one, unit_one, inverse_one, ln1_gain)
    ).astype(jnp.bfloat16)
    small = jnp.concatenate(
        [
            v.reshape(n_dev, -1)
            for v in (
                grad_ln1_gain,
                grad_ln1_bias,
                grad_q_bias,
                grad_v_bias,
                grad_out_bias,
                grad_ln2_gain,
                grad_ln2_bias,
                grad_fc1_bias,
                grad_fc2_bias,
            )
        ],
        axis=1,
    )
    sum_fc2 = scatter_sum(grad_w_fc2)
    sum_fc1 = scatter_sum(grad_w_fc1)
    sum_out = scatter_sum(grad_w_out)
    sum_qkv = scatter_sum(grad_w_qkv)
    part = D // n_dev
    small = scatter_stages(small, stage_orders()[0])[0]
    pieces = []
    at = 0
    for size in (part, part, part, part, part, part, part, FF // n_dev, part):
        pieces.append(small[at : at + size])
        at += size
    summed = (
        pieces[0],
        pieces[1],
        sum_qkv,
        pieces[2],
        pieces[3],
        sum_out,
        pieces[4],
        pieces[5],
        pieces[6],
        sum_fc1,
        pieces[7],
        sum_fc2,
        pieces[8],
    )
    return (
        result[None],
        grad_tokens[None],
        summed[0],
        summed[1],
        summed[2],
        summed[3],
        summed[4],
        summed[5],
        summed[6],
        summed[7],
        summed[8],
        summed[9],
        summed[10],
        summed[11],
        summed[12],
    )


def solution(mesh):
    in_specs = (
        P("seq", "blk", None),
        P("seq", None),
        P("seq", "blk"),
        P("seq", "blk", None),
        P(),
        P(),
        P(),
        P(),
        P(),
        P(),
        P(),
        P(),
        P(),
        P(),
        P(),
        P(),
        P(),
    )
    out_specs = (
        P("seq", "blk", None),
        P("seq", "blk", None),
        P(("seq", "blk")),
        P(("seq", "blk")),
        P(("seq", "blk"), None),
        P(("seq", "blk")),
        P(("seq", "blk")),
        P(("seq", "blk"), None),
        P(("seq", "blk")),
        P(("seq", "blk")),
        P(("seq", "blk")),
        P(("seq", "blk"), None),
        P(("seq", "blk")),
        P(("seq", "blk"), None),
        P(("seq", "blk")),
    )
    return jax.shard_map(body, mesh=mesh, in_specs=in_specs, out_specs=out_specs, check_vma=False)
```

```python
import functools

import jax
import jax.numpy as jnp
from jax import lax
from jax.experimental import pallas as pl
from jax.experimental.pallas import tpu as pltpu
from jax.sharding import PartitionSpec as P

D = 768
FF = 3072
HEADS = 12
HEAD_DIM = 64


epsilon = 1e-06
score_scale = 0.125
masked_score = -1e30


def clip_numbers(clip_lengths, positions):
    bounds = jnp.cumsum(clip_lengths)
    return jnp.sum((positions[:, None] >= bounds[None, :]).astype(jnp.int32), axis=1)


def normalize(values, scales, offset):
    center = values - jnp.mean(values, axis=-1, keepdims=True)
    spread = jnp.mean(center * center, axis=-1, keepdims=True)
    inverse = lax.rsqrt(spread + epsilon)
    unit = center * inverse
    return (unit * scales + offset, unit, inverse)


def norm_back(upstream, unit, inverse, scales):
    scaled = upstream * scales
    return inverse * (
        scaled
        - jnp.mean(scaled, axis=-1, keepdims=True)
        - unit * jnp.mean(scaled * unit, axis=-1, keepdims=True)
    )


def gelu_slope(pre_gelu):
    cdf_part = 0.5 * (1.0 + lax.erf(pre_gelu * 0.7071067811865476))
    return cdf_part + pre_gelu * jnp.exp(-0.5 * pre_gelu * pre_gelu) * 0.3989422804014327


def masked_scores(query_heads, key_heads, clip_ids, positions, block_tags, key_pos):
    raw_scores = (
        jnp.einsum("qhd,khd->qhk", query_heads, key_heads, preferred_element_type=jnp.float32)
        * score_scale
    )
    allowed = (block_tags[None, :] == clip_ids[:, None]) | (positions[:, None] == key_pos[None, :])
    return jnp.where(allowed[:, None, :], raw_scores, masked_score)


def score_grads(
    query_heads,
    key_heads,
    value_heads,
    grad_heads,
    log_total,
    row_delta,
    clip_ids,
    positions,
    block_tags,
    key_pos,
):
    scores = masked_scores(query_heads, key_heads, clip_ids, positions, block_tags, key_pos)
    attn_probs = jnp.exp(scores - log_total[..., None])
    grad_probs = jnp.einsum(
        "qhd,khd->qhk", grad_heads, value_heads, preferred_element_type=jnp.float32
    )
    grad_scores = (attn_probs * (grad_probs - row_delta[..., None])).astype(jnp.bfloat16)
    return (attn_probs, grad_scores)


def stage_orders():
    seq_bits = lax.axis_size("seq").bit_length() - 1
    blk_bits = lax.axis_size("blk").bit_length() - 1
    seq_stages = [blk_bits + b for b in range(seq_bits)]
    blk_stages = list(range(blk_bits))
    one = seq_stages[:2] + blk_stages + seq_stages[2:]
    two = seq_stages[:1] + blk_stages + seq_stages[1:]
    return one, two


def scatter_stages(terms, order):
    n_dev = terms.shape[0]
    bits = n_dev.bit_length() - 1
    me = lax.axis_index("seq") * lax.axis_size("blk") + lax.axis_index("blk")
    rest = terms.shape[1:]
    kind = terms.dtype
    held = terms.reshape((2,) * bits + rest)
    for number, bit in enumerate(order):
        axis = bits - 1 - bit
        mine = (me >> bit) & 1
        sent = lax.dynamic_slice_in_dim(held, 1 - mine, 1, axis)
        kept = lax.dynamic_slice_in_dim(held, mine, 1, axis)
        swap = [(i, i ^ (1 << bit)) for i in range(n_dev)]
        came = lax.ppermute(sent, ("seq", "blk"), swap)
        total = kept.astype(jnp.float32) + came.astype(jnp.float32)
        held = total if number == bits - 1 else total.astype(kind)
    return held.reshape((1,) + rest)


def scatter_sum(grad):
    n_dev = lax.axis_size("seq") * lax.axis_size("blk")
    rows, width = grad.shape
    terms = grad.astype(jnp.bfloat16).reshape(n_dev, rows // n_dev, width)
    one, two = stage_orders()
    left = scatter_stages(terms[:, :, : width // 2], one)[0]
    right = scatter_stages(terms[:, :, width // 2 :], two)[0]
    return jnp.concatenate([left, right], axis=1)


def body(
    tokens,
    lengths,
    padding,
    cotangent,
    ln1_gain,
    ln1_bias,
    w_qkv,
    q_bias,
    v_bias,
    w_out,
    out_bias,
    ln2_gain,
    ln2_bias,
    w_fc1,
    fc1_bias,
    w_fc2,
    fc2_bias,
):
    tok_rows = tokens.shape[1]
    group_size = lax.axis_size("blk")
    n_dev = lax.axis_size("seq") * group_size
    positions = lax.axis_index("blk") * tok_rows + jnp.arange(tok_rows, dtype=jnp.int32)
    clip_ids = clip_numbers(lengths[0], positions)
    key_tags = jnp.where(padding[0] == 1, -1, clip_ids)
    tokens_f32 = tokens[0].astype(jnp.float32)
    first_norm, unit_one, inverse_one = normalize(tokens_f32, ln1_gain, ln1_bias)
    normed_one = first_norm.astype(jnp.bfloat16)
    joint_bias = jnp.concatenate([q_bias, jnp.zeros_like(q_bias), v_bias])
    projected = (
        jnp.dot(normed_one, w_qkv, preferred_element_type=jnp.float32) + joint_bias
    ).astype(jnp.bfloat16)
    keys_own = projected[:, D : 2 * D]
    values_own = projected[:, 2 * D :]
    query_heads = projected[:, :D].reshape(tok_rows, HEADS, HEAD_DIM)
    starts = jnp.arange(group_size, dtype=jnp.int32) * tok_rows

    def fold_keys(running, key_block, offset):
        block_keys, block_values, block_tags = key_block
        key_count = block_keys.shape[0]
        key_pos = offset + jnp.arange(key_count, dtype=jnp.int32)
        scores = masked_scores(
            query_heads,
            block_keys.reshape(key_count, HEADS, HEAD_DIM),
            clip_ids,
            positions,
            block_tags,
            key_pos,
        )
        row_max, row_sum, weighted = running
        new_max = jnp.maximum(row_max, jnp.max(scores, axis=-1))
        rescale = jnp.exp(row_max - new_max)
        exp_scores = jnp.exp(scores - new_max[..., None])
        row_sum = row_sum * rescale + jnp.sum(exp_scores, axis=-1)
        weighted = weighted * rescale[..., None] + jnp.einsum(
            "qhk,khd->qhd",
            exp_scores.astype(jnp.bfloat16),
            block_values.reshape(key_count, HEADS, HEAD_DIM),
            preferred_element_type=jnp.float32,
        )
        return (new_max, row_sum, weighted)

    start_state = (
        jnp.full((tok_rows, HEADS), masked_score, jnp.float32),
        jnp.zeros((tok_rows, HEADS), jnp.float32),
        jnp.zeros((tok_rows, HEADS, HEAD_DIM), jnp.float32),
    )
    group_keys, group_values, group_tags = (
        lax.all_gather(keys_own, "blk", axis=0, tiled=True),
        lax.all_gather(values_own, "blk", axis=0, tiled=True),
        lax.all_gather(key_tags, "blk", axis=0, tiled=True),
    )

    def scan_fold(running, scan_args):
        return (fold_keys(running, (scan_args[0], scan_args[1], scan_args[2]), scan_args[3]), None)

    final_state = lax.scan(
        scan_fold,
        start_state,
        (
            group_keys.reshape(group_size, tok_rows, D),
            group_values.reshape(group_size, tok_rows, D),
            group_tags.reshape(group_size, tok_rows),
            starts,
        ),
    )[0]
    row_max, row_sum, weighted = final_state
    mixed_f32 = weighted / row_sum[..., None]
    log_total = row_max + jnp.log(row_sum)
    mixed = mixed_f32.reshape(tok_rows, D).astype(jnp.bfloat16)
    residual = tokens_f32 + jnp.dot(mixed, w_out, preferred_element_type=jnp.float32) + out_bias
    second_norm, unit_two, inverse_two = normalize(residual, ln2_gain, ln2_bias)
    normed_two = second_norm.astype(jnp.bfloat16)
    pre_gelu = jnp.dot(normed_two, w_fc1, preferred_element_type=jnp.float32) + fc1_bias
    activated = jax.nn.gelu(pre_gelu, approximate=False).astype(jnp.bfloat16)
    result = (
        residual + jnp.dot(activated, w_fc2, preferred_element_type=jnp.float32) + fc2_bias
    ).astype(jnp.bfloat16)
    grad_out = cotangent[0]
    grad_fc2_bias = jnp.sum(grad_out, axis=0, dtype=jnp.float32)
    grad_w_fc2 = jnp.einsum("tf,td->fd", activated, grad_out, preferred_element_type=jnp.float32)
    grad_act = jnp.einsum("td,fd->tf", grad_out, w_fc2, preferred_element_type=jnp.float32)
    grad_pre = (grad_act * gelu_slope(pre_gelu)).astype(jnp.bfloat16)
    grad_fc1_bias = jnp.sum(grad_pre, axis=0, dtype=jnp.float32)
    grad_w_fc1 = jnp.einsum("td,tf->df", normed_two, grad_pre, preferred_element_type=jnp.float32)
    grad_norm_two = jnp.einsum("tf,df->td", grad_pre, w_fc1, preferred_element_type=jnp.float32)
    grad_ln2_gain = jnp.sum(grad_norm_two * unit_two, axis=0)
    grad_ln2_bias = jnp.sum(grad_norm_two, axis=0)
    grad_residual = grad_out.astype(jnp.float32) + norm_back(
        grad_norm_two, unit_two, inverse_two, ln2_gain
    )
    grad_branch = grad_residual.astype(jnp.bfloat16)
    grad_out_bias = jnp.sum(grad_branch, axis=0, dtype=jnp.float32)
    grad_w_out = jnp.einsum("td,te->de", mixed, grad_branch, preferred_element_type=jnp.float32)
    grad_mixed = jnp.einsum(
        "te,de->td", grad_branch, w_out, preferred_element_type=jnp.float32
    ).astype(jnp.bfloat16)
    grad_heads = grad_mixed.reshape(tok_rows, HEADS, HEAD_DIM)
    row_delta = jnp.sum(grad_heads * mixed_f32, axis=-1)
    key_stack = (
        group_keys.reshape(group_size, tok_rows, D),
        group_values.reshape(group_size, tok_rows, D),
        group_tags.reshape(group_size, tok_rows),
        starts,
    )

    def back_block(grad_queries, scan_args):
        block_keys, block_values, block_tags, offset = scan_args
        key_pos = offset + jnp.arange(tok_rows, dtype=jnp.int32)
        key_heads = block_keys.reshape(tok_rows, HEADS, HEAD_DIM)
        value_heads = block_values.reshape(tok_rows, HEADS, HEAD_DIM)
        attn_probs, grad_scores = score_grads(
            query_heads,
            key_heads,
            value_heads,
            grad_heads,
            log_total,
            row_delta,
            clip_ids,
            positions,
            block_tags,
            key_pos,
        )
        grad_values = jnp.einsum(
            "qhk,qhd->khd",
            attn_probs.astype(jnp.bfloat16),
            grad_heads,
            preferred_element_type=jnp.float32,
        )
        grad_queries = (
            grad_queries
            + jnp.einsum("qhk,khd->qhd", grad_scores, key_heads, preferred_element_type=jnp.float32)
            * score_scale
        )
        grad_keys = (
            jnp.einsum("qhk,qhd->khd", grad_scores, query_heads, preferred_element_type=jnp.float32)
            * score_scale
        )
        return (
            grad_queries,
            jnp.concatenate(
                [grad_keys.reshape(tok_rows, D), grad_values.reshape(tok_rows, D)], axis=1
            ),
        )

    grad_queries, key_terms = lax.scan(
        back_block, jnp.zeros((tok_rows, HEADS, HEAD_DIM), jnp.float32), key_stack
    )
    key_sums = lax.psum_scatter(
        key_terms.reshape(group_size * tok_rows, 2 * D).astype(jnp.bfloat16),
        "blk",
        scatter_dimension=0,
        tiled=True,
    )
    grad_qkv = jnp.concatenate(
        [grad_queries.reshape(tok_rows, D).astype(jnp.bfloat16), key_sums], axis=1
    )
    grad_q_bias = jnp.sum(grad_qkv[:, :D], axis=0, dtype=jnp.float32)
    grad_v_bias = jnp.sum(grad_qkv[:, 2 * D :], axis=0, dtype=jnp.float32)
    grad_w_qkv = jnp.einsum("td,te->de", normed_one, grad_qkv, preferred_element_type=jnp.float32)
    grad_norm_one = jnp.einsum("te,de->td", grad_qkv, w_qkv, preferred_element_type=jnp.float32)
    grad_ln1_gain = jnp.sum(grad_norm_one * unit_one, axis=0)
    grad_ln1_bias = jnp.sum(grad_norm_one, axis=0)
    grad_tokens = (
        grad_residual + norm_back(grad_norm_one, unit_one, inverse_one, ln1_gain)
    ).astype(jnp.bfloat16)
    small = jnp.concatenate(
        [
            v.reshape(n_dev, -1)
            for v in (
                grad_ln1_gain,
                grad_ln1_bias,
                grad_q_bias,
                grad_v_bias,
                grad_out_bias,
                grad_ln2_gain,
                grad_ln2_bias,
                grad_fc1_bias,
                grad_fc2_bias,
            )
        ],
        axis=1,
    )
    sum_fc2 = scatter_sum(grad_w_fc2)
    sum_fc1 = scatter_sum(grad_w_fc1)
    sum_out = scatter_sum(grad_w_out)
    sum_qkv = scatter_sum(grad_w_qkv)
    part = D // n_dev
    small = scatter_stages(small, stage_orders()[0])[0]
    pieces = []
    at = 0
    for size in (part, part, part, part, part, part, part, FF // n_dev, part):
        pieces.append(small[at : at + size])
        at += size
    summed = (
        pieces[0],
        pieces[1],
        sum_qkv,
        pieces[2],
        pieces[3],
        sum_out,
        pieces[4],
        pieces[5],
        pieces[6],
        sum_fc1,
        pieces[7],
        sum_fc2,
        pieces[8],
    )
    return (
        result[None],
        grad_tokens[None],
        summed[0],
        summed[1],
        summed[2],
        summed[3],
        summed[4],
        summed[5],
        summed[6],
        summed[7],
        summed[8],
        summed[9],
        summed[10],
        summed[11],
        summed[12],
    )


f32 = jnp.float32
bf16 = jnp.bfloat16
MESH = pl.DeviceIdType.MESH
PAIRS = HEADS // 2
RING = 4
FF_CHUNK = 512
ROW_TILE = 128


def fits(mesh):
    return dict(mesh.shape) == {"seq": 16, "blk": 2}


def dot(a, b):
    return lax.dot_general(a, b, (((1,), (0,)), ((), ())), preferred_element_type=f32)


def dot_nt(a, b):
    return lax.dot_general(a, b, (((1,), (1,)), ((), ())), preferred_element_type=f32)


def dot_tn(a, b):
    return lax.dot_general(a, b, (((0,), (0,)), ((), ())), preferred_element_type=f32)


def unit_of(values):
    center = values - jnp.mean(values, axis=1, keepdims=True)
    inverse = lax.rsqrt(jnp.mean(center * center, axis=1, keepdims=True) + epsilon)
    return center * inverse, inverse


def row(ref):
    return ref[...].reshape(1, ref.shape[0])


def column_sum(values):
    return jnp.sum(values, axis=0, keepdims=True)


def block_kernel(
    tok_hbm,
    len_ref,
    pad_ref,
    cot_hbm,
    ln1_gain,
    ln1_bias,
    wqkv_hbm,
    q_bias,
    v_bias,
    wout_hbm,
    out_bias,
    ln2_gain,
    ln2_bias,
    wfc1_hbm,
    fc1_bias,
    wfc2_hbm,
    fc2_bias,
    result_ref,
    gtok_ref,
    vec_ref,
    fb1_ref,
    gfc1_hbm,
    gfc2_hbm,
    gqo_hbm,
    e_hbm,
    wqkv,
    wout,
    wfc1,
    wfc2,
    tok,
    tokp,
    cot,
    nrm,
    nrm_t,
    nrm2_t,
    qkv,
    kvp,
    gm,
    bias,
    ering,
    slots,
    gfc1,
    gfc2,
    gn_out,
    gn_in,
    tags,
    load_sem,
    e_sem,
    out_sem,
    send_sem,
    recv_sem,
):
    rows = tok.shape[0]
    seq = lax.axis_index("seq")
    blk = lax.axis_index("blk")
    twin = (seq, 1 - blk)

    loads = [
        pltpu.make_async_copy(src, dst, load_sem.at[i])
        for i, (src, dst) in enumerate(
            (
                (tok_hbm.at[0], tok),
                (wqkv_hbm, wqkv),
                (wout_hbm, wout),
                (wfc1_hbm, wfc1),
                (wfc2_hbm, wfc2),
                (cot_hbm.at[0], cot),
            )
        )
    ]
    for copy in loads:
        copy.start()

    ends = []
    total = jnp.int32(0)
    for i in range(len_ref.shape[1]):
        total = total + len_ref[0, i]
        ends.append(total)

    def clips_at(positions):
        number = jnp.zeros_like(positions)
        for end in ends:
            number = number + jnp.where(positions >= end, 1, 0)
        return number

    base = blk * rows
    lane_pos = base + lax.broadcasted_iota(jnp.int32, (8, rows), 1)
    padding = jnp.broadcast_to(pad_ref[...], (8, rows))
    tags[0] = jnp.where(padding == 1, -1, clips_at(lane_pos))

    barrier = pltpu.get_barrier_semaphore()
    pl.semaphore_signal(barrier, inc=1, device_id=twin, device_id_type=MESH)
    pl.semaphore_wait(barrier, 1)

    def to_twin(i, src, dst):
        return pltpu.make_async_remote_copy(
            src_ref=src,
            dst_ref=dst,
            send_sem=send_sem.at[i],
            recv_sem=recv_sem.at[i],
            device_id=twin,
            device_id_type=MESH,
        )

    send_tok = to_twin(0, tok_hbm.at[0], tokp)
    send_tags = to_twin(1, tags.at[0], tags.at[1])
    send_tags.start()
    send_tok.start()

    row_tiles = rows // ROW_TILE

    def tile(t):
        return pl.ds(pl.multiple_of(t * ROW_TILE, ROW_TILE), ROW_TILE)

    def first_norm(src, part):
        gain, offset = row(ln1_gain), row(ln1_bias)

        def step(t, carry):
            unit, _ = unit_of(src[tile(t), :].astype(f32))
            normed = (unit * gain + offset).astype(bf16)
            nrm[tile(t), :] = normed
            at = pl.multiple_of(part * rows + t * ROW_TILE, ROW_TILE)
            nrm_t[:, pl.ds(at, ROW_TILE)] = normed.T
            return carry

        lax.fori_loop(0, row_tiles, step, 0)

    def set_bias(part):
        clip_col = clips_at(base + lax.broadcasted_iota(jnp.int32, (rows, rows), 0))
        tag_row = jnp.broadcast_to(tags[part, 0:1, :], (rows, rows))
        allowed = tag_row == clip_col
        if part == 0:
            here = lax.broadcasted_iota(jnp.int32, (rows, rows), 0)
            there = lax.broadcasted_iota(jnp.int32, (rows, rows), 1)
            allowed = allowed | (here == there)
        bias[...] = jnp.where(allowed, 0.0, masked_score)

    loads[0].wait()
    first_norm(tok, 0)
    set_bias(0)
    loads[1].wait()
    wide = 256

    def project(kind, add, scale, dst, dst_at):
        def step(c, carry):
            col = pl.multiple_of(c * wide, wide)
            out = dot(nrm[...], wqkv[:, pl.ds(kind * D + col, wide)])
            if add is not None:
                out = out + add[pl.ds(col, wide)].reshape(1, wide)
            out = out.astype(bf16)
            if scale:
                out = out * jnp.bfloat16(score_scale)
            dst[:, pl.ds(dst_at + col, wide)] = out
            return carry

        lax.fori_loop(0, D // wide, step, 0)

    project(0, q_bias, True, qkv, 0)
    project(1, None, False, qkv, D)
    project(2, v_bias, False, qkv, 2 * D)

    low_lane = lax.broadcasted_iota(jnp.int32, (rows, 128), 1) < 64

    def half(values, h):
        return jnp.where(low_lane if h == 0 else ~low_lane, values, jnp.zeros_like(values))

    def e_copy(number, slot, out):
        if out:
            return pltpu.make_async_copy(ering.at[slot], e_hbm.at[number], e_sem.at[slot])
        return pltpu.make_async_copy(e_hbm.at[number], ering.at[slot], e_sem.at[slot])

    MIXED, F_OWN, F_TWIN, RES, ACC, GNT = range(6)

    def forward_pair(part, hp, key_ref, key_at, value_at):
        col = pl.multiple_of(hp * 128, 128)
        cols = pl.ds(col, 128)
        number = part * PAIRS + hp
        slot = number % RING

        @pl.when(number >= RING)
        def _():
            e_copy(number - RING, slot, True).wait()

        q = qkv[:, cols]
        k = key_ref[:, pl.ds(key_at + col, 128)]
        v = key_ref[:, pl.ds(value_at + col, 128)]
        outs, tops = [], []
        for h in range(2):
            scores = dot_nt(q, half(k, h)) + bias[...]
            top = jnp.max(scores, axis=1, keepdims=True)
            e = jnp.exp(scores - top).astype(bf16)
            ering[slot, h] = e
            ones = jnp.ones_like(v)
            outs.append(dot(e, jnp.where(low_lane if h == 0 else ~low_lane, v, ones)))
            tops.append(top)
        e_copy(number, slot, True).start()
        weighted = jnp.where(low_lane, outs[0], outs[1])
        sums = pltpu.roll(jnp.where(low_lane, outs[1], outs[0]), 64, 1)
        top = jnp.where(low_lane, tops[0], tops[1])
        if part == 0:
            slots[MIXED, :, cols] = weighted
            slots[F_OWN, :, cols] = sums
            slots[F_TWIN, :, cols] = top
        else:
            top_own = slots[F_TWIN, :, cols]
            both = jnp.maximum(top_own, top)
            scale_own = jnp.exp(top_own - both)
            scale_twin = jnp.exp(top - both)
            inverse = 1.0 / (scale_own * slots[F_OWN, :, cols] + scale_twin * sums)
            scale_own = scale_own * inverse
            scale_twin = scale_twin * inverse
            slots[MIXED, :, cols] = scale_own * slots[MIXED, :, cols] + scale_twin * weighted
            slots[F_OWN, :, cols] = scale_own
            slots[F_TWIN, :, cols] = scale_twin

    def pairs_loop(body):
        def step(hp, carry):
            body(hp)
            return carry

        lax.fori_loop(0, PAIRS, step, 0)

    pairs_loop(lambda hp: forward_pair(0, hp, qkv, D, 2 * D))

    send_tok.wait()
    send_tags.wait()
    first_norm(tokp, 1)
    set_bias(1)
    project(1, None, False, kvp, 0)
    project(2, v_bias, False, kvp, D)
    pairs_loop(lambda hp: forward_pair(1, hp, kvp, 0, D))

    loads[2].wait()

    def branch(c, carry):
        cols = pl.ds(pl.multiple_of(c * wide, wide), wide)
        out = dot(slots[MIXED].astype(bf16), wout[:, cols])
        out = out + out_bias[cols].reshape(1, wide)
        slots[RES, :, cols] = tok[:, cols].astype(f32) + out
        return carry

    lax.fori_loop(0, D // wide, branch, 0)
    gain_two, offset_two = row(ln2_gain), row(ln2_bias)

    def second_norm(t, carry):
        unit, _ = unit_of(slots[RES, tile(t), :])
        normed = (unit * gain_two + offset_two).astype(bf16)
        nrm[tile(t), :] = normed
        nrm2_t[:, tile(t)] = normed.T
        slots[ACC, tile(t), :] = jnp.zeros((ROW_TILE, D), f32)
        slots[GNT, tile(t), :] = jnp.zeros((ROW_TILE, D), f32)
        return carry

    lax.fori_loop(0, row_tiles, second_norm, 0)

    loads[3].wait()
    loads[4].wait()
    loads[5].wait()

    def feed(c, carry):
        units = pl.ds(pl.multiple_of(c * FF_CHUNK, FF_CHUNK), FF_CHUNK)
        w1 = wfc1[:, units]
        w2 = wfc2[units, :]
        pre = dot(nrm[...], w1) + fc1_bias[units].reshape(1, FF_CHUNK)
        phi = 0.5 * (1.0 + lax.erf(pre * 0.7071067811865476))
        slope = phi + pre * jnp.exp(-0.5 * pre * pre) * 0.3989422804014327
        activated = (pre * phi).astype(bf16)
        grad_pre = (dot_nt(cot[...], w2) * slope).astype(bf16)
        slots[ACC] += dot(activated, w2)
        slots[GNT] += dot_nt(grad_pre, w1)
        gfc2[units, :] = dot_tn(activated, cot[...]).astype(bf16)
        gfc1[:, units] = dot(nrm2_t[...], grad_pre).astype(bf16)
        fb1_ref[:, units] = column_sum(grad_pre.astype(f32))
        return carry

    lax.fori_loop(0, FF // FF_CHUNK, feed, 0)
    store_fc1 = pltpu.make_async_copy(gfc1, gfc1_hbm, out_sem.at[0])
    store_fc2 = pltpu.make_async_copy(gfc2, gfc2_hbm, out_sem.at[1])
    store_fc1.start()
    store_fc2.start()

    for number in range(2 * PAIRS - RING, 2 * PAIRS):
        e_copy(number, number % RING, True).wait()
    back_order = [PAIRS + hp for hp in range(PAIRS)] + list(range(PAIRS))

    def e_number(step):
        return lax.rem(step + PAIRS, 2 * PAIRS)

    for step in range(RING):
        e_copy(back_order[step], step % RING, False).start()

    vec_ref[...] = jnp.zeros(vec_ref.shape, f32)
    (V_LN1G, V_LN1B, V_QB, V_VB, V_OB, V_LN2G, V_LN2B, V_FC2B) = range(8)

    def add_vec(kind, values):
        vec_ref[kind : kind + 1, :] += column_sum(values)

    def second_back(t, carry):
        here = tile(t)
        unit, inverse = unit_of(slots[RES, here, :])
        result_ref[0, here, :] = (
            slots[RES, here, :] + slots[ACC, here, :] + row(fc2_bias)
        ).astype(bf16)
        upstream = slots[GNT, here, :]
        grad_out = cot[here, :].astype(f32)
        add_vec(V_FC2B, grad_out)
        add_vec(V_LN2G, upstream * unit)
        add_vec(V_LN2B, upstream)
        scaled = upstream * gain_two
        grad = grad_out + inverse * (
            scaled
            - jnp.mean(scaled, axis=1, keepdims=True)
            - unit * jnp.mean(scaled * unit, axis=1, keepdims=True)
        )
        slots[RES, here, :] = grad
        low = grad.astype(bf16)
        nrm[here, :] = low
        add_vec(V_OB, low.astype(f32))
        return carry

    lax.fori_loop(0, row_tiles, second_back, 0)

    GQ = ACC

    def mixed_back(c, carry):
        cols = pl.ds(pl.multiple_of(c * wide, wide), wide)
        gm[:, cols] = dot_nt(nrm[...], wout[cols, :]).astype(bf16)
        mixed = slots[MIXED, :, cols].astype(bf16)
        wfc1[cols, 3 * D : 4 * D] = dot_tn(mixed, nrm[...]).astype(bf16)
        return carry

    lax.fori_loop(0, D // wide, mixed_back, 0)

    def backward_pair(part, hp, key_ref, key_at, value_at):
        col = pl.multiple_of(hp * 128, 128)
        cols = pl.ds(col, 128)
        step = (1 - part) * PAIRS + hp
        slot = step % RING
        q = qkv[:, cols]
        k = key_ref[:, pl.ds(key_at + col, 128)]
        v = key_ref[:, pl.ds(value_at + col, 128)]
        grad_in = gm[:, cols].astype(f32)
        factor = slots[F_OWN if part == 0 else F_TWIN, :, cols]
        product = grad_in * slots[MIXED, :, cols] * factor
        scaled = (grad_in * factor).astype(bf16)
        q_t = q.T
        scaled_t = scaled.T
        e_copy(e_number(step), slot, False).wait()
        grad_q = None
        grad_k, grad_v = [], []
        for h in range(2):
            delta = jnp.sum(half(product, h), axis=1, keepdims=True)
            e = ering[slot, h]
            grad_probs = dot_nt(scaled, half(v, h))
            grad_scores = (e.astype(f32) * (grad_probs - delta)).astype(bf16)
            term = dot(grad_scores, half(k, h))
            grad_q = term if grad_q is None else grad_q + term
            grad_k.append(dot(q_t[64 * h : 64 * h + 64], grad_scores))
            grad_v.append(dot(scaled_t[64 * h : 64 * h + 64], e))

        @pl.when(step + RING < 2 * PAIRS)
        def _():
            e_copy(e_number(step + RING), slot, False).start()

        key_ref[:, pl.ds(key_at + col, 128)] = jnp.concatenate(grad_k, axis=0).T.astype(bf16)
        key_ref[:, pl.ds(value_at + col, 128)] = jnp.concatenate(grad_v, axis=0).T.astype(bf16)
        if part == 1:
            slots[GQ, :, cols] = grad_q
        else:
            total_q = (slots[GQ, :, cols] + grad_q) * score_scale
            qkv[:, cols] = total_q.astype(bf16)

    pairs_loop(lambda hp: backward_pair(1, hp, kvp, 0, D))

    def partial_out(c, carry):
        cols = pl.ds(pl.multiple_of(c * wide, wide), wide)
        gn_out[:, cols] = dot_nt(kvp[...], wqkv[cols, D : 3 * D]).astype(bf16)
        return carry

    lax.fori_loop(0, D // wide, partial_out, 0)
    send_gn = to_twin(2, gn_out, gn_in)
    send_gn.start()

    pairs_loop(lambda hp: backward_pair(0, hp, qkv, D, 2 * D))

    def weight_own(c, carry):
        cols = pl.ds(pl.multiple_of(c * wide, wide), wide)
        wfc1[:, cols] = dot(nrm_t[:, :rows], qkv[:, cols]).astype(bf16)
        add_vec_cols(V_QB, cols, qkv[:, cols])
        return carry

    def add_vec_cols(kind, cols, values):
        vec_ref[kind : kind + 1, cols] = column_sum(values.astype(f32))

    lax.fori_loop(0, D // wide, weight_own, 0)

    def weight_both(c, carry):
        col = pl.multiple_of(c * wide, wide)
        own = qkv[:, pl.ds(D + col, wide)]
        other = kvp[:, pl.ds(col, wide)]
        joint = jnp.concatenate([own, other], axis=0)
        wfc1[:, pl.ds(D + col, wide)] = dot(nrm_t[...], joint).astype(bf16)
        return carry

    lax.fori_loop(0, 2 * D // wide, weight_both, 0)
    store_qo = pltpu.make_async_copy(wfc1, gqo_hbm, out_sem.at[2])
    store_qo.start()

    def value_sum(c, carry):
        col = pl.multiple_of(c * wide, wide)
        values = qkv[:, pl.ds(2 * D + col, wide)].astype(f32)
        other = kvp[:, pl.ds(D + col, wide)].astype(f32)
        vec_ref[V_VB : V_VB + 1, pl.ds(col, wide)] = column_sum(values + other)
        return carry

    lax.fori_loop(0, D // wide, value_sum, 0)

    def first_back_product(c, carry):
        cols = pl.ds(pl.multiple_of(c * wide, wide), wide)
        slots[GNT, :, cols] = dot_nt(qkv[...], wqkv[cols, :])
        return carry

    lax.fori_loop(0, D // wide, first_back_product, 0)
    send_gn.wait()
    gain_one = row(ln1_gain)

    def first_back(t, carry):
        here = tile(t)
        unit, inverse = unit_of(tok[here, :].astype(f32))
        upstream = slots[GNT, here, :] + gn_in[here, :].astype(f32)
        add_vec(V_LN1G, upstream * unit)
        add_vec(V_LN1B, upstream)
        scaled = upstream * gain_one
        grad = slots[RES, here, :] + inverse * (
            scaled
            - jnp.mean(scaled, axis=1, keepdims=True)
            - unit * jnp.mean(scaled * unit, axis=1, keepdims=True)
        )
        gtok_ref[0, here, :] = grad.astype(bf16)
        return carry

    lax.fori_loop(0, row_tiles, first_back, 0)
    store_fc1.wait()
    store_fc2.wait()
    store_qo.wait()


def block_body(
    tokens,
    lengths,
    padding,
    cotangent,
    ln1_gain,
    ln1_bias,
    w_qkv,
    q_bias,
    v_bias,
    w_out,
    out_bias,
    ln2_gain,
    ln2_bias,
    w_fc1,
    fc1_bias,
    w_fc2,
    fc2_bias,
):
    rows = tokens.shape[1]
    n_dev = lax.axis_size("seq") * lax.axis_size("blk")
    shape = jax.ShapeDtypeStruct
    any_spec = pl.BlockSpec(memory_space=pl.ANY)
    vmem = pl.BlockSpec(memory_space=pltpu.VMEM)
    smem = pl.BlockSpec(memory_space=pltpu.SMEM)
    result, grad_tokens, vec, fb1, gfc1, gfc2, gqo, _ = pl.pallas_call(
        block_kernel,
        name="block",
        out_shape=(
            shape((1, rows, D), bf16),
            shape((1, rows, D), bf16),
            shape((8, D), f32),
            shape((1, FF), f32),
            shape((D, FF), bf16),
            shape((FF, D), bf16),
            shape((D, 4 * D), bf16),
            shape((2 * PAIRS, 2, rows, rows), bf16),
        ),
        in_specs=[
            any_spec, smem, vmem, any_spec, vmem, vmem, any_spec, vmem, vmem,
            any_spec, vmem, vmem, vmem, any_spec, vmem, any_spec, vmem,
        ],
        out_specs=(vmem, vmem, vmem, vmem, any_spec, any_spec, any_spec, any_spec),
        scratch_shapes=[
            pltpu.VMEM((D, 3 * D), bf16),
            pltpu.VMEM((D, D), bf16),
            pltpu.VMEM((D, FF), bf16),
            pltpu.VMEM((FF, D), bf16),
            pltpu.VMEM((rows, D), bf16),
            pltpu.VMEM((rows, D), bf16),
            pltpu.VMEM((rows, D), bf16),
            pltpu.VMEM((rows, D), bf16),
            pltpu.VMEM((D, 2 * rows), bf16),
            pltpu.VMEM((D, rows), bf16),
            pltpu.VMEM((rows, 3 * D), bf16),
            pltpu.VMEM((rows, 2 * D), bf16),
            pltpu.VMEM((rows, D), bf16),
            pltpu.VMEM((rows, rows), f32),
            pltpu.VMEM((RING, 2, rows, rows), bf16),
            pltpu.VMEM((6, rows, D), f32),
            pltpu.VMEM((D, FF), bf16),
            pltpu.VMEM((FF, D), bf16),
            pltpu.VMEM((rows, D), bf16),
            pltpu.VMEM((rows, D), bf16),
            pltpu.VMEM((2, 8, rows), jnp.int32),
            pltpu.SemaphoreType.DMA((6,)),
            pltpu.SemaphoreType.DMA((RING,)),
            pltpu.SemaphoreType.DMA((3,)),
            pltpu.SemaphoreType.DMA((3,)),
            pltpu.SemaphoreType.DMA((3,)),
        ],
        compiler_params=pltpu.CompilerParams(
            collective_id=0, has_side_effects=True, vmem_limit_bytes=VMEM_LIMIT
        ),
        cost_estimate=pl.CostEstimate(
            flops=30 * 10**9, bytes_accessed=60 * 10**6, transcendentals=10**7
        ),
    )(
        tokens, lengths, padding, cotangent, ln1_gain, ln1_bias, w_qkv, q_bias, v_bias,
        w_out, out_bias, ln2_gain, ln2_bias, w_fc1, fc1_bias, w_fc2, fc2_bias,
    )
    small = jnp.concatenate(
        [vec[k].reshape(n_dev, -1) for k in range(8)] + [fb1.reshape(n_dev, -1)], axis=1
    )
    sum_fc2 = scatter_sum(gfc2)
    sum_fc1 = scatter_sum(gfc1)
    sum_qo = scatter_sum(gqo)
    small = scatter_stages(small, stage_orders()[0])[0]
    part = D // n_dev
    one = [small[k * part : (k + 1) * part] for k in range(8)]
    return (
        result,
        grad_tokens,
        one[0],
        one[1],
        sum_qo[:, : 3 * D],
        one[2],
        one[3],
        sum_qo[:, 3 * D :],
        one[4],
        one[5],
        one[6],
        sum_fc1,
        small[8 * part :],
        sum_fc2,
        one[7],
    )


VMEM_LIMIT = 62 * 2**20


def solution(mesh):
    in_specs = (
        P("seq", "blk", None),
        P("seq", None),
        P("seq", "blk"),
        P("seq", "blk", None),
        P(),
        P(),
        P(),
        P(),
        P(),
        P(),
        P(),
        P(),
        P(),
        P(),
        P(),
        P(),
        P(),
    )
    out_specs = (
        P("seq", "blk", None),
        P("seq", "blk", None),
        P(("seq", "blk")),
        P(("seq", "blk")),
        P(("seq", "blk"), None),
        P(("seq", "blk")),
        P(("seq", "blk")),
        P(("seq", "blk"), None),
        P(("seq", "blk")),
        P(("seq", "blk")),
        P(("seq", "blk")),
        P(("seq", "blk"), None),
        P(("seq", "blk")),
        P(("seq", "blk"), None),
        P(("seq", "blk")),
    )
    step = block_body if fits(mesh) else body
    return jax.shard_map(step, mesh=mesh, in_specs=in_specs, out_specs=out_specs, check_vma=False)
```

```python
import functools

import jax
import jax.numpy as jnp
from jax import lax
from jax.experimental import pallas as pl
from jax.experimental.pallas import tpu as pltpu
from jax.sharding import PartitionSpec as P

D = 768
FF = 3072
HEADS = 12
HEAD_DIM = 64


epsilon = 1e-06
score_scale = 0.125
masked_score = -1e30


def clip_numbers(clip_lengths, positions):
    bounds = jnp.cumsum(clip_lengths)
    return jnp.sum((positions[:, None] >= bounds[None, :]).astype(jnp.int32), axis=1)


def normalize(values, scales, offset):
    center = values - jnp.mean(values, axis=-1, keepdims=True)
    spread = jnp.mean(center * center, axis=-1, keepdims=True)
    inverse = lax.rsqrt(spread + epsilon)
    unit = center * inverse
    return (unit * scales + offset, unit, inverse)


def norm_back(upstream, unit, inverse, scales):
    scaled = upstream * scales
    return inverse * (
        scaled
        - jnp.mean(scaled, axis=-1, keepdims=True)
        - unit * jnp.mean(scaled * unit, axis=-1, keepdims=True)
    )


def gelu_slope(pre_gelu):
    cdf_part = 0.5 * (1.0 + lax.erf(pre_gelu * 0.7071067811865476))
    return cdf_part + pre_gelu * jnp.exp(-0.5 * pre_gelu * pre_gelu) * 0.3989422804014327


def masked_scores(query_heads, key_heads, clip_ids, positions, block_tags, key_pos):
    raw_scores = (
        jnp.einsum("qhd,khd->qhk", query_heads, key_heads, preferred_element_type=jnp.float32)
        * score_scale
    )
    allowed = (block_tags[None, :] == clip_ids[:, None]) | (positions[:, None] == key_pos[None, :])
    return jnp.where(allowed[:, None, :], raw_scores, masked_score)


def score_grads(
    query_heads,
    key_heads,
    value_heads,
    grad_heads,
    log_total,
    row_delta,
    clip_ids,
    positions,
    block_tags,
    key_pos,
):
    scores = masked_scores(query_heads, key_heads, clip_ids, positions, block_tags, key_pos)
    attn_probs = jnp.exp(scores - log_total[..., None])
    grad_probs = jnp.einsum(
        "qhd,khd->qhk", grad_heads, value_heads, preferred_element_type=jnp.float32
    )
    grad_scores = (attn_probs * (grad_probs - row_delta[..., None])).astype(jnp.bfloat16)
    return (attn_probs, grad_scores)


def stage_orders():
    seq_bits = lax.axis_size("seq").bit_length() - 1
    blk_bits = lax.axis_size("blk").bit_length() - 1
    seq_stages = [blk_bits + b for b in range(seq_bits)]
    blk_stages = list(range(blk_bits))
    one = seq_stages[:2] + blk_stages + seq_stages[2:]
    two = seq_stages[:1] + blk_stages + seq_stages[1:]
    return one, two


def scatter_stages(terms, order):
    n_dev = terms.shape[0]
    bits = n_dev.bit_length() - 1
    me = lax.axis_index("seq") * lax.axis_size("blk") + lax.axis_index("blk")
    rest = terms.shape[1:]
    kind = terms.dtype
    held = terms.reshape((2,) * bits + rest)
    for number, bit in enumerate(order):
        axis = bits - 1 - bit
        mine = (me >> bit) & 1
        sent = lax.dynamic_slice_in_dim(held, 1 - mine, 1, axis)
        kept = lax.dynamic_slice_in_dim(held, mine, 1, axis)
        swap = [(i, i ^ (1 << bit)) for i in range(n_dev)]
        came = lax.ppermute(sent, ("seq", "blk"), swap)
        total = kept.astype(jnp.float32) + came.astype(jnp.float32)
        held = total if number == bits - 1 else total.astype(kind)
    return held.reshape((1,) + rest)


def scatter_sum(grad):
    n_dev = lax.axis_size("seq") * lax.axis_size("blk")
    rows, width = grad.shape
    terms = grad.astype(jnp.bfloat16).reshape(n_dev, rows // n_dev, width)
    one, two = stage_orders()
    left = scatter_stages(terms[:, :, : width // 2], one)[0]
    right = scatter_stages(terms[:, :, width // 2 :], two)[0]
    return jnp.concatenate([left, right], axis=1)


def body(
    tokens,
    lengths,
    padding,
    cotangent,
    ln1_gain,
    ln1_bias,
    w_qkv,
    q_bias,
    v_bias,
    w_out,
    out_bias,
    ln2_gain,
    ln2_bias,
    w_fc1,
    fc1_bias,
    w_fc2,
    fc2_bias,
):
    tok_rows = tokens.shape[1]
    group_size = lax.axis_size("blk")
    n_dev = lax.axis_size("seq") * group_size
    positions = lax.axis_index("blk") * tok_rows + jnp.arange(tok_rows, dtype=jnp.int32)
    clip_ids = clip_numbers(lengths[0], positions)
    key_tags = jnp.where(padding[0] == 1, -1, clip_ids)
    tokens_f32 = tokens[0].astype(jnp.float32)
    first_norm, unit_one, inverse_one = normalize(tokens_f32, ln1_gain, ln1_bias)
    normed_one = first_norm.astype(jnp.bfloat16)
    joint_bias = jnp.concatenate([q_bias, jnp.zeros_like(q_bias), v_bias])
    projected = (
        jnp.dot(normed_one, w_qkv, preferred_element_type=jnp.float32) + joint_bias
    ).astype(jnp.bfloat16)
    keys_own = projected[:, D : 2 * D]
    values_own = projected[:, 2 * D :]
    query_heads = projected[:, :D].reshape(tok_rows, HEADS, HEAD_DIM)
    starts = jnp.arange(group_size, dtype=jnp.int32) * tok_rows

    def fold_keys(running, key_block, offset):
        block_keys, block_values, block_tags = key_block
        key_count = block_keys.shape[0]
        key_pos = offset + jnp.arange(key_count, dtype=jnp.int32)
        scores = masked_scores(
            query_heads,
            block_keys.reshape(key_count, HEADS, HEAD_DIM),
            clip_ids,
            positions,
            block_tags,
            key_pos,
        )
        row_max, row_sum, weighted = running
        new_max = jnp.maximum(row_max, jnp.max(scores, axis=-1))
        rescale = jnp.exp(row_max - new_max)
        exp_scores = jnp.exp(scores - new_max[..., None])
        row_sum = row_sum * rescale + jnp.sum(exp_scores, axis=-1)
        weighted = weighted * rescale[..., None] + jnp.einsum(
            "qhk,khd->qhd",
            exp_scores.astype(jnp.bfloat16),
            block_values.reshape(key_count, HEADS, HEAD_DIM),
            preferred_element_type=jnp.float32,
        )
        return (new_max, row_sum, weighted)

    start_state = (
        jnp.full((tok_rows, HEADS), masked_score, jnp.float32),
        jnp.zeros((tok_rows, HEADS), jnp.float32),
        jnp.zeros((tok_rows, HEADS, HEAD_DIM), jnp.float32),
    )
    group_keys, group_values, group_tags = (
        lax.all_gather(keys_own, "blk", axis=0, tiled=True),
        lax.all_gather(values_own, "blk", axis=0, tiled=True),
        lax.all_gather(key_tags, "blk", axis=0, tiled=True),
    )

    def scan_fold(running, scan_args):
        return (fold_keys(running, (scan_args[0], scan_args[1], scan_args[2]), scan_args[3]), None)

    final_state = lax.scan(
        scan_fold,
        start_state,
        (
            group_keys.reshape(group_size, tok_rows, D),
            group_values.reshape(group_size, tok_rows, D),
            group_tags.reshape(group_size, tok_rows),
            starts,
        ),
    )[0]
    row_max, row_sum, weighted = final_state
    mixed_f32 = weighted / row_sum[..., None]
    log_total = row_max + jnp.log(row_sum)
    mixed = mixed_f32.reshape(tok_rows, D).astype(jnp.bfloat16)
    residual = tokens_f32 + jnp.dot(mixed, w_out, preferred_element_type=jnp.float32) + out_bias
    second_norm, unit_two, inverse_two = normalize(residual, ln2_gain, ln2_bias)
    normed_two = second_norm.astype(jnp.bfloat16)
    pre_gelu = jnp.dot(normed_two, w_fc1, preferred_element_type=jnp.float32) + fc1_bias
    activated = jax.nn.gelu(pre_gelu, approximate=False).astype(jnp.bfloat16)
    result = (
        residual + jnp.dot(activated, w_fc2, preferred_element_type=jnp.float32) + fc2_bias
    ).astype(jnp.bfloat16)
    grad_out = cotangent[0]
    grad_fc2_bias = jnp.sum(grad_out, axis=0, dtype=jnp.float32)
    grad_w_fc2 = jnp.einsum("tf,td->fd", activated, grad_out, preferred_element_type=jnp.float32)
    grad_act = jnp.einsum("td,fd->tf", grad_out, w_fc2, preferred_element_type=jnp.float32)
    grad_pre = (grad_act * gelu_slope(pre_gelu)).astype(jnp.bfloat16)
    grad_fc1_bias = jnp.sum(grad_pre, axis=0, dtype=jnp.float32)
    grad_w_fc1 = jnp.einsum("td,tf->df", normed_two, grad_pre, preferred_element_type=jnp.float32)
    grad_norm_two = jnp.einsum("tf,df->td", grad_pre, w_fc1, preferred_element_type=jnp.float32)
    grad_ln2_gain = jnp.sum(grad_norm_two * unit_two, axis=0)
    grad_ln2_bias = jnp.sum(grad_norm_two, axis=0)
    grad_residual = grad_out.astype(jnp.float32) + norm_back(
        grad_norm_two, unit_two, inverse_two, ln2_gain
    )
    grad_branch = grad_residual.astype(jnp.bfloat16)
    grad_out_bias = jnp.sum(grad_branch, axis=0, dtype=jnp.float32)
    grad_w_out = jnp.einsum("td,te->de", mixed, grad_branch, preferred_element_type=jnp.float32)
    grad_mixed = jnp.einsum(
        "te,de->td", grad_branch, w_out, preferred_element_type=jnp.float32
    ).astype(jnp.bfloat16)
    grad_heads = grad_mixed.reshape(tok_rows, HEADS, HEAD_DIM)
    row_delta = jnp.sum(grad_heads * mixed_f32, axis=-1)
    key_stack = (
        group_keys.reshape(group_size, tok_rows, D),
        group_values.reshape(group_size, tok_rows, D),
        group_tags.reshape(group_size, tok_rows),
        starts,
    )

    def back_block(grad_queries, scan_args):
        block_keys, block_values, block_tags, offset = scan_args
        key_pos = offset + jnp.arange(tok_rows, dtype=jnp.int32)
        key_heads = block_keys.reshape(tok_rows, HEADS, HEAD_DIM)
        value_heads = block_values.reshape(tok_rows, HEADS, HEAD_DIM)
        attn_probs, grad_scores = score_grads(
            query_heads,
            key_heads,
            value_heads,
            grad_heads,
            log_total,
            row_delta,
            clip_ids,
            positions,
            block_tags,
            key_pos,
        )
        grad_values = jnp.einsum(
            "qhk,qhd->khd",
            attn_probs.astype(jnp.bfloat16),
            grad_heads,
            preferred_element_type=jnp.float32,
        )
        grad_queries = (
            grad_queries
            + jnp.einsum("qhk,khd->qhd", grad_scores, key_heads, preferred_element_type=jnp.float32)
            * score_scale
        )
        grad_keys = (
            jnp.einsum("qhk,qhd->khd", grad_scores, query_heads, preferred_element_type=jnp.float32)
            * score_scale
        )
        return (
            grad_queries,
            jnp.concatenate(
                [grad_keys.reshape(tok_rows, D), grad_values.reshape(tok_rows, D)], axis=1
            ),
        )

    grad_queries, key_terms = lax.scan(
        back_block, jnp.zeros((tok_rows, HEADS, HEAD_DIM), jnp.float32), key_stack
    )
    key_sums = lax.psum_scatter(
        key_terms.reshape(group_size * tok_rows, 2 * D).astype(jnp.bfloat16),
        "blk",
        scatter_dimension=0,
        tiled=True,
    )
    grad_qkv = jnp.concatenate(
        [grad_queries.reshape(tok_rows, D).astype(jnp.bfloat16), key_sums], axis=1
    )
    grad_q_bias = jnp.sum(grad_qkv[:, :D], axis=0, dtype=jnp.float32)
    grad_v_bias = jnp.sum(grad_qkv[:, 2 * D :], axis=0, dtype=jnp.float32)
    grad_w_qkv = jnp.einsum("td,te->de", normed_one, grad_qkv, preferred_element_type=jnp.float32)
    grad_norm_one = jnp.einsum("te,de->td", grad_qkv, w_qkv, preferred_element_type=jnp.float32)
    grad_ln1_gain = jnp.sum(grad_norm_one * unit_one, axis=0)
    grad_ln1_bias = jnp.sum(grad_norm_one, axis=0)
    grad_tokens = (
        grad_residual + norm_back(grad_norm_one, unit_one, inverse_one, ln1_gain)
    ).astype(jnp.bfloat16)
    small = jnp.concatenate(
        [
            v.reshape(n_dev, -1)
            for v in (
                grad_ln1_gain,
                grad_ln1_bias,
                grad_q_bias,
                grad_v_bias,
                grad_out_bias,
                grad_ln2_gain,
                grad_ln2_bias,
                grad_fc1_bias,
                grad_fc2_bias,
            )
        ],
        axis=1,
    )
    sum_fc2 = scatter_sum(grad_w_fc2)
    sum_fc1 = scatter_sum(grad_w_fc1)
    sum_out = scatter_sum(grad_w_out)
    sum_qkv = scatter_sum(grad_w_qkv)
    part = D // n_dev
    small = scatter_stages(small, stage_orders()[0])[0]
    pieces = []
    at = 0
    for size in (part, part, part, part, part, part, part, FF // n_dev, part):
        pieces.append(small[at : at + size])
        at += size
    summed = (
        pieces[0],
        pieces[1],
        sum_qkv,
        pieces[2],
        pieces[3],
        sum_out,
        pieces[4],
        pieces[5],
        pieces[6],
        sum_fc1,
        pieces[7],
        sum_fc2,
        pieces[8],
    )
    return (
        result[None],
        grad_tokens[None],
        summed[0],
        summed[1],
        summed[2],
        summed[3],
        summed[4],
        summed[5],
        summed[6],
        summed[7],
        summed[8],
        summed[9],
        summed[10],
        summed[11],
        summed[12],
    )


f32 = jnp.float32
bf16 = jnp.bfloat16
MESH = pl.DeviceIdType.MESH
PAIRS = HEADS // 2
RING = 3
FF_CHUNK = 512
ROW_TILE = 128
ITEMS = 18
ITEM_ROWS = 512
ITEM_LANES = 768
APART = 2
SLOTS = 2 * APART
STAGES = 5
LANDING = (0, 256, 384, 448, 480)
LANDING_ROWS = 496
FLAT_BITS = ("y", "c", "x", "z0", "z1")
GROUPS = (
    (("c", "x", "y", "z0", "z1"), 0, 384),
    (("c", "y", "x", "z0", "z1"), 384, 128),
    (("c", "z0", "z1", "x", "y"), 512, 256),
)


def fits(mesh):
    return dict(mesh.shape) == {"seq": 16, "blk": 2}


def dot(a, b):
    return lax.dot_general(a, b, (((1,), (0,)), ((), ())), preferred_element_type=f32)


def dot_nt(a, b):
    return lax.dot_general(a, b, (((1,), (1,)), ((), ())), preferred_element_type=f32)


def dot_tn(a, b):
    return lax.dot_general(a, b, (((0,), (0,)), ((), ())), preferred_element_type=f32)


def unit_of(values):
    center = values - jnp.mean(values, axis=1, keepdims=True)
    inverse = lax.rsqrt(jnp.mean(center * center, axis=1, keepdims=True) + epsilon)
    return center * inverse, inverse


def row(ref):
    return ref[...].reshape(1, ref.shape[0])


def column_sum(values):
    return jnp.sum(values, axis=0, keepdims=True)


def block_kernel(
    tok_hbm,
    len_ref,
    pad_ref,
    cot_hbm,
    ln1_gain,
    ln1_bias,
    wqkv_hbm,
    q_bias,
    v_bias,
    wout_hbm,
    out_bias,
    ln2_gain,
    ln2_bias,
    wfc1_hbm,
    fc1_bias,
    wfc2_hbm,
    fc2_bias,
    result_ref,
    gtok_ref,
    out_ln1g,
    out_ln1b,
    out_qkv,
    out_qb,
    out_vb,
    out_out,
    out_ob,
    out_ln2g,
    out_ln2b,
    out_fc1,
    out_fb1,
    out_fc2,
    out_fb2,
    e_hbm,
    wqkv,
    wout,
    wfc1,
    wfc2,
    tok,
    tokp,
    cot,
    nrm,
    nrm_t,
    nrm2_t,
    qkv,
    kvp,
    gm,
    bias,
    ering,
    slots,
    terms,
    landing,
    gn_in,
    tags,
    vec_ref,
    fb1_ref,
    small,
    small_in,
    load_sem,
    e_sem,
    send_sem,
    recv_sem,
    item_send,
    item_recv,
    small_send,
    small_recv,
):
    rows = tok.shape[0]
    seq = lax.axis_index("seq")
    blk = lax.axis_index("blk")
    bit = {
        "y": blk,
        "c": lax.rem(seq, 2),
        "x": lax.rem(seq // 2, 2),
        "z0": lax.rem(seq // 4, 2),
        "z1": seq // 8,
    }
    across = {
        "y": (seq, 1 - blk),
        "c": (seq + 1 - 2 * bit["c"], blk),
        "x": (seq + 2 - 4 * bit["x"], blk),
        "z0": (seq + 4 - 8 * bit["z0"], blk),
        "z1": (seq + 8 - 16 * bit["z1"], blk),
    }
    twin = across["y"]

    loads = [
        pltpu.make_async_copy(src, dst, load_sem.at[i])
        for i, (src, dst) in enumerate(
            (
                (tok_hbm.at[0], tok),
                (wqkv_hbm, wqkv),
                (wout_hbm, wout),
                (wfc1_hbm, wfc1),
                (wfc2_hbm, wfc2),
                (cot_hbm.at[0], cot),
            )
        )
    ]
    for copy in loads:
        copy.start()

    ends = []
    total = jnp.int32(0)
    for i in range(len_ref.shape[1]):
        total = total + len_ref[0, i]
        ends.append(total)

    def clips_at(positions):
        number = jnp.zeros_like(positions)
        for end in ends:
            number = number + jnp.where(positions >= end, 1, 0)
        return number

    base = blk * rows
    lane_pos = base + lax.broadcasted_iota(jnp.int32, (8, rows), 1)
    padding = jnp.broadcast_to(pad_ref[...], (8, rows))
    tags[0] = jnp.where(padding == 1, -1, clips_at(lane_pos))

    barrier = pltpu.get_barrier_semaphore()
    for name in FLAT_BITS:
        pl.semaphore_signal(barrier, inc=1, device_id=across[name], device_id_type=MESH)
    pl.semaphore_wait(barrier, len(FLAT_BITS))

    def to_twin(i, src, dst):
        return pltpu.make_async_remote_copy(
            src_ref=src,
            dst_ref=dst,
            send_sem=send_sem.at[i],
            recv_sem=recv_sem.at[i],
            device_id=twin,
            device_id_type=MESH,
        )

    send_tok = to_twin(0, tok_hbm.at[0], tokp)
    send_tags = to_twin(1, tags.at[0], tags.at[1])
    send_tags.start()
    send_tok.start()

    def place_of(order, there):
        at = 0
        for stage, name in enumerate(order):
            differs = there[name] + bit[name] - 2 * there[name] * bit[name]
            at = at + (16 >> stage) * differs
        return at

    def bits_of(d):
        return {name: (d >> i) & 1 for i, name in enumerate(FLAT_BITS)}

    def item_copy(stage, item, group):
        order, lane, width = GROUPS[group]
        count = ITEM_ROWS >> stage
        slot = lax.rem(item, SLOTS)
        src_at = pl.multiple_of(item * ITEM_ROWS + count, 16)
        dst_at = pl.multiple_of(slot * LANDING_ROWS + LANDING[stage - 1], 16)
        sem = (slot * STAGES + stage - 1) * len(GROUPS) + group
        return pltpu.make_async_remote_copy(
            src_ref=terms.at[pl.ds(src_at, count), pl.ds(lane, width)],
            dst_ref=landing.at[pl.ds(dst_at, count), pl.ds(lane, width)],
            send_sem=item_send.at[sem],
            recv_sem=item_recv.at[sem],
            device_id=across[order[stage - 1]],
            device_id_type=MESH,
        )

    def start_stage(stage, item):
        for group in range(len(GROUPS)):
            item_copy(stage, item, group).start()

    def store_sum(item, kind, values):
        if kind == 1:
            at = pl.multiple_of((item - 6) * 16, 16)
            out_fc2[pl.ds(at, 16), :] = values
            return
        parts = (
            (0, 16, values[:, :256], values[:, 256:512]),
            (16, 8, values[:8, 512:], values[8:, 512:]),
        )
        for top, count, left, right in parts:
            here = pl.ds(top, count)
            if kind == 0:
                col = pl.multiple_of(item * 512, 512)
                out_fc1[here, pl.ds(col, 256)] = left
                out_fc1[here, pl.ds(col + 256, 256)] = right
            else:
                col = pl.multiple_of((item - 12) * 128, 128)
                out_qkv[here, pl.ds(D + col, 128)] = left[:, :128]
                out_qkv[here, pl.ds(2 * D + col, 128)] = left[:, 128:]
                out_qkv[here, pl.ds(col, 128)] = right[:, :128]
                out_out[here, pl.ds(col, 128)] = right[:, 128:]

    def finish_stage(stage, item, low, high):
        for group in range(len(GROUPS)):
            item_copy(stage, item, group).wait()
        count = ITEM_ROWS >> stage
        slot = lax.rem(item, SLOTS)
        here = pl.ds(pl.multiple_of(item * ITEM_ROWS, 16), count)
        came = pl.ds(pl.multiple_of(slot * LANDING_ROWS + LANDING[stage - 1], 16), count)
        if stage < STAGES:
            terms[here, :] = terms[here, :] + landing[came, :]
            start_stage(stage + 1, item)
            return
        values = terms[here, :].astype(f32) + landing[came, :].astype(f32)
        for kind in range(3):
            if high < 6 * kind or low >= 6 * kind + 6:
                continue
            if low >= 6 * kind and high < 6 * kind + 6:
                store_sum(item, kind, values)
            else:
                pl.when((item >= 6 * kind) & (item < 6 * kind + 6))(
                    functools.partial(store_sum, item, kind, values)
                )

    def tick(number, low, high):
        number = jnp.int32(number)
        for stage in range(STAGES, 0, -1):
            first, last = low - APART * stage, high - APART * stage
            if last < 0 or first >= ITEMS:
                continue
            item = number - APART * stage
            act = functools.partial(
                finish_stage, stage, item, max(first, 0), min(last, ITEMS - 1)
            )
            if first >= 0 and last < ITEMS:
                act()
            else:
                pl.when((item >= 0) & (item < ITEMS))(act)
        if high < ITEMS:
            start_stage(1, number)

    def put_24(item, values):
        base_row = item * ITEM_ROWS
        for d in range(32):
            top = values[24 * d : 24 * d + 16, :]
            rest = values[24 * d + 16 : 24 * d + 24, :]
            rest = jnp.concatenate([rest[:, :256], rest[:, 256:]], axis=0)
            block = jnp.concatenate([top, rest], axis=1).astype(bf16)
            for order, lane, width in GROUPS:
                at = pl.multiple_of(base_row + 16 * place_of(order, bits_of(d)), 16)
                terms[pl.ds(at, 16), lane : lane + width] = block[:, lane : lane + width]

    row_tiles = rows // ROW_TILE

    def tile(t):
        return pl.ds(pl.multiple_of(t * ROW_TILE, ROW_TILE), ROW_TILE)

    def first_norm(src, part):
        gain, offset = row(ln1_gain), row(ln1_bias)

        def step(t, carry):
            unit, _ = unit_of(src[tile(t), :].astype(f32))
            normed = (unit * gain + offset).astype(bf16)
            nrm[tile(t), :] = normed
            at = pl.multiple_of(part * rows + t * ROW_TILE, ROW_TILE)
            nrm_t[:, pl.ds(at, ROW_TILE)] = normed.T
            return carry

        lax.fori_loop(0, row_tiles, step, 0)

    def set_bias(part):
        clip_col = clips_at(base + lax.broadcasted_iota(jnp.int32, (rows, rows), 0))
        tag_row = jnp.broadcast_to(tags[part, 0:1, :], (rows, rows))
        allowed = tag_row == clip_col
        if part == 0:
            here = lax.broadcasted_iota(jnp.int32, (rows, rows), 0)
            there = lax.broadcasted_iota(jnp.int32, (rows, rows), 1)
            allowed = allowed | (here == there)
        bias[...] = jnp.where(allowed, 0.0, masked_score)

    loads[0].wait()
    first_norm(tok, 0)
    set_bias(0)
    loads[1].wait()
    wide = 256

    def project(kind, add, scale, dst, dst_at):
        def step(c, carry):
            col = pl.multiple_of(c * wide, wide)
            out = dot(nrm[...], wqkv[:, pl.ds(kind * D + col, wide)])
            if add is not None:
                out = out + add[pl.ds(col, wide)].reshape(1, wide)
            out = out.astype(bf16)
            if scale:
                out = out * jnp.bfloat16(score_scale)
            dst[:, pl.ds(dst_at + col, wide)] = out
            return carry

        lax.fori_loop(0, D // wide, step, 0)

    project(0, q_bias, True, qkv, 0)
    project(1, None, False, qkv, D)
    project(2, v_bias, False, qkv, 2 * D)

    low_lane = lax.broadcasted_iota(jnp.int32, (rows, 128), 1) < 64

    def half(values, h):
        return jnp.where(low_lane if h == 0 else ~low_lane, values, jnp.zeros_like(values))

    def e_copy(number, slot, out):
        if out:
            return pltpu.make_async_copy(ering.at[slot], e_hbm.at[number], e_sem.at[slot])
        return pltpu.make_async_copy(e_hbm.at[number], ering.at[slot], e_sem.at[slot])

    MIXED, F_OWN, F_TWIN, RES, ACC, GNT = range(6)

    def forward_pair(part, hp, key_ref, key_at, value_at):
        col = pl.multiple_of(hp * 128, 128)
        cols = pl.ds(col, 128)
        number = part * PAIRS + hp
        slot = number % RING

        @pl.when(number >= RING)
        def _():
            e_copy(number - RING, slot, True).wait()

        q = qkv[:, cols]
        k = key_ref[:, pl.ds(key_at + col, 128)]
        v = key_ref[:, pl.ds(value_at + col, 128)]
        outs, tops = [], []
        for h in range(2):
            scores = dot_nt(q, half(k, h)) + bias[...]
            top = jnp.max(scores, axis=1, keepdims=True)
            e = jnp.exp(scores - top).astype(bf16)
            ering[slot, h] = e
            ones = jnp.ones_like(v)
            outs.append(dot(e, jnp.where(low_lane if h == 0 else ~low_lane, v, ones)))
            tops.append(top)
        e_copy(number, slot, True).start()
        weighted = jnp.where(low_lane, outs[0], outs[1])
        sums = pltpu.roll(jnp.where(low_lane, outs[1], outs[0]), 64, 1)
        top = jnp.where(low_lane, tops[0], tops[1])
        if part == 0:
            slots[MIXED, :, cols] = weighted
            slots[F_OWN, :, cols] = sums
            slots[F_TWIN, :, cols] = top
        else:
            top_own = slots[F_TWIN, :, cols]
            both = jnp.maximum(top_own, top)
            scale_own = jnp.exp(top_own - both)
            scale_twin = jnp.exp(top - both)
            inverse = 1.0 / (scale_own * slots[F_OWN, :, cols] + scale_twin * sums)
            scale_own = scale_own * inverse
            scale_twin = scale_twin * inverse
            slots[MIXED, :, cols] = scale_own * slots[MIXED, :, cols] + scale_twin * weighted
            slots[F_OWN, :, cols] = scale_own
            slots[F_TWIN, :, cols] = scale_twin

    def pairs_loop(body):
        def step(hp, carry):
            body(hp)
            return carry

        lax.fori_loop(0, PAIRS, step, 0)

    pairs_loop(lambda hp: forward_pair(0, hp, qkv, D, 2 * D))

    send_tok.wait()
    send_tags.wait()
    first_norm(tokp, 1)
    set_bias(1)
    project(1, None, False, kvp, 0)
    project(2, v_bias, False, kvp, D)
    pairs_loop(lambda hp: forward_pair(1, hp, kvp, 0, D))

    loads[2].wait()

    def branch(c, carry):
        cols = pl.ds(pl.multiple_of(c * wide, wide), wide)
        out = dot(slots[MIXED].astype(bf16), wout[:, cols])
        out = out + out_bias[cols].reshape(1, wide)
        slots[RES, :, cols] = tok[:, cols].astype(f32) + out
        return carry

    lax.fori_loop(0, D // wide, branch, 0)
    gain_two, offset_two = row(ln2_gain), row(ln2_bias)

    def second_norm(t, carry):
        unit, _ = unit_of(slots[RES, tile(t), :])
        normed = (unit * gain_two + offset_two).astype(bf16)
        nrm[tile(t), :] = normed
        nrm2_t[:, tile(t)] = normed.T
        slots[ACC, tile(t), :] = jnp.zeros((ROW_TILE, D), f32)
        slots[GNT, tile(t), :] = jnp.zeros((ROW_TILE, D), f32)
        return carry

    lax.fori_loop(0, row_tiles, second_norm, 0)

    loads[3].wait()
    loads[4].wait()
    loads[5].wait()

    def feed(c, carry):
        units = pl.ds(pl.multiple_of(c * FF_CHUNK, FF_CHUNK), FF_CHUNK)
        w1 = wfc1[:, units]
        w2 = wfc2[units, :]
        pre = dot(nrm[...], w1) + fc1_bias[units].reshape(1, FF_CHUNK)
        phi = 0.5 * (1.0 + lax.erf(pre * 0.7071067811865476))
        slope = phi + pre * jnp.exp(-0.5 * pre * pre) * 0.3989422804014327
        activated = (pre * phi).astype(bf16)
        grad_pre = (dot_nt(cot[...], w2) * slope).astype(bf16)
        slots[ACC] += dot(activated, w2)
        slots[GNT] += dot_nt(grad_pre, w1)
        ering[c // 2, lax.rem(c, 2)] = activated
        fb1_ref[0:1, units] = column_sum(grad_pre.astype(f32))
        put_24(c, dot(nrm2_t[...], grad_pre))
        tick(c, 0, FF // FF_CHUNK - 1)
        return carry

    for number in range(2 * PAIRS - RING, 2 * PAIRS):
        e_copy(number, number % RING, True).wait()
    lax.fori_loop(0, FF // FF_CHUNK, feed, 0)

    def weight_fc2(c, carry):
        pieces = []
        for p in range(3):
            piece = 3 * c + p
            chunk = piece // 2
            lanes = pl.ds(pl.multiple_of(256 * lax.rem(piece, 2), 256), 256)
            part = ering[chunk // 2, lax.rem(chunk, 2), :, lanes]
            pieces.append(dot_tn(part, cot[...]))
        values = jnp.concatenate(pieces, axis=0)
        for low in range(8):
            there = bits_of(low)
            there["z0"] = lax.rem(c, 2)
            there["z1"] = c // 2
            for order, lane, width in GROUPS:
                place = 16 * place_of(order, there)
                for j in range(6):
                    top = 96 * low + 16 * j
                    block = values[top : top + 16, lane : lane + width].astype(bf16)
                    at = pl.multiple_of((6 + j) * ITEM_ROWS + place, 16)
                    terms[pl.ds(at, 16), lane : lane + width] = block
        return carry

    lax.fori_loop(0, 4, weight_fc2, 0)
    tick(6, 6, 6)
    back_order = [PAIRS + hp for hp in range(PAIRS)] + list(range(PAIRS))

    def e_number(step):
        return lax.rem(step + PAIRS, 2 * PAIRS)

    for step in range(RING):
        e_copy(back_order[step], step % RING, False).start()

    vec_ref[...] = jnp.zeros(vec_ref.shape, f32)
    fb1_ref[1:8, :] = jnp.zeros((7, FF), f32)
    (V_LN1G, V_LN1B, V_QB, V_VB, V_OB, V_LN2G, V_LN2B, V_FC2B) = range(8)

    def add_vec(kind, values):
        vec_ref[kind : kind + 1, :] += column_sum(values)

    def second_back(t, carry):
        here = tile(t)
        unit, inverse = unit_of(slots[RES, here, :])
        result_ref[0, here, :] = (
            slots[RES, here, :] + slots[ACC, here, :] + row(fc2_bias)
        ).astype(bf16)
        upstream = slots[GNT, here, :]
        grad_out = cot[here, :].astype(f32)
        add_vec(V_FC2B, grad_out)
        add_vec(V_LN2G, upstream * unit)
        add_vec(V_LN2B, upstream)
        scaled = upstream * gain_two
        grad = grad_out + inverse * (
            scaled
            - jnp.mean(scaled, axis=1, keepdims=True)
            - unit * jnp.mean(scaled * unit, axis=1, keepdims=True)
        )
        slots[RES, here, :] = grad
        low = grad.astype(bf16)
        nrm[here, :] = low
        add_vec(V_OB, low.astype(f32))
        return carry

    lax.fori_loop(0, row_tiles, second_back, 0)
    tick(7, 7, 7)

    GQ = ACC

    def mixed_back(c, carry):
        cols = pl.ds(pl.multiple_of(c * wide, wide), wide)
        gm[:, cols] = dot_nt(nrm[...], wout[cols, :]).astype(bf16)
        mixed = slots[MIXED, :, cols].astype(bf16)
        wfc1[cols, :D] = dot_tn(mixed, nrm[...]).astype(bf16)
        return carry

    lax.fori_loop(0, D // wide, mixed_back, 0)
    tick(8, 8, 8)

    def backward_pair(part, hp, key_ref, key_at, value_at):
        col = pl.multiple_of(hp * 128, 128)
        cols = pl.ds(col, 128)
        step = (1 - part) * PAIRS + hp
        slot = step % RING
        q = qkv[:, cols]
        k = key_ref[:, pl.ds(key_at + col, 128)]
        v = key_ref[:, pl.ds(value_at + col, 128)]
        grad_in = gm[:, cols].astype(f32)
        factor = slots[F_OWN if part == 0 else F_TWIN, :, cols]
        product = grad_in * slots[MIXED, :, cols] * factor
        scaled = (grad_in * factor).astype(bf16)
        q_t = q.T
        scaled_t = scaled.T
        e_copy(e_number(step), slot, False).wait()
        grad_q = None
        grad_k, grad_v = [], []
        for h in range(2):
            delta = jnp.sum(half(product, h), axis=1, keepdims=True)
            e = ering[slot, h]
            grad_probs = dot_nt(scaled, half(v, h))
            grad_scores = (e.astype(f32) * (grad_probs - delta)).astype(bf16)
            term = dot(grad_scores, half(k, h))
            grad_q = term if grad_q is None else grad_q + term
            grad_k.append(dot(q_t[64 * h : 64 * h + 64], grad_scores))
            grad_v.append(dot(scaled_t[64 * h : 64 * h + 64], e))

        @pl.when(step + RING < 2 * PAIRS)
        def _():
            e_copy(e_number(step + RING), slot, False).start()

        key_ref[:, pl.ds(key_at + col, 128)] = jnp.concatenate(grad_k, axis=0).T.astype(bf16)
        key_ref[:, pl.ds(value_at + col, 128)] = jnp.concatenate(grad_v, axis=0).T.astype(bf16)
        if part == 1:
            slots[GQ, :, cols] = grad_q
        else:
            total_q = (slots[GQ, :, cols] + grad_q) * score_scale
            qkv[:, cols] = total_q.astype(bf16)

    def twin_step(step, carry):
        for p in range(2):
            backward_pair(1, 2 * step + p, kvp, 0, D)
        tick(9 + step, 9, 11)
        return carry

    lax.fori_loop(0, PAIRS // 2, twin_step, 0)

    def partial_out(c, carry):
        cols = pl.ds(pl.multiple_of(c * wide, wide), wide)
        tokp[:, cols] = dot_nt(kvp[...], wqkv[cols, D : 3 * D]).astype(bf16)
        return carry

    lax.fori_loop(0, D // wide, partial_out, 0)
    send_gn = to_twin(2, tokp, gn_in)
    send_gn.start()

    def own_step(hp, carry):
        backward_pair(0, hp, qkv, D, 2 * D)
        col = pl.multiple_of(hp * 128, 128)
        grad_q = qkv[:, pl.ds(col, 128)]
        own = jnp.concatenate(
            [qkv[:, pl.ds(D + col, 128)], qkv[:, pl.ds(2 * D + col, 128)]], axis=1
        )
        other = jnp.concatenate(
            [kvp[:, pl.ds(col, 128)], kvp[:, pl.ds(D + col, 128)]], axis=1
        )
        vec_ref[V_QB : V_QB + 1, pl.ds(col, 128)] = column_sum(grad_q.astype(f32))
        vec_ref[V_VB : V_VB + 1, pl.ds(col, 128)] = column_sum(
            own[:, 128:].astype(f32) + other[:, 128:].astype(f32)
        )
        weight_kv = dot(nrm_t[...], jnp.concatenate([own, other], axis=0))
        weight_q = dot(nrm_t[:, :rows], grad_q)
        weight_o = wfc1[:, pl.ds(col, 128)].astype(f32)
        put_24(12 + hp, jnp.concatenate([weight_kv, weight_q, weight_o], axis=1))
        tick(12 + hp, 12, 17)
        return carry

    lax.fori_loop(0, PAIRS, own_step, 0)

    def first_back_product(c, carry):
        cols = pl.ds(pl.multiple_of(c * wide, wide), wide)
        slots[GNT, :, cols] = dot_nt(qkv[...], wqkv[cols, :])
        return carry

    lax.fori_loop(0, D // wide, first_back_product, 0)
    tick(18, 18, 18)
    send_gn.wait()
    gain_one = row(ln1_gain)

    def first_back(t, carry):
        here = tile(t)
        unit, inverse = unit_of(tok[here, :].astype(f32))
        upstream = slots[GNT, here, :] + gn_in[here, :].astype(f32)
        add_vec(V_LN1G, upstream * unit)
        add_vec(V_LN1B, upstream)
        scaled = upstream * gain_one
        grad = slots[RES, here, :] + inverse * (
            scaled
            - jnp.mean(scaled, axis=1, keepdims=True)
            - unit * jnp.mean(scaled * unit, axis=1, keepdims=True)
        )
        gtok_ref[0, here, :] = grad.astype(bf16)
        return carry

    lax.fori_loop(0, row_tiles, first_back, 0)
    tick(19, 19, 19)

    def window(ref, first, count):
        block = first // 128 * 128
        shift = first - block
        wide_enough = 256 if shift + count > 128 else 128
        piece = ref[:, block : block + wide_enough]
        if shift:
            piece = pltpu.roll(piece, wide_enough - shift, 1)
        return piece[:, :128]

    small_order = GROUPS[0][0]
    for d in range(32):
        at = pl.multiple_of(16 * place_of(small_order, bits_of(d)), 16)
        small[pl.ds(at, 8), :] = window(vec_ref, 24 * d, 24)
        small[pl.ds(at + 8, 8), :] = window(fb1_ref, 96 * d, 96)

    def small_copy(stage):
        count = ITEM_ROWS >> stage
        return pltpu.make_async_remote_copy(
            src_ref=small.at[pl.ds(count, count)],
            dst_ref=small_in.at[pl.ds(LANDING[stage - 1], count)],
            send_sem=small_send.at[stage - 1],
            recv_sem=small_recv.at[stage - 1],
            device_id=across[small_order[stage - 1]],
            device_id_type=MESH,
        )

    small_copy(1).start()
    for number in range(20, ITEMS + APART * STAGES):
        tick(number, number, number)
        if number % 2 == 1:
            stage = (number - 19) // 2
            count = ITEM_ROWS >> stage
            small_copy(stage).wait()
            small[:count] = small[:count] + small_in[LANDING[stage - 1] : LANDING[stage - 1] + count]
            if stage < STAGES:
                small_copy(stage + 1).start()
    small_copy(STAGES).wait()
    summed = small[:16] + small_in[LANDING[4] : LANDING[4] + 16]
    for kind, ref in enumerate(
        (out_ln1g, out_ln1b, out_qb, out_vb, out_ob, out_ln2g, out_ln2b, out_fb2)
    ):
        ref[...] = summed[kind, :24]
    out_fb1[...] = summed[8, :96]


def block_body(
    tokens,
    lengths,
    padding,
    cotangent,
    ln1_gain,
    ln1_bias,
    w_qkv,
    q_bias,
    v_bias,
    w_out,
    out_bias,
    ln2_gain,
    ln2_bias,
    w_fc1,
    fc1_bias,
    w_fc2,
    fc2_bias,
):
    rows = tokens.shape[1]
    n_dev = lax.axis_size("seq") * lax.axis_size("blk")
    shape = jax.ShapeDtypeStruct
    any_spec = pl.BlockSpec(memory_space=pl.ANY)
    vmem = pl.BlockSpec(memory_space=pltpu.VMEM)
    smem = pl.BlockSpec(memory_space=pltpu.SMEM)
    part = D // n_dev
    line = shape((part,), f32)
    outs = pl.pallas_call(
        block_kernel,
        name="block",
        out_shape=(
            shape((1, rows, D), bf16),
            shape((1, rows, D), bf16),
            line,
            line,
            shape((part, 3 * D), f32),
            line,
            line,
            shape((part, D), f32),
            line,
            line,
            line,
            shape((part, FF), f32),
            shape((FF // n_dev,), f32),
            shape((FF // n_dev, D), f32),
            line,
            shape((2 * PAIRS, 2, rows, rows), bf16),
        ),
        in_specs=[
            any_spec, smem, vmem, any_spec, vmem, vmem, any_spec, vmem, vmem,
            any_spec, vmem, vmem, vmem, any_spec, vmem, any_spec, vmem,
        ],
        out_specs=(vmem,) * 15 + (any_spec,),
        scratch_shapes=[
            pltpu.VMEM((D, 3 * D), bf16),
            pltpu.VMEM((D, D), bf16),
            pltpu.VMEM((D, FF), bf16),
            pltpu.VMEM((FF, D), bf16),
            pltpu.VMEM((rows, D), bf16),
            pltpu.VMEM((rows, D), bf16),
            pltpu.VMEM((rows, D), bf16),
            pltpu.VMEM((rows, D), bf16),
            pltpu.VMEM((D, 2 * rows), bf16),
            pltpu.VMEM((D, rows), bf16),
            pltpu.VMEM((rows, 3 * D), bf16),
            pltpu.VMEM((rows, 2 * D), bf16),
            pltpu.VMEM((rows, D), bf16),
            pltpu.VMEM((rows, rows), f32),
            pltpu.VMEM((RING, 2, rows, rows), bf16),
            pltpu.VMEM((6, rows, D), f32),
            pltpu.VMEM((ITEMS * ITEM_ROWS, ITEM_LANES), bf16),
            pltpu.VMEM((SLOTS * LANDING_ROWS, ITEM_LANES), bf16),
            pltpu.VMEM((rows, D), bf16),
            pltpu.VMEM((2, 8, rows), jnp.int32),
            pltpu.VMEM((8, D), f32),
            pltpu.VMEM((8, FF), f32),
            pltpu.VMEM((ITEM_ROWS, 128), f32),
            pltpu.VMEM((LANDING_ROWS, 128), f32),
            pltpu.SemaphoreType.DMA((6,)),
            pltpu.SemaphoreType.DMA((RING,)),
            pltpu.SemaphoreType.DMA((3,)),
            pltpu.SemaphoreType.DMA((3,)),
            pltpu.SemaphoreType.DMA((SLOTS * STAGES * len(GROUPS),)),
            pltpu.SemaphoreType.DMA((SLOTS * STAGES * len(GROUPS),)),
            pltpu.SemaphoreType.DMA((STAGES,)),
            pltpu.SemaphoreType.DMA((STAGES,)),
        ],
        compiler_params=pltpu.CompilerParams(
            collective_id=0, has_side_effects=True, vmem_limit_bytes=VMEM_LIMIT
        ),
        cost_estimate=pl.CostEstimate(
            flops=30 * 10**9, bytes_accessed=60 * 10**6, transcendentals=10**7
        ),
    )(
        tokens, lengths, padding, cotangent, ln1_gain, ln1_bias, w_qkv, q_bias, v_bias,
        w_out, out_bias, ln2_gain, ln2_bias, w_fc1, fc1_bias, w_fc2, fc2_bias,
    )
    return outs[:15]


VMEM_LIMIT = 63 * 2**20


def solution(mesh):
    in_specs = (
        P("seq", "blk", None),
        P("seq", None),
        P("seq", "blk"),
        P("seq", "blk", None),
        P(),
        P(),
        P(),
        P(),
        P(),
        P(),
        P(),
        P(),
        P(),
        P(),
        P(),
        P(),
        P(),
    )
    out_specs = (
        P("seq", "blk", None),
        P("seq", "blk", None),
        P(("seq", "blk")),
        P(("seq", "blk")),
        P(("seq", "blk"), None),
        P(("seq", "blk")),
        P(("seq", "blk")),
        P(("seq", "blk"), None),
        P(("seq", "blk")),
        P(("seq", "blk")),
        P(("seq", "blk")),
        P(("seq", "blk"), None),
        P(("seq", "blk")),
        P(("seq", "blk"), None),
        P(("seq", "blk")),
    )
    step = block_body if fits(mesh) else body
    return jax.shard_map(step, mesh=mesh, in_specs=in_specs, out_specs=out_specs, check_vma=False)
```

```python
import functools

import jax
import jax.numpy as jnp
from jax import lax
from jax.experimental import pallas as pl
from jax.experimental.pallas import tpu as pltpu
from jax.sharding import PartitionSpec as P

D = 768
FF = 3072
HEADS = 12
HEAD_DIM = 64


epsilon = 1e-06
score_scale = 0.125
masked_score = -1e30


def clip_numbers(clip_lengths, positions):
    bounds = jnp.cumsum(clip_lengths)
    return jnp.sum((positions[:, None] >= bounds[None, :]).astype(jnp.int32), axis=1)


def normalize(values, scales, offset):
    center = values - jnp.mean(values, axis=-1, keepdims=True)
    spread = jnp.mean(center * center, axis=-1, keepdims=True)
    inverse = lax.rsqrt(spread + epsilon)
    unit = center * inverse
    return (unit * scales + offset, unit, inverse)


def norm_back(upstream, unit, inverse, scales):
    scaled = upstream * scales
    return inverse * (
        scaled
        - jnp.mean(scaled, axis=-1, keepdims=True)
        - unit * jnp.mean(scaled * unit, axis=-1, keepdims=True)
    )


def gelu_slope(pre_gelu):
    cdf_part = 0.5 * (1.0 + lax.erf(pre_gelu * 0.7071067811865476))
    return cdf_part + pre_gelu * jnp.exp(-0.5 * pre_gelu * pre_gelu) * 0.3989422804014327


def masked_scores(query_heads, key_heads, clip_ids, positions, block_tags, key_pos):
    raw_scores = (
        jnp.einsum("qhd,khd->qhk", query_heads, key_heads, preferred_element_type=jnp.float32)
        * score_scale
    )
    allowed = (block_tags[None, :] == clip_ids[:, None]) | (positions[:, None] == key_pos[None, :])
    return jnp.where(allowed[:, None, :], raw_scores, masked_score)


def score_grads(
    query_heads,
    key_heads,
    value_heads,
    grad_heads,
    log_total,
    row_delta,
    clip_ids,
    positions,
    block_tags,
    key_pos,
):
    scores = masked_scores(query_heads, key_heads, clip_ids, positions, block_tags, key_pos)
    attn_probs = jnp.exp(scores - log_total[..., None])
    grad_probs = jnp.einsum(
        "qhd,khd->qhk", grad_heads, value_heads, preferred_element_type=jnp.float32
    )
    grad_scores = (attn_probs * (grad_probs - row_delta[..., None])).astype(jnp.bfloat16)
    return (attn_probs, grad_scores)


def stage_orders():
    seq_bits = lax.axis_size("seq").bit_length() - 1
    blk_bits = lax.axis_size("blk").bit_length() - 1
    seq_stages = [blk_bits + b for b in range(seq_bits)]
    blk_stages = list(range(blk_bits))
    one = seq_stages[:2] + blk_stages + seq_stages[2:]
    two = seq_stages[:1] + blk_stages + seq_stages[1:]
    return one, two


def scatter_stages(terms, order):
    n_dev = terms.shape[0]
    bits = n_dev.bit_length() - 1
    me = lax.axis_index("seq") * lax.axis_size("blk") + lax.axis_index("blk")
    rest = terms.shape[1:]
    kind = terms.dtype
    held = terms.reshape((2,) * bits + rest)
    for number, bit in enumerate(order):
        axis = bits - 1 - bit
        mine = (me >> bit) & 1
        sent = lax.dynamic_slice_in_dim(held, 1 - mine, 1, axis)
        kept = lax.dynamic_slice_in_dim(held, mine, 1, axis)
        swap = [(i, i ^ (1 << bit)) for i in range(n_dev)]
        came = lax.ppermute(sent, ("seq", "blk"), swap)
        total = kept.astype(jnp.float32) + came.astype(jnp.float32)
        held = total if number == bits - 1 else total.astype(kind)
    return held.reshape((1,) + rest)


def scatter_sum(grad):
    n_dev = lax.axis_size("seq") * lax.axis_size("blk")
    rows, width = grad.shape
    terms = grad.astype(jnp.bfloat16).reshape(n_dev, rows // n_dev, width)
    one, two = stage_orders()
    left = scatter_stages(terms[:, :, : width // 2], one)[0]
    right = scatter_stages(terms[:, :, width // 2 :], two)[0]
    return jnp.concatenate([left, right], axis=1)


def body(
    tokens,
    lengths,
    padding,
    cotangent,
    ln1_gain,
    ln1_bias,
    w_qkv,
    q_bias,
    v_bias,
    w_out,
    out_bias,
    ln2_gain,
    ln2_bias,
    w_fc1,
    fc1_bias,
    w_fc2,
    fc2_bias,
):
    tok_rows = tokens.shape[1]
    group_size = lax.axis_size("blk")
    n_dev = lax.axis_size("seq") * group_size
    positions = lax.axis_index("blk") * tok_rows + jnp.arange(tok_rows, dtype=jnp.int32)
    clip_ids = clip_numbers(lengths[0], positions)
    key_tags = jnp.where(padding[0] == 1, -1, clip_ids)
    tokens_f32 = tokens[0].astype(jnp.float32)
    first_norm, unit_one, inverse_one = normalize(tokens_f32, ln1_gain, ln1_bias)
    normed_one = first_norm.astype(jnp.bfloat16)
    joint_bias = jnp.concatenate([q_bias, jnp.zeros_like(q_bias), v_bias])
    projected = (
        jnp.dot(normed_one, w_qkv, preferred_element_type=jnp.float32) + joint_bias
    ).astype(jnp.bfloat16)
    keys_own = projected[:, D : 2 * D]
    values_own = projected[:, 2 * D :]
    query_heads = projected[:, :D].reshape(tok_rows, HEADS, HEAD_DIM)
    starts = jnp.arange(group_size, dtype=jnp.int32) * tok_rows

    def fold_keys(running, key_block, offset):
        block_keys, block_values, block_tags = key_block
        key_count = block_keys.shape[0]
        key_pos = offset + jnp.arange(key_count, dtype=jnp.int32)
        scores = masked_scores(
            query_heads,
            block_keys.reshape(key_count, HEADS, HEAD_DIM),
            clip_ids,
            positions,
            block_tags,
            key_pos,
        )
        row_max, row_sum, weighted = running
        new_max = jnp.maximum(row_max, jnp.max(scores, axis=-1))
        rescale = jnp.exp(row_max - new_max)
        exp_scores = jnp.exp(scores - new_max[..., None])
        row_sum = row_sum * rescale + jnp.sum(exp_scores, axis=-1)
        weighted = weighted * rescale[..., None] + jnp.einsum(
            "qhk,khd->qhd",
            exp_scores.astype(jnp.bfloat16),
            block_values.reshape(key_count, HEADS, HEAD_DIM),
            preferred_element_type=jnp.float32,
        )
        return (new_max, row_sum, weighted)

    start_state = (
        jnp.full((tok_rows, HEADS), masked_score, jnp.float32),
        jnp.zeros((tok_rows, HEADS), jnp.float32),
        jnp.zeros((tok_rows, HEADS, HEAD_DIM), jnp.float32),
    )
    group_keys, group_values, group_tags = (
        lax.all_gather(keys_own, "blk", axis=0, tiled=True),
        lax.all_gather(values_own, "blk", axis=0, tiled=True),
        lax.all_gather(key_tags, "blk", axis=0, tiled=True),
    )

    def scan_fold(running, scan_args):
        return (fold_keys(running, (scan_args[0], scan_args[1], scan_args[2]), scan_args[3]), None)

    final_state = lax.scan(
        scan_fold,
        start_state,
        (
            group_keys.reshape(group_size, tok_rows, D),
            group_values.reshape(group_size, tok_rows, D),
            group_tags.reshape(group_size, tok_rows),
            starts,
        ),
    )[0]
    row_max, row_sum, weighted = final_state
    mixed_f32 = weighted / row_sum[..., None]
    log_total = row_max + jnp.log(row_sum)
    mixed = mixed_f32.reshape(tok_rows, D).astype(jnp.bfloat16)
    residual = tokens_f32 + jnp.dot(mixed, w_out, preferred_element_type=jnp.float32) + out_bias
    second_norm, unit_two, inverse_two = normalize(residual, ln2_gain, ln2_bias)
    normed_two = second_norm.astype(jnp.bfloat16)
    pre_gelu = jnp.dot(normed_two, w_fc1, preferred_element_type=jnp.float32) + fc1_bias
    activated = jax.nn.gelu(pre_gelu, approximate=False).astype(jnp.bfloat16)
    result = (
        residual + jnp.dot(activated, w_fc2, preferred_element_type=jnp.float32) + fc2_bias
    ).astype(jnp.bfloat16)
    grad_out = cotangent[0]
    grad_fc2_bias = jnp.sum(grad_out, axis=0, dtype=jnp.float32)
    grad_w_fc2 = jnp.einsum("tf,td->fd", activated, grad_out, preferred_element_type=jnp.float32)
    grad_act = jnp.einsum("td,fd->tf", grad_out, w_fc2, preferred_element_type=jnp.float32)
    grad_pre = (grad_act * gelu_slope(pre_gelu)).astype(jnp.bfloat16)
    grad_fc1_bias = jnp.sum(grad_pre, axis=0, dtype=jnp.float32)
    grad_w_fc1 = jnp.einsum("td,tf->df", normed_two, grad_pre, preferred_element_type=jnp.float32)
    grad_norm_two = jnp.einsum("tf,df->td", grad_pre, w_fc1, preferred_element_type=jnp.float32)
    grad_ln2_gain = jnp.sum(grad_norm_two * unit_two, axis=0)
    grad_ln2_bias = jnp.sum(grad_norm_two, axis=0)
    grad_residual = grad_out.astype(jnp.float32) + norm_back(
        grad_norm_two, unit_two, inverse_two, ln2_gain
    )
    grad_branch = grad_residual.astype(jnp.bfloat16)
    grad_out_bias = jnp.sum(grad_branch, axis=0, dtype=jnp.float32)
    grad_w_out = jnp.einsum("td,te->de", mixed, grad_branch, preferred_element_type=jnp.float32)
    grad_mixed = jnp.einsum(
        "te,de->td", grad_branch, w_out, preferred_element_type=jnp.float32
    ).astype(jnp.bfloat16)
    grad_heads = grad_mixed.reshape(tok_rows, HEADS, HEAD_DIM)
    row_delta = jnp.sum(grad_heads * mixed_f32, axis=-1)
    key_stack = (
        group_keys.reshape(group_size, tok_rows, D),
        group_values.reshape(group_size, tok_rows, D),
        group_tags.reshape(group_size, tok_rows),
        starts,
    )

    def back_block(grad_queries, scan_args):
        block_keys, block_values, block_tags, offset = scan_args
        key_pos = offset + jnp.arange(tok_rows, dtype=jnp.int32)
        key_heads = block_keys.reshape(tok_rows, HEADS, HEAD_DIM)
        value_heads = block_values.reshape(tok_rows, HEADS, HEAD_DIM)
        attn_probs, grad_scores = score_grads(
            query_heads,
            key_heads,
            value_heads,
            grad_heads,
            log_total,
            row_delta,
            clip_ids,
            positions,
            block_tags,
            key_pos,
        )
        grad_values = jnp.einsum(
            "qhk,qhd->khd",
            attn_probs.astype(jnp.bfloat16),
            grad_heads,
            preferred_element_type=jnp.float32,
        )
        grad_queries = (
            grad_queries
            + jnp.einsum("qhk,khd->qhd", grad_scores, key_heads, preferred_element_type=jnp.float32)
            * score_scale
        )
        grad_keys = (
            jnp.einsum("qhk,qhd->khd", grad_scores, query_heads, preferred_element_type=jnp.float32)
            * score_scale
        )
        return (
            grad_queries,
            jnp.concatenate(
                [grad_keys.reshape(tok_rows, D), grad_values.reshape(tok_rows, D)], axis=1
            ),
        )

    grad_queries, key_terms = lax.scan(
        back_block, jnp.zeros((tok_rows, HEADS, HEAD_DIM), jnp.float32), key_stack
    )
    key_sums = lax.psum_scatter(
        key_terms.reshape(group_size * tok_rows, 2 * D).astype(jnp.bfloat16),
        "blk",
        scatter_dimension=0,
        tiled=True,
    )
    grad_qkv = jnp.concatenate(
        [grad_queries.reshape(tok_rows, D).astype(jnp.bfloat16), key_sums], axis=1
    )
    grad_q_bias = jnp.sum(grad_qkv[:, :D], axis=0, dtype=jnp.float32)
    grad_v_bias = jnp.sum(grad_qkv[:, 2 * D :], axis=0, dtype=jnp.float32)
    grad_w_qkv = jnp.einsum("td,te->de", normed_one, grad_qkv, preferred_element_type=jnp.float32)
    grad_norm_one = jnp.einsum("te,de->td", grad_qkv, w_qkv, preferred_element_type=jnp.float32)
    grad_ln1_gain = jnp.sum(grad_norm_one * unit_one, axis=0)
    grad_ln1_bias = jnp.sum(grad_norm_one, axis=0)
    grad_tokens = (
        grad_residual + norm_back(grad_norm_one, unit_one, inverse_one, ln1_gain)
    ).astype(jnp.bfloat16)
    small = jnp.concatenate(
        [
            v.reshape(n_dev, -1)
            for v in (
                grad_ln1_gain,
                grad_ln1_bias,
                grad_q_bias,
                grad_v_bias,
                grad_out_bias,
                grad_ln2_gain,
                grad_ln2_bias,
                grad_fc1_bias,
                grad_fc2_bias,
            )
        ],
        axis=1,
    )
    sum_fc2 = scatter_sum(grad_w_fc2)
    sum_fc1 = scatter_sum(grad_w_fc1)
    sum_out = scatter_sum(grad_w_out)
    sum_qkv = scatter_sum(grad_w_qkv)
    part = D // n_dev
    small = scatter_stages(small, stage_orders()[0])[0]
    pieces = []
    at = 0
    for size in (part, part, part, part, part, part, part, FF // n_dev, part):
        pieces.append(small[at : at + size])
        at += size
    summed = (
        pieces[0],
        pieces[1],
        sum_qkv,
        pieces[2],
        pieces[3],
        sum_out,
        pieces[4],
        pieces[5],
        pieces[6],
        sum_fc1,
        pieces[7],
        sum_fc2,
        pieces[8],
    )
    return (
        result[None],
        grad_tokens[None],
        summed[0],
        summed[1],
        summed[2],
        summed[3],
        summed[4],
        summed[5],
        summed[6],
        summed[7],
        summed[8],
        summed[9],
        summed[10],
        summed[11],
        summed[12],
    )


f32 = jnp.float32
bf16 = jnp.bfloat16
MESH = pl.DeviceIdType.MESH
PAIRS = HEADS // 2
FF_CHUNK = 512
ROW_TILE = 128
ITEMS = 18
ITEM_ROWS = 512
ITEM_LANES = 768
SLOTS = 4
STAGES = 5
STARTS = (0, 1, 2, 3, 4, 5, 7, 8, 9, 10, 11, 12, 15, 16, 17, 18, 19, 20)
ENDS = (0, 1, 3, 5, 7, 9)
LANDING = (0, 256, 384, 448, 480)
LANDING_ROWS = 496
FLAT_BITS = ("y", "c", "x", "z0", "z1")
GROUPS = (
    (("c", "x", "y", "z0", "z1"), 0, 512),
    (("c", "z0", "z1", "y", "x"), 512, 256),
)


def fits(mesh):
    return dict(mesh.shape) == {"seq": 16, "blk": 2}


def dot(a, b):
    return lax.dot_general(a, b, (((1,), (0,)), ((), ())), preferred_element_type=f32)


def dot_nt(a, b):
    return lax.dot_general(a, b, (((1,), (1,)), ((), ())), preferred_element_type=f32)


def dot_tn(a, b):
    return lax.dot_general(a, b, (((0,), (0,)), ((), ())), preferred_element_type=f32)


def aligned(at, step):
    return at if isinstance(at, int) else pl.multiple_of(at, step)


def unit_of(values):
    center = values - jnp.mean(values, axis=1, keepdims=True)
    inverse = lax.rsqrt(jnp.mean(center * center, axis=1, keepdims=True) + epsilon)
    return center * inverse, inverse


def row(ref):
    return ref[...].reshape(1, ref.shape[0])


def column_sum(values):
    return jnp.sum(values, axis=0, keepdims=True)


def block_kernel(
    tok_hbm,
    len_ref,
    pad_ref,
    cot_hbm,
    ln1_gain,
    ln1_bias,
    wqkv_hbm,
    q_bias,
    v_bias,
    wout_hbm,
    out_bias,
    ln2_gain,
    ln2_bias,
    wfc1_hbm,
    fc1_bias,
    wfc2_hbm,
    fc2_bias,
    result_hbm,
    gtok_hbm,
    out_ln1g,
    out_ln1b,
    out_qkv,
    out_qb,
    out_vb,
    out_out,
    out_ob,
    out_ln2g,
    out_ln2b,
    out_fc1,
    out_fb1,
    out_fc2,
    out_fb2,
    e_hbm,
    wqkv,
    wout,
    wfc1,
    wfc2,
    tok,
    tokp,
    cot,
    nrm,
    unit_t,
    nrm2_t,
    qkv,
    kvp,
    gm,
    bias,
    ering,
    slots,
    terms,
    landing,
    gn_in,
    tags,
    vec_ref,
    fb1_ref,
    small,
    small_in,
    cs_ref,
    cs_in,
    load_sem,
    e_sem,
    send_sem,
    recv_sem,
    item_send,
    item_recv,
    small_send,
    small_recv,
    sums_send,
    sums_recv,
):
    rows = tok.shape[0]
    seq = lax.axis_index("seq")
    blk = lax.axis_index("blk")
    bit = {
        "y": blk,
        "c": lax.rem(seq, 2),
        "x": lax.rem(seq // 2, 2),
        "z0": lax.rem(seq // 4, 2),
        "z1": seq // 8,
    }
    across = {
        "y": (seq, 1 - blk),
        "c": (seq + 1 - 2 * bit["c"], blk),
        "x": (seq + 2 - 4 * bit["x"], blk),
        "z0": (seq + 4 - 8 * bit["z0"], blk),
        "z1": (seq + 8 - 16 * bit["z1"], blk),
    }
    twin = across["y"]

    barrier = pltpu.get_barrier_semaphore()
    for name in FLAT_BITS:
        pl.semaphore_signal(barrier, inc=1, device_id=across[name], device_id_type=MESH)

    loads = [
        pltpu.make_async_copy(src, dst, load_sem.at[i])
        for i, (src, dst) in enumerate(
            (
                (tok_hbm.at[0], tok),
                (wqkv_hbm, wqkv),
                (wout_hbm, wout),
                (wfc1_hbm, wfc1),
                (wfc2_hbm, wfc2),
                (cot_hbm.at[0], cot),
            )
        )
    ]
    for copy in loads:
        copy.start()

    ends = []
    total = jnp.int32(0)
    for i in range(len_ref.shape[1]):
        total = total + len_ref[0, i]
        ends.append(total)

    def clips_at(positions):
        number = jnp.zeros_like(positions)
        for end in ends:
            number = number + jnp.where(positions >= end, 1, 0)
        return number

    base = blk * rows
    lane_pos = base + lax.broadcasted_iota(jnp.int32, (8, rows), 1)
    padding = jnp.broadcast_to(pad_ref[...], (8, rows))
    tags[0] = jnp.where(padding == 1, -1, clips_at(lane_pos))

    pl.semaphore_wait(barrier, len(FLAT_BITS))

    def to_twin(i, src, dst):
        return pltpu.make_async_remote_copy(
            src_ref=src,
            dst_ref=dst,
            send_sem=send_sem.at[i],
            recv_sem=recv_sem.at[i],
            device_id=twin,
            device_id_type=MESH,
        )

    part_rows = rows // 2
    send_tags = to_twin(1, tags.at[0], tags.at[1])
    send_tags.start()
    send_tok = []
    for part, sem in ((0, 0), (1, 4)):
        here = pl.ds(part * part_rows, part_rows)
        send_tok.append(to_twin(sem, tok_hbm.at[0, here], tokp.at[here]))
        send_tok[part].start()

    def place_of(order, there):
        at = 0
        for stage, name in enumerate(order):
            differs = there[name] + bit[name] - 2 * there[name] * bit[name]
            at = at + (16 >> stage) * differs
        return at

    def bits_of(d):
        return {name: (d >> i) & 1 for i, name in enumerate(FLAT_BITS)}

    def terms_of(item):
        if isinstance(item, int) and item >= 12:
            return wfc2, (item - 12) * ITEM_ROWS
        return terms, item * ITEM_ROWS

    def item_copies(stage, item):
        count = ITEM_ROWS >> stage
        slot = item % SLOTS if isinstance(item, int) else lax.rem(item, SLOTS)
        ref, first = terms_of(item)
        src_at = aligned(first + count, 16)
        dst_at = aligned(slot * LANDING_ROWS + LANDING[stage - 1], 16)
        copies = []
        for group, (order, lane, width) in enumerate(GROUPS):
            if stage == 1:
                if group > 0:
                    break
                width = ITEM_LANES
            lanes = pl.ds(lane, width)
            sem = (slot * STAGES + stage - 1) * len(GROUPS) + group
            copies.append(
                pltpu.make_async_remote_copy(
                    src_ref=ref.at[pl.ds(src_at, count), lanes],
                    dst_ref=landing.at[pl.ds(dst_at, count), lanes],
                    send_sem=item_send.at[sem],
                    recv_sem=item_recv.at[sem],
                    device_id=across[order[stage - 1]],
                    device_id_type=MESH,
                )
            )
        return copies

    def start_stage(stage, item):
        for copy in item_copies(stage, item):
            copy.start()

    def store_sum(item, kind, values):
        if kind == 1:
            at = aligned((item - 6) * 16, 16)
            out_fc2[pl.ds(at, 16), :] = values
            return
        parts = (
            (0, 16, values[:, :256], values[:, 256:512]),
            (16, 8, values[:8, 512:], values[8:, 512:]),
        )
        for top, count, left, right in parts:
            here = pl.ds(top, count)
            if kind == 0:
                col = aligned(item * 512, 512)
                out_fc1[here, pl.ds(col, 256)] = left
                out_fc1[here, pl.ds(col + 256, 256)] = right
            else:
                col = aligned((item - 12) * 128, 128)
                out_qkv[here, pl.ds(D + col, 128)] = left[:, :128]
                out_qkv[here, pl.ds(2 * D + col, 128)] = left[:, 128:]
                out_qkv[here, pl.ds(col, 128)] = right[:, :128]
                out_out[here, pl.ds(col, 128)] = right[:, 128:]

    def finish_stage(stage, item, low, high):
        for copy in item_copies(stage, item):
            copy.wait()
        count = ITEM_ROWS >> stage
        slot = item % SLOTS if isinstance(item, int) else lax.rem(item, SLOTS)
        ref, first = terms_of(item)
        here = pl.ds(aligned(first, 16), count)
        came = pl.ds(aligned(slot * LANDING_ROWS + LANDING[stage - 1], 16), count)
        if stage < STAGES:
            ref[here, :] = ref[here, :] + landing[came, :]
            start_stage(stage + 1, item)
            return
        values = ref[here, :].astype(f32) + landing[came, :].astype(f32)
        for kind in range(3):
            if high < 6 * kind or low >= 6 * kind + 6:
                continue
            if low >= 6 * kind and high < 6 * kind + 6:
                store_sum(item, kind, values)
            else:
                pl.when((item >= 6 * kind) & (item < 6 * kind + 6))(
                    functools.partial(store_sum, item, kind, values)
                )

    def feed_tick(number):
        for stage in range(STAGES, 0, -1):
            if ENDS[stage] < 6:
                item = number - ENDS[stage]
                act = functools.partial(finish_stage, stage, item, 0, 5)
                pl.when(item >= 0)(act)
        start_stage(1, number)

    def tick(number):
        for stage in range(STAGES, 0, -1):
            if number - ENDS[stage] in STARTS:
                item = STARTS.index(number - ENDS[stage])
                finish_stage(stage, item, item, item)
        if number in STARTS:
            start_stage(1, STARTS.index(number))

    def put_24(item, values):
        ref, base_row = terms_of(item)
        for d in range(32):
            top = values[24 * d : 24 * d + 16, :]
            rest = values[24 * d + 16 : 24 * d + 24, :]
            rest = jnp.concatenate([rest[:, :256], rest[:, 256:]], axis=0)
            block = jnp.concatenate([top, rest], axis=1).astype(bf16)
            for order, lane, width in GROUPS:
                at = pl.multiple_of(base_row + 16 * place_of(order, bits_of(d)), 16)
                ref[pl.ds(at, 16), lane : lane + width] = block[:, lane : lane + width]

    row_tiles = rows // ROW_TILE

    def tile(t):
        return pl.ds(pl.multiple_of(t * ROW_TILE, ROW_TILE), ROW_TILE)

    def first_norm(src, columns_at, first, last):
        gain, offset = row(ln1_gain), row(ln1_bias)

        def step(t, carry):
            unit, _ = unit_of(src[tile(t), :].astype(f32))
            normed = (unit * gain + offset).astype(bf16)
            nrm[tile(t), :] = normed
            at = pl.multiple_of(columns_at + t * ROW_TILE, ROW_TILE)
            unit_t[:, pl.ds(at, ROW_TILE)] = unit.astype(bf16).T
            return carry

        lax.fori_loop(first, last, step, 0)

    def set_bias(own, first, count):
        clip_col = clips_at(base + lax.broadcasted_iota(jnp.int32, (rows, count), 0))
        tag_row = tags[0 if own else 1, 0:1, first : first + count]
        allowed = jnp.broadcast_to(tag_row, (rows, count)) == clip_col
        if own:
            here = lax.broadcasted_iota(jnp.int32, (rows, count), 0)
            there = lax.broadcasted_iota(jnp.int32, (rows, count), 1)
            allowed = allowed | (here == there)
        bias[:, :count] = jnp.where(allowed, 0.0, masked_score)

    loads[0].wait()
    first_norm(tok, 0, 0, row_tiles)
    set_bias(True, 0, rows)
    loads[1].wait()
    wide = 256

    def project(kind, add, scale, dst, dst_at, first=0, count=rows):
        here = pl.ds(first, count)

        def step(c, carry):
            col = pl.multiple_of(c * wide, wide)
            out = dot(nrm[here, :], wqkv[:, pl.ds(kind * D + col, wide)])
            if add is not None:
                out = out + add[pl.ds(col, wide)].reshape(1, wide)
            out = out.astype(bf16)
            if scale:
                out = out * jnp.bfloat16(score_scale)
            dst[here, pl.ds(dst_at + col, wide)] = out
            return carry

        lax.fori_loop(0, D // wide, step, 0)

    project(0, q_bias, True, qkv, 0)
    project(1, None, False, qkv, D)
    project(2, v_bias, False, qkv, 2 * D)

    low_lane = lax.broadcasted_iota(jnp.int32, (rows, 128), 1) < 64

    def half(values, h):
        mask = low_lane[: values.shape[0]]
        return jnp.where(mask if h == 0 else ~mask, values, jnp.zeros_like(values))

    def half_and_ones(values, h):
        return jnp.concatenate([half(values, h), half(jnp.ones_like(values), h)], axis=1)

    def e_out(hp):
        return pltpu.make_async_copy(ering.at[hp], e_hbm.at[hp], e_sem.at[hp])

    def e_in(hp):
        return pltpu.make_async_copy(e_hbm.at[hp], ering.at[hp], e_sem.at[hp])

    MIXED, F_OWN, F_A, F_B, RES, ACC, GNT = range(7)

    S_OWN, S_A, O_A = F_B, ACC, RES

    def forward_pair(part, hp):
        own = part == 0
        count = rows if own else part_rows
        first = 0 if own else (part - 1) * part_rows
        keys = pl.ds(first, count)
        ref, key_at, value_at = (qkv, D, 2 * D) if own else (kvp, 0, D)
        cols = pl.ds(hp * 128, 128)
        q = qkv[:, cols]
        k = ref[keys, pl.ds(key_at + hp * 128, 128)]
        v = ref[keys, pl.ds(value_at + hp * 128, 128)]
        outs, tops = [], []
        for h in range(2):
            scores = dot_nt(q, half(k, h)) + bias[:, :count]
            top = jnp.max(scores, axis=1, keepdims=True)
            e = jnp.exp(scores - top).astype(bf16)
            ering[hp, h, :, first : first + count] = e
            outs.append(dot(e, half_and_ones(v, h)))
            tops.append(top)
        both_heads = outs[0] + outs[1]
        weighted, sums = both_heads[:, :128], both_heads[:, 128:]
        top = jnp.where(low_lane, tops[0], tops[1])
        if part == 0:
            slots[MIXED, :, cols] = weighted
            slots[S_OWN, :, cols] = sums
            slots[F_OWN, :, cols] = top
            return
        if part == 1:
            slots[O_A, :, cols] = weighted
            slots[S_A, :, cols] = sums
            slots[F_A, :, cols] = top
            return
        top_own, top_a = slots[F_OWN, :, cols], slots[F_A, :, cols]
        highest = jnp.maximum(jnp.maximum(top_own, top_a), top)
        w_own = jnp.exp(top_own - highest)
        w_a = jnp.exp(top_a - highest)
        w_b = jnp.exp(top - highest)
        inverse = 1.0 / (w_own * slots[S_OWN, :, cols] + w_a * slots[S_A, :, cols] + w_b * sums)
        w_own, w_a, w_b = w_own * inverse, w_a * inverse, w_b * inverse
        slots[MIXED, :, cols] = (
            w_own * slots[MIXED, :, cols] + w_a * slots[O_A, :, cols] + w_b * weighted
        )
        slots[F_OWN, :, cols] = w_own
        slots[F_A, :, cols] = w_a
        slots[F_B, :, cols] = w_b

    for hp in range(PAIRS):
        forward_pair(0, hp)
        if hp % 3 == 2:
            for done in range(hp - 2, hp + 1):
                e_out(done).start()

    send_tags.wait()
    for part in (1, 2):
        first = (part - 1) * part_rows
        send_tok[part - 1].wait()
        first_norm(tokp, rows, first // ROW_TILE, (first + part_rows) // ROW_TILE)
        set_bias(False, first, part_rows)
        project(1, None, False, kvp, 0, first, part_rows)
        project(2, v_bias, False, kvp, D, first, part_rows)
        if part == 1:
            for hp in range(PAIRS):
                e_out(hp).wait()
        for hp in range(PAIRS):
            forward_pair(part, hp)

    loads[2].wait()

    def branch(c, carry):
        cols = pl.ds(pl.multiple_of(c * wide, wide), wide)
        out = dot(slots[MIXED].astype(bf16), wout[:, cols])
        out = out + out_bias[cols].reshape(1, wide)
        slots[RES, :, cols] = tok[:, cols].astype(f32) + out
        return carry

    lax.fori_loop(0, D // wide, branch, 0)
    gain_two, offset_two = row(ln2_gain), row(ln2_bias)

    def second_norm(t, carry):
        unit, _ = unit_of(slots[RES, tile(t), :])
        normed = (unit * gain_two + offset_two).astype(bf16)
        nrm[tile(t), :] = normed
        nrm2_t[:, tile(t)] = normed.T
        slots[ACC, tile(t), :] = jnp.zeros((ROW_TILE, D), f32)
        slots[GNT, tile(t), :] = jnp.zeros((ROW_TILE, D), f32)
        return carry

    lax.fori_loop(0, row_tiles, second_norm, 0)

    loads[3].wait()
    loads[4].wait()
    loads[5].wait()

    def feed(c, carry):
        units = pl.ds(pl.multiple_of(c * FF_CHUNK, FF_CHUNK), FF_CHUNK)
        w1 = wfc1[:, units]
        w2 = wfc2[units, :]
        pre = dot(nrm[...], w1) + fc1_bias[units].reshape(1, FF_CHUNK)
        phi = 0.5 * (1.0 + lax.erf(pre * 0.7071067811865476))
        slope = phi + pre * jnp.exp(-0.5 * pre * pre) * 0.3989422804014327
        activated = (pre * phi).astype(bf16)
        grad_pre = (dot_nt(cot[...], w2) * slope).astype(bf16)
        slots[ACC] += dot(activated, w2)
        slots[GNT] += dot_nt(grad_pre, w1)
        @pl.when(c < 4)
        def _():
            wqkv[:rows, units] = activated

        @pl.when(c >= 4)
        def _():
            for part in range(2):
                at = pl.multiple_of((2 * (c - 4) + part) * FF_CHUNK, FF_CHUNK)
                here = slice(part * part_rows, (part + 1) * part_rows)
                wqkv[rows:, pl.ds(at, FF_CHUNK)] = activated[here]

        fb1_ref[0:1, units] = column_sum(grad_pre.astype(f32))
        put_24(c, dot(nrm2_t[...], grad_pre))
        feed_tick(c)
        return carry

    lax.fori_loop(0, FF // FF_CHUNK, feed, 0)

    def weight_fc2(c):
        pieces = []
        for piece in range(3 * c, 3 * c + 3):
            if piece < 8:
                pieces.append(dot_tn(wqkv[:rows, 256 * piece : 256 * piece + 256], cot[...]))
                continue
            at = (piece - 8) // 2 * 2 * FF_CHUNK + (piece - 8) % 2 * 256
            low = wqkv[rows:, at : at + 256]
            high = wqkv[rows:, at + FF_CHUNK : at + FF_CHUNK + 256]
            pieces.append(dot_tn(jnp.concatenate([low, high], axis=0), cot[...]))
        values = jnp.concatenate(pieces, axis=0)
        for d in range(8 * c, 8 * c + 8):
            for order, lane, width in GROUPS:
                place = 16 * place_of(order, bits_of(d))
                for j in range(6):
                    top = 96 * (d - 8 * c) + 16 * j
                    block = values[top : top + 16, lane : lane + width].astype(bf16)
                    at = pl.multiple_of((6 + j) * ITEM_ROWS + place, 16)
                    terms[pl.ds(at, 16), lane : lane + width] = block

    for c in range(4):
        weight_fc2(c)
        if c == 1:
            tick(6)
    reload = pltpu.make_async_copy(wqkv_hbm, wqkv, load_sem.at[1])
    reload.start()
    tick(7)

    vec_ref[...] = jnp.zeros(vec_ref.shape, f32)
    fb1_ref[1:8, :] = jnp.zeros((7, FF), f32)
    V_OB, V_LN2G, V_LN2B, V_FC2B = range(4)
    cs_ref[0] = jnp.zeros(cs_ref.shape[1:], f32)

    def add_vec(kind, values):
        vec_ref[kind : kind + 1, :] += column_sum(values)

    def second_back(t, carry):
        here = tile(t)
        unit, inverse = unit_of(slots[RES, here, :])
        tokp[here, :] = (
            slots[RES, here, :] + slots[ACC, here, :] + row(fc2_bias)
        ).astype(bf16)
        upstream = slots[GNT, here, :]
        grad_out = cot[here, :].astype(f32)
        add_vec(V_FC2B, grad_out)
        add_vec(V_LN2G, upstream * unit)
        add_vec(V_LN2B, upstream)
        scaled = upstream * gain_two
        grad = grad_out + inverse * (
            scaled
            - jnp.mean(scaled, axis=1, keepdims=True)
            - unit * jnp.mean(scaled * unit, axis=1, keepdims=True)
        )
        slots[RES, here, :] = grad
        low = grad.astype(bf16)
        nrm[here, :] = low
        add_vec(V_OB, low.astype(f32))
        return carry

    lax.fori_loop(0, 2, second_back, 0)
    tick(8)
    lax.fori_loop(2, row_tiles, second_back, 0)
    store_result = pltpu.make_async_copy(tokp, result_hbm.at[0], load_sem.at[0])
    store_result.start()
    tick(9)

    GQ = ACC

    def mixed_back(c, carry):
        cols = pl.ds(pl.multiple_of(c * wide, wide), wide)
        gm[:, cols] = dot_nt(nrm[...], wout[cols, :]).astype(bf16)
        mixed = slots[MIXED, :, cols].astype(bf16)
        wfc1[cols, :D] = dot_tn(mixed, nrm[...]).astype(bf16)
        return carry

    lax.fori_loop(0, D // wide, mixed_back, 0)
    def window(ref, first, count):
        block = first // 128 * 128
        shift = first - block
        wide_enough = 256 if shift + count > 128 else 128
        piece = ref[:, block : block + wide_enough]
        if shift:
            piece = pltpu.roll(piece, wide_enough - shift, 1)
        return piece[:, :128]

    small_order = GROUPS[0][0]
    for d in range(32):
        at = pl.multiple_of(16 * place_of(small_order, bits_of(d)), 16)
        small[pl.ds(at, 8), :] = window(vec_ref, 24 * d, 24)
        small[pl.ds(at + 8, 8), :] = window(fb1_ref, 96 * d, 96)

    def small_copy(stage):
        count = ITEM_ROWS >> stage
        return pltpu.make_async_remote_copy(
            src_ref=small.at[pl.ds(count, count)],
            dst_ref=small_in.at[pl.ds(LANDING[stage - 1], count)],
            send_sem=small_send.at[stage - 1],
            recv_sem=small_recv.at[stage - 1],
            device_id=across[small_order[stage - 1]],
            device_id_type=MESH,
        )

    def small_step(stage):
        small_copy(stage).wait()
        count = ITEM_ROWS >> stage
        came = small_in[LANDING[stage - 1] : LANDING[stage - 1] + count]
        small[:count] = small[:count] + came
        if stage < STAGES:
            small_copy(stage + 1).start()
            return
        for kind, ref in enumerate((out_ob, out_ln2g, out_ln2b, out_fb2)):
            ref[...] = small[kind, :24]
        out_fb1[...] = small[8, :96]

    small_copy(1).start()

    def sums_copy(stage):
        return pltpu.make_async_remote_copy(
            src_ref=cs_ref.at[stage - 1],
            dst_ref=cs_in.at[stage - 1],
            send_sem=sums_send.at[stage - 1],
            recv_sem=sums_recv.at[stage - 1],
            device_id=across[small_order[stage - 1]],
            device_id_type=MESH,
        )

    def sums_step(stage):
        sums_copy(stage).wait()
        cs_ref[stage] = cs_ref[stage - 1] + cs_in[stage - 1]
        if stage < STAGES:
            sums_copy(stage + 1).start()

    tick(10)

    def backward_pair(part, hp):
        own = part == 0
        ref, key_at, value_at = (qkv, D, 2 * D) if own else (kvp, 0, D)
        kind = (F_OWN, F_A, F_B)[part]
        count = rows if own else part_rows
        first = 0 if own else (part - 1) * part_rows
        keys = pl.ds(first, count)
        cols = pl.ds(hp * 128, 128)
        q = qkv[:, cols]
        q_t = q.T
        k = ref[keys, pl.ds(key_at + hp * 128, 128)]
        v = ref[keys, pl.ds(value_at + hp * 128, 128)]
        grad_in = gm[:, cols].astype(f32)
        scaled = grad_in * slots[kind, :, cols]
        weighted = scaled * slots[MIXED, :, cols]
        scaled = scaled.astype(bf16)
        scaled_t = scaled.T
        grad_q = None
        grad_k, grad_v = [], []
        for h in range(2):
            delta = jnp.sum(half(weighted, h), axis=1, keepdims=True)
            e = ering[hp, h, :, first : first + count]
            grad_probs = dot_nt(scaled, half(v, h))
            grad_scores = (e.astype(f32) * (grad_probs - delta)).astype(bf16)
            term = dot(grad_scores, half(k, h))
            grad_q = term if grad_q is None else grad_q + term
            grad_k.append(dot(q_t[64 * h : 64 * h + 64], grad_scores))
            grad_v.append(dot(scaled_t[64 * h : 64 * h + 64], e))
        grad_k = jnp.concatenate(grad_k, axis=0).T.astype(bf16)
        grad_v = jnp.concatenate(grad_v, axis=0).T.astype(bf16)
        ref[keys, pl.ds(key_at + hp * 128, 128)] = grad_k
        ref[keys, pl.ds(value_at + hp * 128, 128)] = grad_v
        if part == 1:
            slots[GQ, :, cols] = grad_q
        elif part == 2:
            slots[GQ, :, cols] += grad_q
        else:
            total_q = (slots[GQ, :, cols] + grad_q) * score_scale
            qkv[:, cols] = total_q.astype(bf16)

    store_result.wait()
    reload.wait()
    send_gn = []
    for part in (1, 2):
        first = (part - 1) * part_rows
        here = pl.ds(first, part_rows)
        for hp in range(PAIRS):
            backward_pair(part, hp)
            if hp == 2:
                tick(2 * part + 9)
        if part == 2:
            for hp in range(PAIRS):
                e_in(hp).start()

        def partial_out(c, carry):
            cols = pl.ds(pl.multiple_of(c * wide, wide), wide)
            tokp[here, cols] = dot_nt(kvp[here, :], wqkv[cols, D : 3 * D]).astype(bf16)
            return carry

        lax.fori_loop(0, D // wide, partial_out, 0)
        send_gn.append(to_twin(1 + part, tokp.at[here], gn_in.at[here]))
        send_gn[-1].start()
        tick(2 * part + 10)
        small_step(part)

    for hp in range(PAIRS):
        if hp % 2 == 0:
            e_in(hp).wait()
            e_in(hp + 1).wait()
        backward_pair(0, hp)
        col = hp * 128
        grad_q = qkv[:, pl.ds(col, 128)]
        own = jnp.concatenate(
            [qkv[:, pl.ds(D + col, 128)], qkv[:, pl.ds(2 * D + col, 128)]], axis=1
        )
        other = jnp.concatenate(
            [kvp[:, pl.ds(col, 128)], kvp[:, pl.ds(D + col, 128)]], axis=1
        )
        sum_kv = column_sum(own.astype(f32) + other.astype(f32))
        cs_ref[0, 0:1, pl.ds(col, 128)] = column_sum(grad_q.astype(f32))
        cs_ref[0, 1:2, pl.ds(col, 128)] = sum_kv[:, :128]
        cs_ref[0, 2:3, pl.ds(col, 128)] = sum_kv[:, 128:]
        weight_kv = dot(unit_t[...], jnp.concatenate([own, other], axis=0))
        weight_q = dot(unit_t[:, :rows], grad_q)
        weight_o = wfc1[:, pl.ds(col, 128)].astype(f32)
        put_24(12 + hp, jnp.concatenate([weight_kv, weight_q, weight_o], axis=1))
        tick(15 + hp)
        if hp % 2 == 1:
            small_step(3 + hp // 2)

    def first_back_product(c, carry):
        cols = pl.ds(pl.multiple_of(c * wide, wide), wide)
        slots[GNT, :, cols] = dot_nt(qkv[...], wqkv[cols, :])
        return carry

    sums_copy(1).start()
    lax.fori_loop(0, D // wide, first_back_product, 0)
    tick(21)
    sums_step(1)
    tick(22)
    sums_step(2)
    gain_one = row(ln1_gain)

    def first_back(t, carry):
        here = tile(t)
        unit, inverse = unit_of(tok[here, :].astype(f32))
        upstream = slots[GNT, here, :] + gn_in[here, :].astype(f32)
        scaled = upstream * gain_one
        grad = slots[RES, here, :] + inverse * (
            scaled
            - jnp.mean(scaled, axis=1, keepdims=True)
            - unit * jnp.mean(scaled * unit, axis=1, keepdims=True)
        )
        gm[here, :] = grad.astype(bf16)
        return carry

    for copy in send_gn:
        copy.wait()
    lax.fori_loop(0, row_tiles, first_back, 0)
    store_gtok = pltpu.make_async_copy(gm, gtok_hbm.at[0], load_sem.at[2])
    store_gtok.start()
    tick(23)
    sums_step(3)
    tick(24)
    tick(25)
    sums_step(4)
    tick(26)
    tick(27)
    sums_step(5)
    tick(28)
    tick(29)

    me = seq * 2 + blk
    low_row = me * 24 // 16 * 16
    weights = wqkv[pl.ds(pl.multiple_of(low_row, 16), 32), :].astype(f32)
    weights = jnp.where(me * 24 == low_row, weights[:24], weights[8:])
    sums = cs_ref[STAGES]
    lanes = lax.broadcasted_iota(jnp.int32, (24, D), 1)
    mine = lanes == me * 24 + lax.broadcasted_iota(jnp.int32, (24, D), 0)

    def my_column(values):
        return jnp.sum(jnp.where(mine, values, 0.0), axis=1, keepdims=True)

    gain_mine, bias_mine = my_column(row(ln1_gain)), my_column(row(ln1_bias))
    gain_sum = jnp.zeros((24, 1), f32)
    bias_sum = jnp.zeros((24, 1), f32)
    for kind in range(3):
        cols = slice(kind * D, (kind + 1) * D)
        product = out_qkv[:, cols]
        total = sums[kind : kind + 1, :]
        gain_sum += jnp.sum(weights[:, cols] * product, axis=1, keepdims=True)
        bias_sum += jnp.sum(weights[:, cols] * total, axis=1, keepdims=True)
        out_qkv[:, cols] = gain_mine * product + bias_mine * total
    diagonal = lax.broadcasted_iota(jnp.int32, (24, 128), 0) == lax.broadcasted_iota(
        jnp.int32, (24, 128), 1
    )
    for ref, values in (
        (out_ln1g, gain_sum),
        (out_ln1b, bias_sum),
        (out_qb, my_column(sums[0:1])),
        (out_vb, my_column(sums[2:3])),
    ):
        ref[...] = column_sum(jnp.where(diagonal, values, 0.0))[0, :24]
    store_gtok.wait()


def hand_on(*refs):
    for i in range(15):
        refs[15 + i][...] = refs[i][...]


def block_body(
    tokens,
    lengths,
    padding,
    cotangent,
    ln1_gain,
    ln1_bias,
    w_qkv,
    q_bias,
    v_bias,
    w_out,
    out_bias,
    ln2_gain,
    ln2_bias,
    w_fc1,
    fc1_bias,
    w_fc2,
    fc2_bias,
):
    rows = tokens.shape[1]
    n_dev = lax.axis_size("seq") * lax.axis_size("blk")
    shape = jax.ShapeDtypeStruct
    any_spec = pl.BlockSpec(memory_space=pl.ANY)
    vmem = pl.BlockSpec(memory_space=pltpu.VMEM)
    smem = pl.BlockSpec(memory_space=pltpu.SMEM)
    part = D // n_dev
    line = shape((part,), f32)
    outs = pl.pallas_call(
        block_kernel,
        name="block",
        out_shape=(
            shape((1, rows, D), bf16),
            shape((1, rows, D), bf16),
            line,
            line,
            shape((part, 3 * D), f32),
            line,
            line,
            shape((part, D), f32),
            line,
            line,
            line,
            shape((part, FF), f32),
            shape((FF // n_dev,), f32),
            shape((FF // n_dev, D), f32),
            line,
            shape((PAIRS, 2, rows, rows), bf16),
        ),
        in_specs=[
            any_spec, smem, vmem, any_spec, vmem, vmem, any_spec, vmem, vmem,
            any_spec, vmem, vmem, vmem, any_spec, vmem, any_spec, vmem,
        ],
        out_specs=(any_spec,) * 2 + (vmem,) * 13 + (any_spec,),
        scratch_shapes=[
            pltpu.VMEM((D, 3 * D), bf16),
            pltpu.VMEM((D, D), bf16),
            pltpu.VMEM((D, FF), bf16),
            pltpu.VMEM((FF, D), bf16),
            pltpu.VMEM((rows, D), bf16),
            pltpu.VMEM((rows, D), bf16),
            pltpu.VMEM((rows, D), bf16),
            pltpu.VMEM((rows, D), bf16),
            pltpu.VMEM((D, 2 * rows), bf16),
            pltpu.VMEM((D, rows), bf16),
            pltpu.VMEM((rows, 3 * D), bf16),
            pltpu.VMEM((rows, 2 * D), bf16),
            pltpu.VMEM((rows, D), bf16),
            pltpu.VMEM((rows, rows), f32),
            pltpu.VMEM((PAIRS, 2, rows, rows), bf16),
            pltpu.VMEM((7, rows, D), f32),
            pltpu.VMEM((12 * ITEM_ROWS, ITEM_LANES), bf16),
            pltpu.VMEM((SLOTS * LANDING_ROWS, ITEM_LANES), bf16),
            pltpu.VMEM((rows, D), bf16),
            pltpu.VMEM((2, 8, rows), jnp.int32),
            pltpu.VMEM((8, D), f32),
            pltpu.VMEM((8, FF), f32),
            pltpu.VMEM((ITEM_ROWS, 128), f32),
            pltpu.VMEM((LANDING_ROWS, 128), f32),
            pltpu.VMEM((STAGES + 1, 8, D), f32),
            pltpu.VMEM((STAGES, 8, D), f32),
            pltpu.SemaphoreType.DMA((6,)),
            pltpu.SemaphoreType.DMA((PAIRS,)),
            pltpu.SemaphoreType.DMA((5,)),
            pltpu.SemaphoreType.DMA((5,)),
            pltpu.SemaphoreType.DMA((SLOTS * STAGES * len(GROUPS),)),
            pltpu.SemaphoreType.DMA((SLOTS * STAGES * len(GROUPS),)),
            pltpu.SemaphoreType.DMA((STAGES,)),
            pltpu.SemaphoreType.DMA((STAGES,)),
            pltpu.SemaphoreType.DMA((STAGES,)),
            pltpu.SemaphoreType.DMA((STAGES,)),
        ],
        compiler_params=pltpu.CompilerParams(
            collective_id=0, has_side_effects=True, vmem_limit_bytes=VMEM_LIMIT
        ),
        cost_estimate=pl.CostEstimate(
            flops=30 * 10**9, bytes_accessed=60 * 10**6, transcendentals=10**7
        ),
    )(
        tokens, lengths, padding, cotangent, ln1_gain, ln1_bias, w_qkv, q_bias, v_bias,
        w_out, out_bias, ln2_gain, ln2_bias, w_fc1, fc1_bias, w_fc2, fc2_bias,
    )
    return pl.pallas_call(
        hand_on,
        name="hand_on",
        out_shape=tuple(shape(o.shape, o.dtype) for o in outs[:15]),
        in_specs=[vmem] * 15,
        out_specs=(vmem,) * 15,
    )(*outs[:15])


VMEM_LIMIT = 63 * 2**20


def solution(mesh):
    in_specs = (
        P("seq", "blk", None),
        P("seq", None),
        P("seq", "blk"),
        P("seq", "blk", None),
        P(),
        P(),
        P(),
        P(),
        P(),
        P(),
        P(),
        P(),
        P(),
        P(),
        P(),
        P(),
        P(),
    )
    out_specs = (
        P("seq", "blk", None),
        P("seq", "blk", None),
        P(("seq", "blk")),
        P(("seq", "blk")),
        P(("seq", "blk"), None),
        P(("seq", "blk")),
        P(("seq", "blk")),
        P(("seq", "blk"), None),
        P(("seq", "blk")),
        P(("seq", "blk")),
        P(("seq", "blk")),
        P(("seq", "blk"), None),
        P(("seq", "blk")),
        P(("seq", "blk"), None),
        P(("seq", "blk")),
    )
    step = block_body if fits(mesh) else body
    return jax.shard_map(step, mesh=mesh, in_specs=in_specs, out_specs=out_specs, check_vma=False)
```

```python
import functools

import jax
import jax.numpy as jnp
from jax import lax
from jax.experimental import pallas as pl
from jax.experimental.pallas import tpu as pltpu
from jax.sharding import PartitionSpec as P

D = 768
FF = 3072
HEADS = 12
HEAD_DIM = 64


epsilon = 1e-06
score_scale = 0.125
masked_score = -1e30


def clip_numbers(clip_lengths, positions):
    bounds = jnp.cumsum(clip_lengths)
    return jnp.sum((positions[:, None] >= bounds[None, :]).astype(jnp.int32), axis=1)


def normalize(values, scales, offset):
    center = values - jnp.mean(values, axis=-1, keepdims=True)
    spread = jnp.mean(center * center, axis=-1, keepdims=True)
    inverse = lax.rsqrt(spread + epsilon)
    unit = center * inverse
    return (unit * scales + offset, unit, inverse)


def norm_back(upstream, unit, inverse, scales):
    scaled = upstream * scales
    return inverse * (
        scaled
        - jnp.mean(scaled, axis=-1, keepdims=True)
        - unit * jnp.mean(scaled * unit, axis=-1, keepdims=True)
    )


def gelu_slope(pre_gelu):
    cdf_part = 0.5 * (1.0 + lax.erf(pre_gelu * 0.7071067811865476))
    return cdf_part + pre_gelu * jnp.exp(-0.5 * pre_gelu * pre_gelu) * 0.3989422804014327


def masked_scores(query_heads, key_heads, clip_ids, positions, block_tags, key_pos):
    raw_scores = (
        jnp.einsum("qhd,khd->qhk", query_heads, key_heads, preferred_element_type=jnp.float32)
        * score_scale
    )
    allowed = (block_tags[None, :] == clip_ids[:, None]) | (positions[:, None] == key_pos[None, :])
    return jnp.where(allowed[:, None, :], raw_scores, masked_score)


def score_grads(
    query_heads,
    key_heads,
    value_heads,
    grad_heads,
    log_total,
    row_delta,
    clip_ids,
    positions,
    block_tags,
    key_pos,
):
    scores = masked_scores(query_heads, key_heads, clip_ids, positions, block_tags, key_pos)
    attn_probs = jnp.exp(scores - log_total[..., None])
    grad_probs = jnp.einsum(
        "qhd,khd->qhk", grad_heads, value_heads, preferred_element_type=jnp.float32
    )
    grad_scores = (attn_probs * (grad_probs - row_delta[..., None])).astype(jnp.bfloat16)
    return (attn_probs, grad_scores)


def stage_orders():
    seq_bits = lax.axis_size("seq").bit_length() - 1
    blk_bits = lax.axis_size("blk").bit_length() - 1
    seq_stages = [blk_bits + b for b in range(seq_bits)]
    blk_stages = list(range(blk_bits))
    one = seq_stages[:2] + blk_stages + seq_stages[2:]
    two = seq_stages[:1] + blk_stages + seq_stages[1:]
    return one, two


def scatter_stages(terms, order):
    n_dev = terms.shape[0]
    bits = n_dev.bit_length() - 1
    me = lax.axis_index("seq") * lax.axis_size("blk") + lax.axis_index("blk")
    rest = terms.shape[1:]
    kind = terms.dtype
    held = terms.reshape((2,) * bits + rest)
    for number, bit in enumerate(order):
        axis = bits - 1 - bit
        mine = (me >> bit) & 1
        sent = lax.dynamic_slice_in_dim(held, 1 - mine, 1, axis)
        kept = lax.dynamic_slice_in_dim(held, mine, 1, axis)
        swap = [(i, i ^ (1 << bit)) for i in range(n_dev)]
        came = lax.ppermute(sent, ("seq", "blk"), swap)
        total = kept.astype(jnp.float32) + came.astype(jnp.float32)
        held = total if number == bits - 1 else total.astype(kind)
    return held.reshape((1,) + rest)


def scatter_sum(grad):
    n_dev = lax.axis_size("seq") * lax.axis_size("blk")
    rows, width = grad.shape
    terms = grad.astype(jnp.bfloat16).reshape(n_dev, rows // n_dev, width)
    one, two = stage_orders()
    left = scatter_stages(terms[:, :, : width // 2], one)[0]
    right = scatter_stages(terms[:, :, width // 2 :], two)[0]
    return jnp.concatenate([left, right], axis=1)


def body(
    tokens,
    lengths,
    padding,
    cotangent,
    ln1_gain,
    ln1_bias,
    w_qkv,
    q_bias,
    v_bias,
    w_out,
    out_bias,
    ln2_gain,
    ln2_bias,
    w_fc1,
    fc1_bias,
    w_fc2,
    fc2_bias,
):
    tok_rows = tokens.shape[1]
    group_size = lax.axis_size("blk")
    n_dev = lax.axis_size("seq") * group_size
    positions = lax.axis_index("blk") * tok_rows + jnp.arange(tok_rows, dtype=jnp.int32)
    clip_ids = clip_numbers(lengths[0], positions)
    key_tags = jnp.where(padding[0] == 1, -1, clip_ids)
    tokens_f32 = tokens[0].astype(jnp.float32)
    first_norm, unit_one, inverse_one = normalize(tokens_f32, ln1_gain, ln1_bias)
    normed_one = first_norm.astype(jnp.bfloat16)
    joint_bias = jnp.concatenate([q_bias, jnp.zeros_like(q_bias), v_bias])
    projected = (
        jnp.dot(normed_one, w_qkv, preferred_element_type=jnp.float32) + joint_bias
    ).astype(jnp.bfloat16)
    keys_own = projected[:, D : 2 * D]
    values_own = projected[:, 2 * D :]
    query_heads = projected[:, :D].reshape(tok_rows, HEADS, HEAD_DIM)
    starts = jnp.arange(group_size, dtype=jnp.int32) * tok_rows

    def fold_keys(running, key_block, offset):
        block_keys, block_values, block_tags = key_block
        key_count = block_keys.shape[0]
        key_pos = offset + jnp.arange(key_count, dtype=jnp.int32)
        scores = masked_scores(
            query_heads,
            block_keys.reshape(key_count, HEADS, HEAD_DIM),
            clip_ids,
            positions,
            block_tags,
            key_pos,
        )
        row_max, row_sum, weighted = running
        new_max = jnp.maximum(row_max, jnp.max(scores, axis=-1))
        rescale = jnp.exp(row_max - new_max)
        exp_scores = jnp.exp(scores - new_max[..., None])
        row_sum = row_sum * rescale + jnp.sum(exp_scores, axis=-1)
        weighted = weighted * rescale[..., None] + jnp.einsum(
            "qhk,khd->qhd",
            exp_scores.astype(jnp.bfloat16),
            block_values.reshape(key_count, HEADS, HEAD_DIM),
            preferred_element_type=jnp.float32,
        )
        return (new_max, row_sum, weighted)

    start_state = (
        jnp.full((tok_rows, HEADS), masked_score, jnp.float32),
        jnp.zeros((tok_rows, HEADS), jnp.float32),
        jnp.zeros((tok_rows, HEADS, HEAD_DIM), jnp.float32),
    )
    group_keys, group_values, group_tags = (
        lax.all_gather(keys_own, "blk", axis=0, tiled=True),
        lax.all_gather(values_own, "blk", axis=0, tiled=True),
        lax.all_gather(key_tags, "blk", axis=0, tiled=True),
    )

    def scan_fold(running, scan_args):
        return (fold_keys(running, (scan_args[0], scan_args[1], scan_args[2]), scan_args[3]), None)

    final_state = lax.scan(
        scan_fold,
        start_state,
        (
            group_keys.reshape(group_size, tok_rows, D),
            group_values.reshape(group_size, tok_rows, D),
            group_tags.reshape(group_size, tok_rows),
            starts,
        ),
    )[0]
    row_max, row_sum, weighted = final_state
    mixed_f32 = weighted / row_sum[..., None]
    log_total = row_max + jnp.log(row_sum)
    mixed = mixed_f32.reshape(tok_rows, D).astype(jnp.bfloat16)
    residual = tokens_f32 + jnp.dot(mixed, w_out, preferred_element_type=jnp.float32) + out_bias
    second_norm, unit_two, inverse_two = normalize(residual, ln2_gain, ln2_bias)
    normed_two = second_norm.astype(jnp.bfloat16)
    pre_gelu = jnp.dot(normed_two, w_fc1, preferred_element_type=jnp.float32) + fc1_bias
    activated = jax.nn.gelu(pre_gelu, approximate=False).astype(jnp.bfloat16)
    result = (
        residual + jnp.dot(activated, w_fc2, preferred_element_type=jnp.float32) + fc2_bias
    ).astype(jnp.bfloat16)
    grad_out = cotangent[0]
    grad_fc2_bias = jnp.sum(grad_out, axis=0, dtype=jnp.float32)
    grad_w_fc2 = jnp.einsum("tf,td->fd", activated, grad_out, preferred_element_type=jnp.float32)
    grad_act = jnp.einsum("td,fd->tf", grad_out, w_fc2, preferred_element_type=jnp.float32)
    grad_pre = (grad_act * gelu_slope(pre_gelu)).astype(jnp.bfloat16)
    grad_fc1_bias = jnp.sum(grad_pre, axis=0, dtype=jnp.float32)
    grad_w_fc1 = jnp.einsum("td,tf->df", normed_two, grad_pre, preferred_element_type=jnp.float32)
    grad_norm_two = jnp.einsum("tf,df->td", grad_pre, w_fc1, preferred_element_type=jnp.float32)
    grad_ln2_gain = jnp.sum(grad_norm_two * unit_two, axis=0)
    grad_ln2_bias = jnp.sum(grad_norm_two, axis=0)
    grad_residual = grad_out.astype(jnp.float32) + norm_back(
        grad_norm_two, unit_two, inverse_two, ln2_gain
    )
    grad_branch = grad_residual.astype(jnp.bfloat16)
    grad_out_bias = jnp.sum(grad_branch, axis=0, dtype=jnp.float32)
    grad_w_out = jnp.einsum("td,te->de", mixed, grad_branch, preferred_element_type=jnp.float32)
    grad_mixed = jnp.einsum(
        "te,de->td", grad_branch, w_out, preferred_element_type=jnp.float32
    ).astype(jnp.bfloat16)
    grad_heads = grad_mixed.reshape(tok_rows, HEADS, HEAD_DIM)
    row_delta = jnp.sum(grad_heads * mixed_f32, axis=-1)
    key_stack = (
        group_keys.reshape(group_size, tok_rows, D),
        group_values.reshape(group_size, tok_rows, D),
        group_tags.reshape(group_size, tok_rows),
        starts,
    )

    def back_block(grad_queries, scan_args):
        block_keys, block_values, block_tags, offset = scan_args
        key_pos = offset + jnp.arange(tok_rows, dtype=jnp.int32)
        key_heads = block_keys.reshape(tok_rows, HEADS, HEAD_DIM)
        value_heads = block_values.reshape(tok_rows, HEADS, HEAD_DIM)
        attn_probs, grad_scores = score_grads(
            query_heads,
            key_heads,
            value_heads,
            grad_heads,
            log_total,
            row_delta,
            clip_ids,
            positions,
            block_tags,
            key_pos,
        )
        grad_values = jnp.einsum(
            "qhk,qhd->khd",
            attn_probs.astype(jnp.bfloat16),
            grad_heads,
            preferred_element_type=jnp.float32,
        )
        grad_queries = (
            grad_queries
            + jnp.einsum("qhk,khd->qhd", grad_scores, key_heads, preferred_element_type=jnp.float32)
            * score_scale
        )
        grad_keys = (
            jnp.einsum("qhk,qhd->khd", grad_scores, query_heads, preferred_element_type=jnp.float32)
            * score_scale
        )
        return (
            grad_queries,
            jnp.concatenate(
                [grad_keys.reshape(tok_rows, D), grad_values.reshape(tok_rows, D)], axis=1
            ),
        )

    grad_queries, key_terms = lax.scan(
        back_block, jnp.zeros((tok_rows, HEADS, HEAD_DIM), jnp.float32), key_stack
    )
    key_sums = lax.psum_scatter(
        key_terms.reshape(group_size * tok_rows, 2 * D).astype(jnp.bfloat16),
        "blk",
        scatter_dimension=0,
        tiled=True,
    )
    grad_qkv = jnp.concatenate(
        [grad_queries.reshape(tok_rows, D).astype(jnp.bfloat16), key_sums], axis=1
    )
    grad_q_bias = jnp.sum(grad_qkv[:, :D], axis=0, dtype=jnp.float32)
    grad_v_bias = jnp.sum(grad_qkv[:, 2 * D :], axis=0, dtype=jnp.float32)
    grad_w_qkv = jnp.einsum("td,te->de", normed_one, grad_qkv, preferred_element_type=jnp.float32)
    grad_norm_one = jnp.einsum("te,de->td", grad_qkv, w_qkv, preferred_element_type=jnp.float32)
    grad_ln1_gain = jnp.sum(grad_norm_one * unit_one, axis=0)
    grad_ln1_bias = jnp.sum(grad_norm_one, axis=0)
    grad_tokens = (
        grad_residual + norm_back(grad_norm_one, unit_one, inverse_one, ln1_gain)
    ).astype(jnp.bfloat16)
    small = jnp.concatenate(
        [
            v.reshape(n_dev, -1)
            for v in (
                grad_ln1_gain,
                grad_ln1_bias,
                grad_q_bias,
                grad_v_bias,
                grad_out_bias,
                grad_ln2_gain,
                grad_ln2_bias,
                grad_fc1_bias,
                grad_fc2_bias,
            )
        ],
        axis=1,
    )
    sum_fc2 = scatter_sum(grad_w_fc2)
    sum_fc1 = scatter_sum(grad_w_fc1)
    sum_out = scatter_sum(grad_w_out)
    sum_qkv = scatter_sum(grad_w_qkv)
    part = D // n_dev
    small = scatter_stages(small, stage_orders()[0])[0]
    pieces = []
    at = 0
    for size in (part, part, part, part, part, part, part, FF // n_dev, part):
        pieces.append(small[at : at + size])
        at += size
    summed = (
        pieces[0],
        pieces[1],
        sum_qkv,
        pieces[2],
        pieces[3],
        sum_out,
        pieces[4],
        pieces[5],
        pieces[6],
        sum_fc1,
        pieces[7],
        sum_fc2,
        pieces[8],
    )
    return (
        result[None],
        grad_tokens[None],
        summed[0],
        summed[1],
        summed[2],
        summed[3],
        summed[4],
        summed[5],
        summed[6],
        summed[7],
        summed[8],
        summed[9],
        summed[10],
        summed[11],
        summed[12],
    )


f32 = jnp.float32
bf16 = jnp.bfloat16
MESH = pl.DeviceIdType.MESH
PAIRS = HEADS // 2
FF_CHUNK = 512
ROW_TILE = 128
TWIN_UNROLL = 1
ITEMS = 18
ITEM_ROWS = 512
ITEM_LANES = 768
SLOTS = 6
STAGES = 5
STARTS = (0, 1, 2, 3, 4, 5, 7, 8, 9, 10, 11, 12, 15, 16, 17, 18, 19, 20)
ENDS = (0, 1, 4, 7, 10, 13)
SUMS_AT = (1, 3, 6, 9, 12)
LANDING = (0, 256, 384, 448, 480)
LANDING_ROWS = 496
FLAT_BITS = ("y", "c", "x", "z0", "z1")
GROUPS = (
    (("c", "x", "y", "z0", "z1"), 0, 512),
    (("c", "z0", "z1", "y", "x"), 512, 256),
)


def fits(mesh):
    return dict(mesh.shape) == {"seq": 16, "blk": 2}


def dot(a, b):
    return lax.dot_general(a, b, (((1,), (0,)), ((), ())), preferred_element_type=f32)


def dot_nt(a, b):
    return lax.dot_general(a, b, (((1,), (1,)), ((), ())), preferred_element_type=f32)


def dot_tn(a, b):
    return lax.dot_general(a, b, (((0,), (0,)), ((), ())), preferred_element_type=f32)


def aligned(at, step):
    return at if isinstance(at, int) else pl.multiple_of(at, step)


def unit_of(values):
    center = values - jnp.mean(values, axis=1, keepdims=True)
    inverse = lax.rsqrt(jnp.mean(center * center, axis=1, keepdims=True) + epsilon)
    return center * inverse, inverse


def row(ref):
    return ref[...].reshape(1, ref.shape[0])


def column_sum(values):
    return jnp.sum(values, axis=0, keepdims=True)


def block_kernel(
    tok_hbm,
    len_ref,
    pad_ref,
    cot_hbm,
    ln1_gain,
    ln1_bias,
    wqkv_hbm,
    q_bias,
    v_bias,
    wout_hbm,
    out_bias,
    ln2_gain,
    ln2_bias,
    wfc1_hbm,
    fc1_bias,
    wfc2_hbm,
    fc2_bias,
    result_hbm,
    gtok_hbm,
    out_ln1g,
    out_ln1b,
    out_qkv,
    out_qb,
    out_vb,
    out_out,
    out_ob,
    out_ln2g,
    out_ln2b,
    out_fc1,
    out_fb1,
    out_fc2,
    out_fb2,
    e_hbm,
    wqkv,
    wout,
    wfc1,
    tok,
    tokp,
    cot,
    nrm,
    unit_t,
    nrm2_t,
    qkv,
    kvp,
    gm,
    bias,
    ering,
    slots,
    terms,
    landing,
    gn_in,
    tags,
    vec_ref,
    fb1_ref,
    small,
    small_in,
    cs_ref,
    cs_in,
    load_sem,
    e_sem,
    send_sem,
    recv_sem,
    item_send,
    item_recv,
    small_send,
    small_recv,
    sums_send,
    sums_recv,
):
    rows = tok.shape[0]
    seq = lax.axis_index("seq")
    blk = lax.axis_index("blk")
    bit = {
        "y": blk,
        "c": lax.rem(seq, 2),
        "x": lax.rem(seq // 2, 2),
        "z0": lax.rem(seq // 4, 2),
        "z1": seq // 8,
    }
    across = {
        "y": (seq, 1 - blk),
        "c": (seq + 1 - 2 * bit["c"], blk),
        "x": (seq + 2 - 4 * bit["x"], blk),
        "z0": (seq + 4 - 8 * bit["z0"], blk),
        "z1": (seq + 8 - 16 * bit["z1"], blk),
    }
    twin = across["y"]

    barrier = pltpu.get_barrier_semaphore()
    for name in FLAT_BITS:
        pl.semaphore_signal(barrier, inc=1, device_id=across[name], device_id_type=MESH)

    wfc2_at = (ITEMS - 6) * ITEM_ROWS
    wfc2 = terms.at[pl.ds(wfc2_at, FF)]
    loads = [
        pltpu.make_async_copy(src, dst, load_sem.at[i])
        for i, (src, dst) in enumerate(
            (
                (tok_hbm.at[0], tok),
                (wqkv_hbm, wqkv),
                (wout_hbm, wout),
                (wfc1_hbm, wfc1),
                (wfc2_hbm, wfc2),
                (cot_hbm.at[0], cot),
            )
        )
    ]
    for copy in loads:
        copy.start()

    ends = []
    total = jnp.int32(0)
    for i in range(len_ref.shape[1]):
        total = total + len_ref[0, i]
        ends.append(total)

    def clips_at(positions):
        number = jnp.zeros_like(positions)
        for end in ends:
            number = number + jnp.where(positions >= end, 1, 0)
        return number

    base = blk * rows
    lane_pos = base + lax.broadcasted_iota(jnp.int32, (8, rows), 1)
    padding = jnp.broadcast_to(pad_ref[...], (8, rows))
    tags[0] = jnp.where(padding == 1, -1, clips_at(lane_pos))

    pl.semaphore_wait(barrier, len(FLAT_BITS))

    def to_twin(i, src, dst):
        return pltpu.make_async_remote_copy(
            src_ref=src,
            dst_ref=dst,
            send_sem=send_sem.at[i],
            recv_sem=recv_sem.at[i],
            device_id=twin,
            device_id_type=MESH,
        )

    part_rows = rows // 2
    send_tags = to_twin(1, tags.at[0], tags.at[1])
    send_tags.start()
    send_tok = []
    for part, sem in ((0, 0), (1, 8)):
        here = pl.ds(part * part_rows, part_rows)
        send_tok.append(to_twin(sem, tok_hbm.at[0, here], tokp.at[here]))
        send_tok[part].start()

    def place_of(order, there):
        at = 0
        for stage, name in enumerate(order):
            differs = there[name] + bit[name] - 2 * there[name] * bit[name]
            at = at + (16 >> stage) * differs
        return at

    def bits_of(d):
        return {name: (d >> i) & 1 for i, name in enumerate(FLAT_BITS)}

    def item_copies(stage, item):
        count = ITEM_ROWS >> stage
        slot = item % SLOTS if isinstance(item, int) else lax.rem(item, SLOTS)
        first = item * ITEM_ROWS
        src_at = aligned(first + count, 16)
        dst_at = aligned(slot * LANDING_ROWS + LANDING[stage - 1], 16)
        copies = []
        for group, (order, lane, width) in enumerate(GROUPS):
            if stage == 1:
                if group > 0:
                    break
                width = ITEM_LANES
            lanes = pl.ds(lane, width)
            sem = (slot * STAGES + stage - 1) * len(GROUPS) + group
            copies.append(
                pltpu.make_async_remote_copy(
                    src_ref=terms.at[pl.ds(src_at, count), lanes],
                    dst_ref=landing.at[pl.ds(dst_at, count), lanes],
                    send_sem=item_send.at[sem],
                    recv_sem=item_recv.at[sem],
                    device_id=across[order[stage - 1]],
                    device_id_type=MESH,
                )
            )
        return copies

    def start_stage(stage, item):
        for copy in item_copies(stage, item):
            copy.start()

    def store_sum(item, kind, values):
        if kind == 1:
            at = aligned((item - 6) * 16, 16)
            out_fc2[pl.ds(at, 16), :] = values
            return
        parts = (
            (0, 16, values[:, :256], values[:, 256:512]),
            (16, 8, values[:8, 512:], values[8:, 512:]),
        )
        for top, count, left, right in parts:
            here = pl.ds(top, count)
            if kind == 0:
                col = aligned(item * 512, 512)
                out_fc1[here, pl.ds(col, 256)] = left
                out_fc1[here, pl.ds(col + 256, 256)] = right
            else:
                col = aligned((item - 12) * 128, 128)
                out_qkv[here, pl.ds(D + col, 128)] = left[:, :128]
                out_qkv[here, pl.ds(2 * D + col, 128)] = left[:, 128:]
                out_qkv[here, pl.ds(col, 128)] = right[:, :128]
                out_out[here, pl.ds(col, 128)] = right[:, 128:]

    def finish_stage(stage, item, low, high):
        for copy in item_copies(stage, item):
            copy.wait()
        count = ITEM_ROWS >> stage
        slot = item % SLOTS if isinstance(item, int) else lax.rem(item, SLOTS)
        first = item * ITEM_ROWS
        here = pl.ds(aligned(first, 16), count)
        came = pl.ds(aligned(slot * LANDING_ROWS + LANDING[stage - 1], 16), count)
        if stage < STAGES:
            terms[here, :] = terms[here, :] + landing[came, :]
            start_stage(stage + 1, item)
            return
        values = terms[here, :].astype(f32) + landing[came, :].astype(f32)
        for kind in range(3):
            if high < 6 * kind or low >= 6 * kind + 6:
                continue
            if low >= 6 * kind and high < 6 * kind + 6:
                store_sum(item, kind, values)
            else:
                pl.when((item >= 6 * kind) & (item < 6 * kind + 6))(
                    functools.partial(store_sum, item, kind, values)
                )

    def feed_tick(number):
        for stage in range(STAGES, 0, -1):
            if ENDS[stage] < 6:
                item = number - ENDS[stage]
                act = functools.partial(finish_stage, stage, item, 0, 5)
                pl.when(item >= 0)(act)
        start_stage(1, number)

    def tick(number, low=None, high=None):
        low = number if low is None else low
        high = number if high is None else high
        for stage in range(STAGES, -1, -1):
            begun = range(low - ENDS[stage], high - ENDS[stage] + 1)
            items = [STARTS.index(t) for t in begun if t in STARTS]
            if not items:
                continue
            if low == high:
                item = items[0]
            else:
                t = number - ENDS[stage]
                item = t - jnp.where(t >= 7, 1, 0) - jnp.where(t >= 15, 2, 0)
            if stage == 0:
                act = functools.partial(start_stage, 1, item)
            else:
                act = functools.partial(finish_stage, stage, item, items[0], items[-1])
            if len(items) == len(begun):
                act()
            else:
                valid = None
                for t_out in begun:
                    if t_out not in STARTS:
                        here = t != t_out
                        valid = here if valid is None else valid & here
                pl.when(valid)(act)

    def put_24(item, values):
        base_row = item * ITEM_ROWS
        for d in range(32):
            top = values[24 * d : 24 * d + 16, :]
            rest = values[24 * d + 16 : 24 * d + 24, :]
            rest = jnp.concatenate([rest[:, :256], rest[:, 256:]], axis=0)
            block = jnp.concatenate([top, rest], axis=1).astype(bf16)
            for order, lane, width in GROUPS:
                at = pl.multiple_of(base_row + 16 * place_of(order, bits_of(d)), 16)
                terms[pl.ds(at, 16), lane : lane + width] = block[:, lane : lane + width]

    row_tiles = rows // ROW_TILE

    def tile(t):
        return pl.ds(pl.multiple_of(t * ROW_TILE, ROW_TILE), ROW_TILE)

    def first_norm(src, columns_at, first, last):
        gain, offset = row(ln1_gain), row(ln1_bias)

        def step(t, carry):
            unit, _ = unit_of(src[tile(t), :].astype(f32))
            normed = (unit * gain + offset).astype(bf16)
            nrm[tile(t), :] = normed
            at = pl.multiple_of(columns_at + t * ROW_TILE, ROW_TILE)
            unit_t[:, pl.ds(at, ROW_TILE)] = unit.astype(bf16).T
            return carry

        lax.fori_loop(first, last, step, 0)

    def set_bias(own, first, count):
        clip_col = clips_at(base + lax.broadcasted_iota(jnp.int32, (rows, count), 0))
        tag_row = tags[0 if own else 1, 0:1, first : first + count]
        allowed = jnp.broadcast_to(tag_row, (rows, count)) == clip_col
        if own:
            here = lax.broadcasted_iota(jnp.int32, (rows, count), 0)
            there = lax.broadcasted_iota(jnp.int32, (rows, count), 1)
            allowed = allowed | (here == there)
        bias[:, :count] = jnp.where(allowed, 0.0, masked_score)

    loads[0].wait()
    first_norm(tok, 0, 0, row_tiles)
    set_bias(True, 0, rows)
    loads[1].wait()
    wide = 256

    def project(kind, add, scale, dst, dst_at, first=0, count=rows):
        here = pl.ds(first, count)

        def step(c, carry):
            col = pl.multiple_of(c * wide, wide)
            out = dot(nrm[here, :], wqkv[:, pl.ds(kind * D + col, wide)])
            if add is not None:
                out = out + add[pl.ds(col, wide)].reshape(1, wide)
            out = out.astype(bf16)
            if scale:
                out = out * jnp.bfloat16(score_scale)
            dst[here, pl.ds(dst_at + col, wide)] = out
            return carry

        lax.fori_loop(0, D // wide, step, 0)

    project(0, q_bias, True, qkv, 0)
    project(1, None, False, qkv, D)
    project(2, v_bias, False, qkv, 2 * D)

    low_lane = lax.broadcasted_iota(jnp.int32, (rows, 128), 1) < 64

    def half(values, h):
        mask = low_lane[: values.shape[0]]
        return jnp.where(mask if h == 0 else ~mask, values, jnp.zeros_like(values))

    def half_and_ones(values, h):
        return jnp.concatenate([half(values, h), half(jnp.ones_like(values), h)], axis=1)

    def e_out(hp):
        return pltpu.make_async_copy(ering.at[hp], e_hbm.at[hp], e_sem.at[hp])

    def e_in(hp):
        return pltpu.make_async_copy(e_hbm.at[hp], ering.at[hp], e_sem.at[hp])

    MIXED, F_OWN, F_A, F_B, RES, ACC, GNT = range(7)

    S_OWN, S_A, O_A = F_B, ACC, RES

    def forward_pair(part, hp):
        own = part == 0
        count = rows if own else part_rows
        first = 0 if own else (part - 1) * part_rows
        keys = pl.ds(first, count)
        ref, key_at, value_at = (qkv, D, 2 * D) if own else (kvp, 0, D)
        col = aligned(hp * 128, 128)
        cols = pl.ds(col, 128)
        q = qkv[:, cols]
        k = ref[keys, pl.ds(key_at + col, 128)]
        v = ref[keys, pl.ds(value_at + col, 128)]
        outs, tops = [], []
        for h in range(2):
            scores = dot_nt(q, half(k, h)) + bias[:, :count]
            top = jnp.max(scores, axis=1, keepdims=True)
            e = jnp.exp(scores - top).astype(bf16)
            ering[hp, h, :, first : first + count] = e
            outs.append(dot(e, half_and_ones(v, h)))
            tops.append(top)
        both_heads = outs[0] + outs[1]
        weighted, sums = both_heads[:, :128], both_heads[:, 128:]
        top = jnp.where(low_lane, tops[0], tops[1])
        if part == 0:
            slots[MIXED, :, cols] = weighted
            slots[S_OWN, :, cols] = sums
            slots[F_OWN, :, cols] = top
            return
        if part == 1:
            slots[O_A, :, cols] = weighted
            slots[S_A, :, cols] = sums
            slots[F_A, :, cols] = top
            return
        top_own, top_a = slots[F_OWN, :, cols], slots[F_A, :, cols]
        highest = jnp.maximum(jnp.maximum(top_own, top_a), top)
        w_own = jnp.exp(top_own - highest)
        w_a = jnp.exp(top_a - highest)
        w_b = jnp.exp(top - highest)
        inverse = 1.0 / (w_own * slots[S_OWN, :, cols] + w_a * slots[S_A, :, cols] + w_b * sums)
        w_own, w_a, w_b = w_own * inverse, w_a * inverse, w_b * inverse
        slots[MIXED, :, cols] = (
            w_own * slots[MIXED, :, cols] + w_a * slots[O_A, :, cols] + w_b * weighted
        )
        slots[F_OWN, :, cols] = w_own
        slots[F_A, :, cols] = w_a
        slots[F_B, :, cols] = w_b

    def forward_three(part):
        def step(i, carry):
            for p in range(3):
                forward_pair(part, 3 * i + p)
            if part == 0:
                for p in range(3):
                    e_out(3 * i + p).start()
            return carry

        lax.fori_loop(0, PAIRS // 3, step, 0)

    forward_three(0)

    send_tags.wait()
    for part in (1, 2):
        first = (part - 1) * part_rows
        send_tok[part - 1].wait()
        first_norm(tokp, rows, first // ROW_TILE, (first + part_rows) // ROW_TILE)
        set_bias(False, first, part_rows)
        project(1, None, False, kvp, 0, first, part_rows)
        project(2, v_bias, False, kvp, D, first, part_rows)
        if part == 1:
            for hp in range(PAIRS):
                e_out(hp).wait()
        forward_three(part)

    loads[2].wait()

    def branch(c, carry):
        cols = pl.ds(pl.multiple_of(c * wide, wide), wide)
        out = dot(slots[MIXED].astype(bf16), wout[:, cols])
        out = out + out_bias[cols].reshape(1, wide)
        slots[RES, :, cols] = tok[:, cols].astype(f32) + out
        return carry

    lax.fori_loop(0, D // wide, branch, 0)
    gain_two, offset_two = row(ln2_gain), row(ln2_bias)

    def second_norm(t, carry):
        unit, _ = unit_of(slots[RES, tile(t), :])
        normed = (unit * gain_two + offset_two).astype(bf16)
        nrm[tile(t), :] = normed
        nrm2_t[:, tile(t)] = normed.T
        slots[ACC, tile(t), :] = jnp.zeros((ROW_TILE, D), f32)
        slots[GNT, tile(t), :] = jnp.zeros((ROW_TILE, D), f32)
        return carry

    lax.fori_loop(0, row_tiles, second_norm, 0)

    loads[3].wait()
    loads[4].wait()
    loads[5].wait()

    def feed(c, carry):
        units = pl.ds(pl.multiple_of(c * FF_CHUNK, FF_CHUNK), FF_CHUNK)
        w1 = wfc1[:, units]
        w2 = terms[pl.ds(pl.multiple_of(wfc2_at + c * FF_CHUNK, FF_CHUNK), FF_CHUNK), :]
        pre = dot(nrm[...], w1) + fc1_bias[units].reshape(1, FF_CHUNK)
        phi = 0.5 * (1.0 + lax.erf(pre * 0.7071067811865476))
        slope = phi + pre * jnp.exp(-0.5 * pre * pre) * 0.3989422804014327
        activated = (pre * phi).astype(bf16)
        grad_pre = (dot_nt(cot[...], w2) * slope).astype(bf16)
        slots[ACC] += dot(activated, w2)
        slots[GNT] += dot_nt(grad_pre, w1)
        @pl.when(c < 4)
        def _():
            wqkv[:rows, units] = activated

        @pl.when(c == 4)
        def _():
            wqkv[:rows, 8 * wide : 9 * wide] = activated[:, :wide]
            gm[:, :wide] = activated[:, wide:]

        @pl.when(c == 5)
        def _():
            gm[:, wide:] = activated

        fb1_ref[0:1, units] = column_sum(grad_pre.astype(f32))
        put_24(c, dot(nrm2_t[...], grad_pre))
        feed_tick(c)
        return carry

    lax.fori_loop(0, FF // FF_CHUNK, feed, 0)

    def weight_fc2(c, activated):
        values = jnp.concatenate(
            [dot_tn(activated[:, p * wide : (p + 1) * wide], cot[...]) for p in range(3)], axis=0
        )
        for low in range(8):
            there = bits_of(low)
            there["z0"], there["z1"] = (c % 2, c // 2) if isinstance(c, int) else (lax.rem(c, 2), c // 2)
            for order, lane, width in GROUPS:
                place = 16 * place_of(order, there)
                for j in range(6):
                    top = 96 * low + 16 * j
                    block = values[top : top + 16, lane : lane + width].astype(bf16)
                    at = pl.multiple_of((6 + j) * ITEM_ROWS + place, 16)
                    terms[pl.ds(at, 16), lane : lane + width] = block

    def weight_fc2_step(c, carry):
        weight_fc2(c, wqkv[:rows, pl.ds(pl.multiple_of(c * D, D), D)])
        return carry

    lax.fori_loop(0, 3, weight_fc2_step, 0)
    tick(6)
    weight_fc2(3, gm[...])
    reload = pltpu.make_async_copy(wqkv_hbm, wqkv, load_sem.at[1])
    reload.start()
    tick(7)

    vec_ref[...] = jnp.zeros(vec_ref.shape, f32)
    fb1_ref[1:8, :] = jnp.zeros((7, FF), f32)
    V_OB, V_LN2G, V_LN2B, V_FC2B = range(4)
    cs_ref[0] = jnp.zeros(cs_ref.shape[1:], f32)

    def add_vec(kind, values):
        vec_ref[kind : kind + 1, :] += column_sum(values)

    def second_back(t, carry):
        here = tile(t)
        unit, inverse = unit_of(slots[RES, here, :])
        tokp[here, :] = (
            slots[RES, here, :] + slots[ACC, here, :] + row(fc2_bias)
        ).astype(bf16)
        upstream = slots[GNT, here, :]
        grad_out = cot[here, :].astype(f32)
        add_vec(V_FC2B, grad_out)
        add_vec(V_LN2G, upstream * unit)
        add_vec(V_LN2B, upstream)
        scaled = upstream * gain_two
        grad = grad_out + inverse * (
            scaled
            - jnp.mean(scaled, axis=1, keepdims=True)
            - unit * jnp.mean(scaled * unit, axis=1, keepdims=True)
        )
        slots[RES, here, :] = grad
        low = grad.astype(bf16)
        nrm[here, :] = low
        add_vec(V_OB, low.astype(f32))
        return carry

    lax.fori_loop(0, 2, second_back, 0)
    tick(8)
    lax.fori_loop(2, row_tiles, second_back, 0)
    store_result = pltpu.make_async_copy(tokp, result_hbm.at[0], load_sem.at[0])
    store_result.start()
    tick(9)

    GQ = ACC

    def mixed_back(c, carry):
        cols = pl.ds(pl.multiple_of(c * wide, wide), wide)
        gm[:, cols] = dot_nt(nrm[...], wout[cols, :]).astype(bf16)
        mixed = slots[MIXED, :, cols].astype(bf16)
        wfc1[cols, :D] = dot_tn(mixed, nrm[...]).astype(bf16)
        return carry

    lax.fori_loop(0, D // wide, mixed_back, 0)
    def window(ref, first, count):
        block = first // 128 * 128
        shift = first - block
        wide_enough = 256 if shift + count > 128 else 128
        piece = ref[:, block : block + wide_enough]
        if shift:
            piece = pltpu.roll(piece, wide_enough - shift, 1)
        return piece[:, :128]

    small_order = GROUPS[0][0]
    for d in range(32):
        at = pl.multiple_of(16 * place_of(small_order, bits_of(d)), 16)
        small[pl.ds(at, 8), :] = window(vec_ref, 24 * d, 24)
        small[pl.ds(at + 8, 8), :] = window(fb1_ref, 96 * d, 96)

    def small_copy(stage):
        count = ITEM_ROWS >> stage
        return pltpu.make_async_remote_copy(
            src_ref=small.at[pl.ds(count, count)],
            dst_ref=small_in.at[pl.ds(LANDING[stage - 1], count)],
            send_sem=small_send.at[stage - 1],
            recv_sem=small_recv.at[stage - 1],
            device_id=across[small_order[stage - 1]],
            device_id_type=MESH,
        )

    def small_step(stage):
        small_copy(stage).wait()
        count = ITEM_ROWS >> stage
        came = small_in[LANDING[stage - 1] : LANDING[stage - 1] + count]
        small[:count] = small[:count] + came
        if stage < STAGES:
            small_copy(stage + 1).start()
            return
        for kind, ref in enumerate((out_ob, out_ln2g, out_ln2b, out_fb2)):
            ref[...] = small[kind, :24]
        out_fb1[...] = small[8, :96]

    small_copy(1).start()

    def sums_copy(stage):
        return pltpu.make_async_remote_copy(
            src_ref=cs_ref.at[stage - 1],
            dst_ref=cs_in.at[stage - 1],
            send_sem=sums_send.at[stage - 1],
            recv_sem=sums_recv.at[stage - 1],
            device_id=across[small_order[stage - 1]],
            device_id_type=MESH,
        )

    def sums_step(stage):
        sums_copy(stage).wait()
        cs_ref[stage] = cs_ref[stage - 1] + cs_in[stage - 1]
        if stage < STAGES:
            sums_copy(stage + 1).start()

    tick(10)

    def backward_pair(part, hp):
        own = part == 0
        ref, key_at, value_at = (qkv, D, 2 * D) if own else (kvp, 0, D)
        kind = (F_OWN, F_A, F_B)[part]
        count = rows if own else part_rows
        first = 0 if own else (part - 1) * part_rows
        keys = pl.ds(first, count)
        col = aligned(hp * 128, 128)
        cols = pl.ds(col, 128)
        q = qkv[:, cols]
        q_t = q.T
        k = ref[keys, pl.ds(key_at + col, 128)]
        v = ref[keys, pl.ds(value_at + col, 128)]
        grad_in = gm[:, cols].astype(f32)
        scaled = grad_in * slots[kind, :, cols]
        weighted = scaled * slots[MIXED, :, cols]
        scaled = scaled.astype(bf16)
        scaled_t = scaled.T
        grad_q = None
        grad_k, grad_v = [], []
        for h in range(2):
            delta = jnp.sum(half(weighted, h), axis=1, keepdims=True)
            e = ering[hp, h, :, first : first + count]
            grad_probs = dot_nt(scaled, half(v, h))
            grad_scores = (e.astype(f32) * (grad_probs - delta)).astype(bf16)
            term = dot(grad_scores, half(k, h))
            grad_q = term if grad_q is None else grad_q + term
            grad_k.append(dot(q_t[64 * h : 64 * h + 64], grad_scores))
            grad_v.append(dot(scaled_t[64 * h : 64 * h + 64], e))
        grad_k = jnp.concatenate(grad_k, axis=0).T.astype(bf16)
        grad_v = jnp.concatenate(grad_v, axis=0).T.astype(bf16)
        ref[keys, pl.ds(key_at + col, 128)] = grad_k
        ref[keys, pl.ds(value_at + col, 128)] = grad_v
        if part == 1:
            slots[GQ, :, cols] = grad_q
        elif part == 2:
            slots[GQ, :, cols] += grad_q
        else:
            total_q = (slots[GQ, :, cols] + grad_q) * score_scale
            qkv[:, cols] = total_q.astype(bf16)

    store_result.wait()
    reload.wait()
    send_gn = []
    for part in (1, 2):
        first = (part - 1) * part_rows
        here = pl.ds(first, part_rows)

        def twin_step(i, carry):
            for p in range(TWIN_UNROLL):
                backward_pair(part, TWIN_UNROLL * i + p)

            @pl.when(i == PAIRS // TWIN_UNROLL // 2 - 1)
            def _():
                tick(2 * part + 9)

            return carry

        lax.fori_loop(0, PAIRS // TWIN_UNROLL, twin_step, 0)
        if part == 2:
            for hp in range(PAIRS):
                e_in(hp).start()

        def partial_out(c, carry):
            cols = pl.ds(pl.multiple_of(c * wide, wide), wide)
            tokp[here, cols] = dot_nt(kvp[here, :], wqkv[cols, D : 3 * D]).astype(bf16)
            return carry

        lax.fori_loop(0, D // wide, partial_out, 0)
        for c in range(3):
            cols = pl.ds(wide * c, wide)
            sem = 2 + 3 * (part - 1) + c
            send_gn.append(to_twin(sem, tokp.at[here, cols], gn_in.at[here, cols]))
        tick(2 * part + 10)
        send_gn[part - 1].start()
        small_step(part)

    def own_step(hp, carry):
        e_in(hp).wait()
        backward_pair(0, hp)
        col = pl.multiple_of(hp * 128, 128)
        grad_q = qkv[:, pl.ds(col, 128)]
        own = jnp.concatenate(
            [qkv[:, pl.ds(D + col, 128)], qkv[:, pl.ds(2 * D + col, 128)]], axis=1
        )
        other = jnp.concatenate(
            [kvp[:, pl.ds(col, 128)], kvp[:, pl.ds(D + col, 128)]], axis=1
        )
        sum_kv = column_sum(own.astype(f32) + other.astype(f32))
        cs_ref[0, 0:1, pl.ds(col, 128)] = column_sum(grad_q.astype(f32))
        cs_ref[0, 1:2, pl.ds(col, 128)] = sum_kv[:, :128]
        cs_ref[0, 2:3, pl.ds(col, 128)] = sum_kv[:, 128:]
        weight_kv = dot(unit_t[...], jnp.concatenate([own, other], axis=0))
        weight_q = dot(unit_t[:, :rows], grad_q)
        weight_o = wfc1[:, pl.ds(col, 128)].astype(f32)
        put_24(12 + hp, jnp.concatenate([weight_kv, weight_q, weight_o], axis=1))
        tick(15 + hp, 15, 20)
        for c in range(4):
            pl.when(hp == c)(send_gn[2 + c].start)
        for c in range(3):
            pl.when(hp == 2 * c + 1)(functools.partial(small_step, 3 + c))
        return carry

    lax.fori_loop(0, PAIRS, own_step, 0)

    def first_back_product(c, carry):
        cols = pl.ds(pl.multiple_of(c * wide, wide), wide)
        slots[GNT, :, cols] = dot_nt(qkv[...], wqkv[cols, :])
        return carry

    sums_copy(1).start()
    lax.fori_loop(0, D // wide, first_back_product, 0)
    gain_one = row(ln1_gain)

    def first_back(t, carry):
        here = tile(t)
        unit, inverse = unit_of(tok[here, :].astype(f32))
        upstream = slots[GNT, here, :] + gn_in[here, :].astype(f32)
        scaled = upstream * gain_one
        grad = slots[RES, here, :] + inverse * (
            scaled
            - jnp.mean(scaled, axis=1, keepdims=True)
            - unit * jnp.mean(scaled * unit, axis=1, keepdims=True)
        )
        gm[here, :] = grad.astype(bf16)
        return carry

    last_tick = STARTS[-1] + ENDS[-1]
    middle = STARTS[-1] + 2

    def late_ticks(low, high):
        def step(number, carry):
            tick(number, low, high)
            for i, since in enumerate(SUMS_AT):
                if low <= STARTS[-1] + since <= high:
                    pl.when(number == STARTS[-1] + since)(functools.partial(sums_step, 1 + i))
            return carry

        lax.fori_loop(low, high + 1, step, 0)

    late_ticks(STARTS[-1] + 1, middle)
    for copy in send_gn:
        copy.wait()
    lax.fori_loop(0, row_tiles, first_back, 0)
    store_gtok = pltpu.make_async_copy(gm, gtok_hbm.at[0], load_sem.at[2])
    store_gtok.start()
    late_ticks(middle + 1, last_tick)

    me = seq * 2 + blk
    low_row = me * 24 // 16 * 16
    weights = wqkv[pl.ds(pl.multiple_of(low_row, 16), 32), :].astype(f32)
    weights = jnp.where(me * 24 == low_row, weights[:24], weights[8:])
    sums = cs_ref[STAGES]
    lanes = lax.broadcasted_iota(jnp.int32, (24, D), 1)
    mine = lanes == me * 24 + lax.broadcasted_iota(jnp.int32, (24, D), 0)

    def my_column(values):
        return jnp.sum(jnp.where(mine, values, 0.0), axis=1, keepdims=True)

    gain_mine, bias_mine = my_column(row(ln1_gain)), my_column(row(ln1_bias))
    gain_sum = jnp.zeros((24, 1), f32)
    bias_sum = jnp.zeros((24, 1), f32)
    for kind in range(3):
        cols = slice(kind * D, (kind + 1) * D)
        product = out_qkv[:, cols]
        total = sums[kind : kind + 1, :]
        gain_sum += jnp.sum(weights[:, cols] * product, axis=1, keepdims=True)
        bias_sum += jnp.sum(weights[:, cols] * total, axis=1, keepdims=True)
        out_qkv[:, cols] = gain_mine * product + bias_mine * total
    diagonal = lax.broadcasted_iota(jnp.int32, (24, 128), 0) == lax.broadcasted_iota(
        jnp.int32, (24, 128), 1
    )
    for ref, values in (
        (out_ln1g, gain_sum),
        (out_ln1b, bias_sum),
        (out_qb, my_column(sums[0:1])),
        (out_vb, my_column(sums[2:3])),
    ):
        ref[...] = column_sum(jnp.where(diagonal, values, 0.0))[0, :24]
    store_gtok.wait()


def hand_on(*refs):
    for i in range(15):
        refs[15 + i][...] = refs[i][...]


def block_body(
    tokens,
    lengths,
    padding,
    cotangent,
    ln1_gain,
    ln1_bias,
    w_qkv,
    q_bias,
    v_bias,
    w_out,
    out_bias,
    ln2_gain,
    ln2_bias,
    w_fc1,
    fc1_bias,
    w_fc2,
    fc2_bias,
):
    rows = tokens.shape[1]
    n_dev = lax.axis_size("seq") * lax.axis_size("blk")
    shape = jax.ShapeDtypeStruct
    any_spec = pl.BlockSpec(memory_space=pl.ANY)
    vmem = pl.BlockSpec(memory_space=pltpu.VMEM)
    smem = pl.BlockSpec(memory_space=pltpu.SMEM)
    part = D // n_dev
    line = shape((part,), f32)
    outs = pl.pallas_call(
        block_kernel,
        name="block",
        out_shape=(
            shape((1, rows, D), bf16),
            shape((1, rows, D), bf16),
            line,
            line,
            shape((part, 3 * D), f32),
            line,
            line,
            shape((part, D), f32),
            line,
            line,
            line,
            shape((part, FF), f32),
            shape((FF // n_dev,), f32),
            shape((FF // n_dev, D), f32),
            line,
            shape((PAIRS, 2, rows, rows), bf16),
        ),
        in_specs=[
            any_spec, smem, vmem, any_spec, vmem, vmem, any_spec, vmem, vmem,
            any_spec, vmem, vmem, vmem, any_spec, vmem, any_spec, vmem,
        ],
        out_specs=(any_spec,) * 2 + (vmem,) * 13 + (any_spec,),
        scratch_shapes=[
            pltpu.VMEM((D, 3 * D), bf16),
            pltpu.VMEM((D, D), bf16),
            pltpu.VMEM((D, FF), bf16),
            pltpu.VMEM((rows, D), bf16),
            pltpu.VMEM((rows, D), bf16),
            pltpu.VMEM((rows, D), bf16),
            pltpu.VMEM((rows, D), bf16),
            pltpu.VMEM((D, 2 * rows), bf16),
            pltpu.VMEM((D, rows), bf16),
            pltpu.VMEM((rows, 3 * D), bf16),
            pltpu.VMEM((rows, 2 * D), bf16),
            pltpu.VMEM((rows, D), bf16),
            pltpu.VMEM((rows, rows), f32),
            pltpu.VMEM((PAIRS, 2, rows, rows), bf16),
            pltpu.VMEM((7, rows, D), f32),
            pltpu.VMEM((ITEMS * ITEM_ROWS, ITEM_LANES), bf16),
            pltpu.VMEM((SLOTS * LANDING_ROWS, ITEM_LANES), bf16),
            pltpu.VMEM((rows, D), bf16),
            pltpu.VMEM((2, 8, rows), jnp.int32),
            pltpu.VMEM((8, D), f32),
            pltpu.VMEM((8, FF), f32),
            pltpu.VMEM((ITEM_ROWS, 128), f32),
            pltpu.VMEM((LANDING_ROWS, 128), f32),
            pltpu.VMEM((STAGES + 1, 8, D), f32),
            pltpu.VMEM((STAGES, 8, D), f32),
            pltpu.SemaphoreType.DMA((6,)),
            pltpu.SemaphoreType.DMA((PAIRS,)),
            pltpu.SemaphoreType.DMA((9,)),
            pltpu.SemaphoreType.DMA((9,)),
            pltpu.SemaphoreType.DMA((SLOTS * STAGES * len(GROUPS),)),
            pltpu.SemaphoreType.DMA((SLOTS * STAGES * len(GROUPS),)),
            pltpu.SemaphoreType.DMA((STAGES,)),
            pltpu.SemaphoreType.DMA((STAGES,)),
            pltpu.SemaphoreType.DMA((STAGES,)),
            pltpu.SemaphoreType.DMA((STAGES,)),
        ],
        compiler_params=pltpu.CompilerParams(
            collective_id=0, has_side_effects=True, vmem_limit_bytes=VMEM_LIMIT
        ),
        cost_estimate=pl.CostEstimate(
            flops=30 * 10**9, bytes_accessed=60 * 10**6, transcendentals=10**7
        ),
    )(
        tokens, lengths, padding, cotangent, ln1_gain, ln1_bias, w_qkv, q_bias, v_bias,
        w_out, out_bias, ln2_gain, ln2_bias, w_fc1, fc1_bias, w_fc2, fc2_bias,
    )
    return pl.pallas_call(
        hand_on,
        name="hand_on",
        out_shape=tuple(shape(o.shape, o.dtype) for o in outs[:15]),
        in_specs=[vmem] * 15,
        out_specs=(vmem,) * 15,
    )(*outs[:15])


VMEM_LIMIT = 63 * 2**20


def solution(mesh):
    in_specs = (
        P("seq", "blk", None),
        P("seq", None),
        P("seq", "blk"),
        P("seq", "blk", None),
        P(),
        P(),
        P(),
        P(),
        P(),
        P(),
        P(),
        P(),
        P(),
        P(),
        P(),
        P(),
        P(),
    )
    out_specs = (
        P("seq", "blk", None),
        P("seq", "blk", None),
        P(("seq", "blk")),
        P(("seq", "blk")),
        P(("seq", "blk"), None),
        P(("seq", "blk")),
        P(("seq", "blk")),
        P(("seq", "blk"), None),
        P(("seq", "blk")),
        P(("seq", "blk")),
        P(("seq", "blk")),
        P(("seq", "blk"), None),
        P(("seq", "blk")),
        P(("seq", "blk"), None),
        P(("seq", "blk")),
    )
    step = block_body if fits(mesh) else body
    return jax.shard_map(step, mesh=mesh, in_specs=in_specs, out_specs=out_specs, check_vma=False)
```

```python
import functools

import jax
import jax.numpy as jnp
from jax import lax
from jax.experimental import pallas as pl
from jax.experimental.pallas import tpu as pltpu
from jax.sharding import PartitionSpec as P

D = 768
FF = 3072
HEADS = 12
HEAD_DIM = 64


epsilon = 1e-06
score_scale = 0.125
masked_score = -1e30


def clip_numbers(clip_lengths, positions):
    bounds = jnp.cumsum(clip_lengths)
    return jnp.sum((positions[:, None] >= bounds[None, :]).astype(jnp.int32), axis=1)


def normalize(values, scales, offset):
    center = values - jnp.mean(values, axis=-1, keepdims=True)
    spread = jnp.mean(center * center, axis=-1, keepdims=True)
    inverse = lax.rsqrt(spread + epsilon)
    unit = center * inverse
    return (unit * scales + offset, unit, inverse)


def norm_back(upstream, unit, inverse, scales):
    scaled = upstream * scales
    return inverse * (
        scaled
        - jnp.mean(scaled, axis=-1, keepdims=True)
        - unit * jnp.mean(scaled * unit, axis=-1, keepdims=True)
    )


def gelu_slope(pre_gelu):
    cdf_part = 0.5 * (1.0 + lax.erf(pre_gelu * 0.7071067811865476))
    return cdf_part + pre_gelu * jnp.exp(-0.5 * pre_gelu * pre_gelu) * 0.3989422804014327


def masked_scores(query_heads, key_heads, clip_ids, positions, block_tags, key_pos):
    raw_scores = (
        jnp.einsum("qhd,khd->qhk", query_heads, key_heads, preferred_element_type=jnp.float32)
        * score_scale
    )
    allowed = (block_tags[None, :] == clip_ids[:, None]) | (positions[:, None] == key_pos[None, :])
    return jnp.where(allowed[:, None, :], raw_scores, masked_score)


def score_grads(
    query_heads,
    key_heads,
    value_heads,
    grad_heads,
    log_total,
    row_delta,
    clip_ids,
    positions,
    block_tags,
    key_pos,
):
    scores = masked_scores(query_heads, key_heads, clip_ids, positions, block_tags, key_pos)
    attn_probs = jnp.exp(scores - log_total[..., None])
    grad_probs = jnp.einsum(
        "qhd,khd->qhk", grad_heads, value_heads, preferred_element_type=jnp.float32
    )
    grad_scores = (attn_probs * (grad_probs - row_delta[..., None])).astype(jnp.bfloat16)
    return (attn_probs, grad_scores)


def stage_orders():
    seq_bits = lax.axis_size("seq").bit_length() - 1
    blk_bits = lax.axis_size("blk").bit_length() - 1
    seq_stages = [blk_bits + b for b in range(seq_bits)]
    blk_stages = list(range(blk_bits))
    one = seq_stages[:2] + blk_stages + seq_stages[2:]
    two = seq_stages[:1] + blk_stages + seq_stages[1:]
    return one, two


def scatter_stages(terms, order):
    n_dev = terms.shape[0]
    bits = n_dev.bit_length() - 1
    me = lax.axis_index("seq") * lax.axis_size("blk") + lax.axis_index("blk")
    rest = terms.shape[1:]
    kind = terms.dtype
    held = terms.reshape((2,) * bits + rest)
    for number, bit in enumerate(order):
        axis = bits - 1 - bit
        mine = (me >> bit) & 1
        sent = lax.dynamic_slice_in_dim(held, 1 - mine, 1, axis)
        kept = lax.dynamic_slice_in_dim(held, mine, 1, axis)
        swap = [(i, i ^ (1 << bit)) for i in range(n_dev)]
        came = lax.ppermute(sent, ("seq", "blk"), swap)
        total = kept.astype(jnp.float32) + came.astype(jnp.float32)
        held = total if number == bits - 1 else total.astype(kind)
    return held.reshape((1,) + rest)


def scatter_sum(grad):
    n_dev = lax.axis_size("seq") * lax.axis_size("blk")
    rows, width = grad.shape
    terms = grad.astype(jnp.bfloat16).reshape(n_dev, rows // n_dev, width)
    one, two = stage_orders()
    left = scatter_stages(terms[:, :, : width // 2], one)[0]
    right = scatter_stages(terms[:, :, width // 2 :], two)[0]
    return jnp.concatenate([left, right], axis=1)


def body(
    tokens,
    lengths,
    padding,
    cotangent,
    ln1_gain,
    ln1_bias,
    w_qkv,
    q_bias,
    v_bias,
    w_out,
    out_bias,
    ln2_gain,
    ln2_bias,
    w_fc1,
    fc1_bias,
    w_fc2,
    fc2_bias,
):
    tok_rows = tokens.shape[1]
    group_size = lax.axis_size("blk")
    n_dev = lax.axis_size("seq") * group_size
    positions = lax.axis_index("blk") * tok_rows + jnp.arange(tok_rows, dtype=jnp.int32)
    clip_ids = clip_numbers(lengths[0], positions)
    key_tags = jnp.where(padding[0] == 1, -1, clip_ids)
    tokens_f32 = tokens[0].astype(jnp.float32)
    first_norm, unit_one, inverse_one = normalize(tokens_f32, ln1_gain, ln1_bias)
    normed_one = first_norm.astype(jnp.bfloat16)
    joint_bias = jnp.concatenate([q_bias, jnp.zeros_like(q_bias), v_bias])
    projected = (
        jnp.dot(normed_one, w_qkv, preferred_element_type=jnp.float32) + joint_bias
    ).astype(jnp.bfloat16)
    keys_own = projected[:, D : 2 * D]
    values_own = projected[:, 2 * D :]
    query_heads = projected[:, :D].reshape(tok_rows, HEADS, HEAD_DIM)
    starts = jnp.arange(group_size, dtype=jnp.int32) * tok_rows

    def fold_keys(running, key_block, offset):
        block_keys, block_values, block_tags = key_block
        key_count = block_keys.shape[0]
        key_pos = offset + jnp.arange(key_count, dtype=jnp.int32)
        scores = masked_scores(
            query_heads,
            block_keys.reshape(key_count, HEADS, HEAD_DIM),
            clip_ids,
            positions,
            block_tags,
            key_pos,
        )
        row_max, row_sum, weighted = running
        new_max = jnp.maximum(row_max, jnp.max(scores, axis=-1))
        rescale = jnp.exp(row_max - new_max)
        exp_scores = jnp.exp(scores - new_max[..., None])
        row_sum = row_sum * rescale + jnp.sum(exp_scores, axis=-1)
        weighted = weighted * rescale[..., None] + jnp.einsum(
            "qhk,khd->qhd",
            exp_scores.astype(jnp.bfloat16),
            block_values.reshape(key_count, HEADS, HEAD_DIM),
            preferred_element_type=jnp.float32,
        )
        return (new_max, row_sum, weighted)

    start_state = (
        jnp.full((tok_rows, HEADS), masked_score, jnp.float32),
        jnp.zeros((tok_rows, HEADS), jnp.float32),
        jnp.zeros((tok_rows, HEADS, HEAD_DIM), jnp.float32),
    )
    group_keys, group_values, group_tags = (
        lax.all_gather(keys_own, "blk", axis=0, tiled=True),
        lax.all_gather(values_own, "blk", axis=0, tiled=True),
        lax.all_gather(key_tags, "blk", axis=0, tiled=True),
    )

    def scan_fold(running, scan_args):
        return (fold_keys(running, (scan_args[0], scan_args[1], scan_args[2]), scan_args[3]), None)

    final_state = lax.scan(
        scan_fold,
        start_state,
        (
            group_keys.reshape(group_size, tok_rows, D),
            group_values.reshape(group_size, tok_rows, D),
            group_tags.reshape(group_size, tok_rows),
            starts,
        ),
    )[0]
    row_max, row_sum, weighted = final_state
    mixed_f32 = weighted / row_sum[..., None]
    log_total = row_max + jnp.log(row_sum)
    mixed = mixed_f32.reshape(tok_rows, D).astype(jnp.bfloat16)
    residual = tokens_f32 + jnp.dot(mixed, w_out, preferred_element_type=jnp.float32) + out_bias
    second_norm, unit_two, inverse_two = normalize(residual, ln2_gain, ln2_bias)
    normed_two = second_norm.astype(jnp.bfloat16)
    pre_gelu = jnp.dot(normed_two, w_fc1, preferred_element_type=jnp.float32) + fc1_bias
    activated = jax.nn.gelu(pre_gelu, approximate=False).astype(jnp.bfloat16)
    result = (
        residual + jnp.dot(activated, w_fc2, preferred_element_type=jnp.float32) + fc2_bias
    ).astype(jnp.bfloat16)
    grad_out = cotangent[0]
    grad_fc2_bias = jnp.sum(grad_out, axis=0, dtype=jnp.float32)
    grad_w_fc2 = jnp.einsum("tf,td->fd", activated, grad_out, preferred_element_type=jnp.float32)
    grad_act = jnp.einsum("td,fd->tf", grad_out, w_fc2, preferred_element_type=jnp.float32)
    grad_pre = (grad_act * gelu_slope(pre_gelu)).astype(jnp.bfloat16)
    grad_fc1_bias = jnp.sum(grad_pre, axis=0, dtype=jnp.float32)
    grad_w_fc1 = jnp.einsum("td,tf->df", normed_two, grad_pre, preferred_element_type=jnp.float32)
    grad_norm_two = jnp.einsum("tf,df->td", grad_pre, w_fc1, preferred_element_type=jnp.float32)
    grad_ln2_gain = jnp.sum(grad_norm_two * unit_two, axis=0)
    grad_ln2_bias = jnp.sum(grad_norm_two, axis=0)
    grad_residual = grad_out.astype(jnp.float32) + norm_back(
        grad_norm_two, unit_two, inverse_two, ln2_gain
    )
    grad_branch = grad_residual.astype(jnp.bfloat16)
    grad_out_bias = jnp.sum(grad_branch, axis=0, dtype=jnp.float32)
    grad_w_out = jnp.einsum("td,te->de", mixed, grad_branch, preferred_element_type=jnp.float32)
    grad_mixed = jnp.einsum(
        "te,de->td", grad_branch, w_out, preferred_element_type=jnp.float32
    ).astype(jnp.bfloat16)
    grad_heads = grad_mixed.reshape(tok_rows, HEADS, HEAD_DIM)
    row_delta = jnp.sum(grad_heads * mixed_f32, axis=-1)
    key_stack = (
        group_keys.reshape(group_size, tok_rows, D),
        group_values.reshape(group_size, tok_rows, D),
        group_tags.reshape(group_size, tok_rows),
        starts,
    )

    def back_block(grad_queries, scan_args):
        block_keys, block_values, block_tags, offset = scan_args
        key_pos = offset + jnp.arange(tok_rows, dtype=jnp.int32)
        key_heads = block_keys.reshape(tok_rows, HEADS, HEAD_DIM)
        value_heads = block_values.reshape(tok_rows, HEADS, HEAD_DIM)
        attn_probs, grad_scores = score_grads(
            query_heads,
            key_heads,
            value_heads,
            grad_heads,
            log_total,
            row_delta,
            clip_ids,
            positions,
            block_tags,
            key_pos,
        )
        grad_values = jnp.einsum(
            "qhk,qhd->khd",
            attn_probs.astype(jnp.bfloat16),
            grad_heads,
            preferred_element_type=jnp.float32,
        )
        grad_queries = (
            grad_queries
            + jnp.einsum("qhk,khd->qhd", grad_scores, key_heads, preferred_element_type=jnp.float32)
            * score_scale
        )
        grad_keys = (
            jnp.einsum("qhk,qhd->khd", grad_scores, query_heads, preferred_element_type=jnp.float32)
            * score_scale
        )
        return (
            grad_queries,
            jnp.concatenate(
                [grad_keys.reshape(tok_rows, D), grad_values.reshape(tok_rows, D)], axis=1
            ),
        )

    grad_queries, key_terms = lax.scan(
        back_block, jnp.zeros((tok_rows, HEADS, HEAD_DIM), jnp.float32), key_stack
    )
    key_sums = lax.psum_scatter(
        key_terms.reshape(group_size * tok_rows, 2 * D).astype(jnp.bfloat16),
        "blk",
        scatter_dimension=0,
        tiled=True,
    )
    grad_qkv = jnp.concatenate(
        [grad_queries.reshape(tok_rows, D).astype(jnp.bfloat16), key_sums], axis=1
    )
    grad_q_bias = jnp.sum(grad_qkv[:, :D], axis=0, dtype=jnp.float32)
    grad_v_bias = jnp.sum(grad_qkv[:, 2 * D :], axis=0, dtype=jnp.float32)
    grad_w_qkv = jnp.einsum("td,te->de", normed_one, grad_qkv, preferred_element_type=jnp.float32)
    grad_norm_one = jnp.einsum("te,de->td", grad_qkv, w_qkv, preferred_element_type=jnp.float32)
    grad_ln1_gain = jnp.sum(grad_norm_one * unit_one, axis=0)
    grad_ln1_bias = jnp.sum(grad_norm_one, axis=0)
    grad_tokens = (
        grad_residual + norm_back(grad_norm_one, unit_one, inverse_one, ln1_gain)
    ).astype(jnp.bfloat16)
    small = jnp.concatenate(
        [
            v.reshape(n_dev, -1)
            for v in (
                grad_ln1_gain,
                grad_ln1_bias,
                grad_q_bias,
                grad_v_bias,
                grad_out_bias,
                grad_ln2_gain,
                grad_ln2_bias,
                grad_fc1_bias,
                grad_fc2_bias,
            )
        ],
        axis=1,
    )
    sum_fc2 = scatter_sum(grad_w_fc2)
    sum_fc1 = scatter_sum(grad_w_fc1)
    sum_out = scatter_sum(grad_w_out)
    sum_qkv = scatter_sum(grad_w_qkv)
    part = D // n_dev
    small = scatter_stages(small, stage_orders()[0])[0]
    pieces = []
    at = 0
    for size in (part, part, part, part, part, part, part, FF // n_dev, part):
        pieces.append(small[at : at + size])
        at += size
    summed = (
        pieces[0],
        pieces[1],
        sum_qkv,
        pieces[2],
        pieces[3],
        sum_out,
        pieces[4],
        pieces[5],
        pieces[6],
        sum_fc1,
        pieces[7],
        sum_fc2,
        pieces[8],
    )
    return (
        result[None],
        grad_tokens[None],
        summed[0],
        summed[1],
        summed[2],
        summed[3],
        summed[4],
        summed[5],
        summed[6],
        summed[7],
        summed[8],
        summed[9],
        summed[10],
        summed[11],
        summed[12],
    )


f32 = jnp.float32
bf16 = jnp.bfloat16
MESH = pl.DeviceIdType.MESH
PAIRS = HEADS // 2
FF_CHUNK = 512
ROW_TILE = 128
TWIN_UNROLL = 3
ITEMS = 18
ITEM_ROWS = 512
ITEM_LANES = 768
SLOTS = 6
STAGES = 5
STARTS = (0, 1, 2, 3, 4, 5, 7, 8, 9, 10, 11, 12, 15, 16, 17, 18, 19, 20)
ENDS = (0, 1, 4, 7, 10, 13)
SUMS_AT = (1, 3, 6, 9, 12)
LANDING = (0, 256, 384, 448, 480)
LANDING_ROWS = 496
FLAT_BITS = ("y", "c", "x", "z0", "z1")
GROUPS = (
    (("c", "x", "y", "z0", "z1"), 0, 384),
    (("c", "z0", "z1", "y", "x"), 384, 256),
    (("c", "y", "x", "z0", "z1"), 640, 128),
)


def fits(mesh):
    return dict(mesh.shape) == {"seq": 16, "blk": 2}


def dot(a, b):
    return lax.dot_general(a, b, (((1,), (0,)), ((), ())), preferred_element_type=f32)


def dot_nt(a, b):
    return lax.dot_general(a, b, (((1,), (1,)), ((), ())), preferred_element_type=f32)


def dot_tn(a, b):
    return lax.dot_general(a, b, (((0,), (0,)), ((), ())), preferred_element_type=f32)


def aligned(at, step):
    return at if isinstance(at, int) else pl.multiple_of(at, step)


def unit_of(values):
    center = values - jnp.mean(values, axis=1, keepdims=True)
    inverse = lax.rsqrt(jnp.mean(center * center, axis=1, keepdims=True) + epsilon)
    return center * inverse, inverse


def row(ref):
    return ref[...].reshape(1, ref.shape[0])


def column_sum(values):
    return jnp.sum(values, axis=0, keepdims=True)


def block_kernel(
    tok_hbm,
    len_ref,
    pad_ref,
    cot_hbm,
    ln1_gain,
    ln1_bias,
    wqkv_hbm,
    q_bias,
    v_bias,
    wout_hbm,
    out_bias,
    ln2_gain,
    ln2_bias,
    wfc1_hbm,
    fc1_bias,
    wfc2_hbm,
    fc2_bias,
    result_hbm,
    gtok_hbm,
    out_qkv,
    out_out,
    out_fc1,
    out_fc2,
    out_small,
    e_hbm,
    wqkv,
    wout,
    wfc1,
    tok,
    tokp,
    cot,
    nrm,
    unit_t,
    nrm2_t,
    qkv,
    kvp,
    gm,
    bias,
    ering,
    slots,
    terms,
    landing,
    gn_in,
    tags,
    vec_ref,
    fb1_ref,
    small,
    small_in,
    cs_ref,
    cs_in,
    load_sem,
    e_sem,
    send_sem,
    recv_sem,
    item_send,
    item_recv,
    small_send,
    small_recv,
    sums_send,
    sums_recv,
):
    rows = tok.shape[0]
    seq = lax.axis_index("seq")
    blk = lax.axis_index("blk")
    bit = {
        "y": blk,
        "c": lax.rem(seq, 2),
        "x": lax.rem(seq // 2, 2),
        "z0": lax.rem(seq // 4, 2),
        "z1": seq // 8,
    }
    across = {
        "y": (seq, 1 - blk),
        "c": (seq + 1 - 2 * bit["c"], blk),
        "x": (seq + 2 - 4 * bit["x"], blk),
        "z0": (seq + 4 - 8 * bit["z0"], blk),
        "z1": (seq + 8 - 16 * bit["z1"], blk),
    }
    twin = across["y"]

    barrier = pltpu.get_barrier_semaphore()
    for name in FLAT_BITS:
        pl.semaphore_signal(barrier, inc=1, device_id=across[name], device_id_type=MESH)

    wfc2_at = (ITEMS - 6) * ITEM_ROWS
    wfc2 = terms.at[pl.ds(wfc2_at, FF)]
    loads = [
        pltpu.make_async_copy(src, dst, load_sem.at[i])
        for i, (src, dst) in enumerate(
            (
                (tok_hbm.at[0], tok),
                (wqkv_hbm, wqkv),
                (wout_hbm, wout),
                (wfc1_hbm, wfc1),
                (wfc2_hbm, wfc2),
                (cot_hbm.at[0], cot),
            )
        )
    ]
    for copy in loads[:2]:
        copy.start()

    ends = []
    total = jnp.int32(0)
    for i in range(len_ref.shape[1]):
        total = total + len_ref[0, i]
        ends.append(total)

    def clips_at(positions):
        number = jnp.zeros_like(positions)
        for end in ends:
            number = number + jnp.where(positions >= end, 1, 0)
        return number

    base = blk * rows
    lane_pos = base + lax.broadcasted_iota(jnp.int32, (8, rows), 1)
    padding = jnp.broadcast_to(pad_ref[...], (8, rows))
    tags[0] = jnp.where(padding == 1, -1, clips_at(lane_pos))

    pl.semaphore_wait(barrier, len(FLAT_BITS))

    def to_twin(i, src, dst):
        return pltpu.make_async_remote_copy(
            src_ref=src,
            dst_ref=dst,
            send_sem=send_sem.at[i],
            recv_sem=recv_sem.at[i],
            device_id=twin,
            device_id_type=MESH,
        )

    part_rows = rows // 2
    send_tags = to_twin(1, tags.at[0], tags.at[1])
    send_tags.start()
    send_tok = []
    for part, sem in ((0, 0), (1, 8)):
        here = pl.ds(part * part_rows, part_rows)
        send_tok.append(to_twin(sem, tok_hbm.at[0, here], tokp.at[here]))
        send_tok[part].start()

    def place_of(order, there):
        at = 0
        for stage, name in enumerate(order):
            differs = there[name] + bit[name] - 2 * there[name] * bit[name]
            at = at + (16 >> stage) * differs
        return at

    def bits_of(d):
        return {name: (d >> i) & 1 for i, name in enumerate(FLAT_BITS)}

    def item_copies(stage, item):
        count = ITEM_ROWS >> stage
        slot = item % SLOTS if isinstance(item, int) else lax.rem(item, SLOTS)
        first = item * ITEM_ROWS
        src_at = aligned(first + count, 16)
        dst_at = aligned(slot * LANDING_ROWS + LANDING[stage - 1], 16)
        copies = []
        for group, (order, lane, width) in enumerate(GROUPS):
            if stage == 1:
                if group > 0:
                    break
                width = ITEM_LANES
            lanes = pl.ds(lane, width)
            sem = (slot * STAGES + stage - 1) * len(GROUPS) + group
            copies.append(
                pltpu.make_async_remote_copy(
                    src_ref=terms.at[pl.ds(src_at, count), lanes],
                    dst_ref=landing.at[pl.ds(dst_at, count), lanes],
                    send_sem=item_send.at[sem],
                    recv_sem=item_recv.at[sem],
                    device_id=across[order[stage - 1]],
                    device_id_type=MESH,
                )
            )
        return copies

    def start_stage(stage, item):
        for copy in item_copies(stage, item):
            copy.start()

    def store_sum(item, kind, values):
        if kind == 1:
            at = aligned((item - 6) * 16, 16)
            out_fc2[pl.ds(at, 16), :] = values
            return
        parts = (
            (0, 16, values[:, :256], values[:, 256:512]),
            (16, 8, values[:8, 512:], values[8:, 512:]),
        )
        for top, count, left, right in parts:
            here = pl.ds(top, count)
            if kind == 0:
                col = aligned(item * 512, 512)
                out_fc1[here, pl.ds(col, 256)] = left
                out_fc1[here, pl.ds(col + 256, 256)] = right
            else:
                col = aligned((item - 12) * 128, 128)
                out_qkv[here, pl.ds(D + col, 128)] = left[:, :128]
                out_qkv[here, pl.ds(2 * D + col, 128)] = left[:, 128:]
                out_qkv[here, pl.ds(col, 128)] = right[:, :128]
                out_out[here, pl.ds(col, 128)] = right[:, 128:]

    def finish_stage(stage, item, low, high):
        for copy in item_copies(stage, item):
            copy.wait()
        count = ITEM_ROWS >> stage
        slot = item % SLOTS if isinstance(item, int) else lax.rem(item, SLOTS)
        first = item * ITEM_ROWS
        here = pl.ds(aligned(first, 16), count)
        came = pl.ds(aligned(slot * LANDING_ROWS + LANDING[stage - 1], 16), count)
        if stage < STAGES:
            terms[here, :] = terms[here, :] + landing[came, :]
            start_stage(stage + 1, item)
            return
        values = terms[here, :].astype(f32) + landing[came, :].astype(f32)
        for kind in range(3):
            if high < 6 * kind or low >= 6 * kind + 6:
                continue
            if low >= 6 * kind and high < 6 * kind + 6:
                store_sum(item, kind, values)
            else:
                pl.when((item >= 6 * kind) & (item < 6 * kind + 6))(
                    functools.partial(store_sum, item, kind, values)
                )

    def feed_tick(number):
        for stage in range(STAGES, 0, -1):
            if ENDS[stage] < 6:
                item = number - ENDS[stage]
                act = functools.partial(finish_stage, stage, item, 0, 5)
                pl.when(item >= 0)(act)
        start_stage(1, number)

    def tick(number, low=None, high=None):
        low = number if low is None else low
        high = number if high is None else high
        for stage in range(STAGES, -1, -1):
            begun = range(low - ENDS[stage], high - ENDS[stage] + 1)
            items = [STARTS.index(t) for t in begun if t in STARTS]
            if not items:
                continue
            if low == high:
                item = items[0]
            else:
                t = number - ENDS[stage]
                item = t - jnp.where(t >= 7, 1, 0) - jnp.where(t >= 15, 2, 0)
            if stage == 0:
                act = functools.partial(start_stage, 1, item)
            else:
                act = functools.partial(finish_stage, stage, item, items[0], items[-1])
            if len(items) == len(begun):
                act()
            else:
                valid = None
                for t_out in begun:
                    if t_out not in STARTS:
                        here = t != t_out
                        valid = here if valid is None else valid & here
                pl.when(valid)(act)

    def put_24(item, values):
        base_row = item * ITEM_ROWS
        for d in range(32):
            top = values[24 * d : 24 * d + 16, :]
            rest = values[24 * d + 16 : 24 * d + 24, :]
            rest = jnp.concatenate([rest[:, :256], rest[:, 256:]], axis=0)
            block = jnp.concatenate([top, rest], axis=1).astype(bf16)
            for order, lane, width in GROUPS:
                at = pl.multiple_of(base_row + 16 * place_of(order, bits_of(d)), 16)
                terms[pl.ds(at, 16), lane : lane + width] = block[:, lane : lane + width]

    row_tiles = rows // ROW_TILE

    def tile(t):
        return pl.ds(pl.multiple_of(t * ROW_TILE, ROW_TILE), ROW_TILE)

    def first_norm(src, columns_at, first, last):
        gain, offset = row(ln1_gain), row(ln1_bias)

        def step(t, carry):
            unit, _ = unit_of(src[tile(t), :].astype(f32))
            normed = (unit * gain + offset).astype(bf16)
            nrm[tile(t), :] = normed
            at = pl.multiple_of(columns_at + t * ROW_TILE, ROW_TILE)
            unit_t[:, pl.ds(at, ROW_TILE)] = unit.astype(bf16).T
            return carry

        lax.fori_loop(first, last, step, 0)

    def set_bias(own, first, count):
        clip_col = clips_at(base + lax.broadcasted_iota(jnp.int32, (rows, count), 0))
        tag_row = tags[0 if own else 1, 0:1, first : first + count]
        allowed = jnp.broadcast_to(tag_row, (rows, count)) == clip_col
        if own:
            here = lax.broadcasted_iota(jnp.int32, (rows, count), 0)
            there = lax.broadcasted_iota(jnp.int32, (rows, count), 1)
            allowed = allowed | (here == there)
        bias[:, :count] = jnp.where(allowed, 0.0, masked_score)

    loads[0].wait()
    first_norm(tok, 0, 0, row_tiles)
    set_bias(True, 0, rows)
    loads[1].wait()
    for copy in loads[2:]:
        copy.start()
    wide = 256

    def project(kind, add, scale, dst, dst_at, first=0, count=rows):
        here = pl.ds(first, count)

        def step(c, carry):
            col = pl.multiple_of(c * wide, wide)
            out = dot(nrm[here, :], wqkv[:, pl.ds(kind * D + col, wide)])
            if add is not None:
                out = out + add[pl.ds(col, wide)].reshape(1, wide)
            out = out.astype(bf16)
            if scale:
                out = out * jnp.bfloat16(score_scale)
            dst[here, pl.ds(dst_at + col, wide)] = out
            return carry

        lax.fori_loop(0, D // wide, step, 0)

    project(0, q_bias, True, qkv, 0)
    project(1, None, False, qkv, D)
    project(2, v_bias, False, qkv, 2 * D)

    low_lane = lax.broadcasted_iota(jnp.int32, (rows, 128), 1) < 64

    def half(values, h):
        mask = low_lane[: values.shape[0]]
        return jnp.where(mask if h == 0 else ~mask, values, jnp.zeros_like(values))

    def half_and_ones(values, h):
        return jnp.concatenate([half(values, h), half(jnp.ones_like(values), h)], axis=1)

    def e_out(hp):
        return pltpu.make_async_copy(ering.at[hp], e_hbm.at[hp], e_sem.at[hp])

    def e_in(hp):
        return pltpu.make_async_copy(e_hbm.at[hp], ering.at[hp], e_sem.at[hp])

    MIXED, F_OWN, F_A, F_B, RES, ACC, GNT = range(7)

    S_OWN, S_A, O_A = F_B, ACC, RES

    def forward_pair(part, hp):
        own = part == 0
        count = rows if own else part_rows
        first = 0 if own else (part - 1) * part_rows
        keys = pl.ds(first, count)
        ref, key_at, value_at = (qkv, D, 2 * D) if own else (kvp, 0, D)
        col = aligned(hp * 128, 128)
        cols = pl.ds(col, 128)
        q = qkv[:, cols]
        k = ref[keys, pl.ds(key_at + col, 128)]
        v = ref[keys, pl.ds(value_at + col, 128)]
        outs, tops = [], []
        for h in range(2):
            scores = dot_nt(q, half(k, h)) + bias[:, :count]
            top = jnp.max(scores, axis=1, keepdims=True)
            e = jnp.exp(scores - top).astype(bf16)
            ering[hp, h, :, first : first + count] = e
            outs.append(dot(e, half_and_ones(v, h)))
            tops.append(top)
        both_heads = outs[0] + outs[1]
        weighted, sums = both_heads[:, :128], both_heads[:, 128:]
        top = jnp.where(low_lane, tops[0], tops[1])
        if part == 0:
            slots[MIXED, :, cols] = weighted
            slots[S_OWN, :, cols] = sums
            slots[F_OWN, :, cols] = top
            return
        if part == 1:
            slots[O_A, :, cols] = weighted
            slots[S_A, :, cols] = sums
            slots[F_A, :, cols] = top
            return
        top_own, top_a = slots[F_OWN, :, cols], slots[F_A, :, cols]
        highest = jnp.maximum(jnp.maximum(top_own, top_a), top)
        w_own = jnp.exp(top_own - highest)
        w_a = jnp.exp(top_a - highest)
        w_b = jnp.exp(top - highest)
        inverse = 1.0 / (w_own * slots[S_OWN, :, cols] + w_a * slots[S_A, :, cols] + w_b * sums)
        w_own, w_a, w_b = w_own * inverse, w_a * inverse, w_b * inverse
        slots[MIXED, :, cols] = (
            w_own * slots[MIXED, :, cols] + w_a * slots[O_A, :, cols] + w_b * weighted
        )
        slots[F_OWN, :, cols] = w_own
        slots[F_A, :, cols] = w_a
        slots[F_B, :, cols] = w_b

    def forward_three(part):
        def step(i, carry):
            for p in range(3):
                forward_pair(part, 3 * i + p)
            if part == 0:
                for p in range(3):
                    e_out(3 * i + p).start()
            return carry

        lax.fori_loop(0, PAIRS // 3, step, 0)

    forward_three(0)

    def chunk_rows(first, c):
        return pl.ds(pl.multiple_of(first + c * FF_CHUNK, FF_CHUNK), FF_CHUNK)

    send_tags.wait()
    for part in (1, 2):
        first = (part - 1) * part_rows
        send_tok[part - 1].wait()
        first_norm(tokp, rows, first // ROW_TILE, (first + part_rows) // ROW_TILE)
        set_bias(False, first, part_rows)
        project(1, None, False, kvp, 0, first, part_rows)
        project(2, v_bias, False, kvp, D, first, part_rows)
        if part == 1:
            for hp in range(PAIRS):
                e_out(hp).wait()
        forward_three(part)

    loads[2].wait()

    gain_two, offset_two = row(ln2_gain), row(ln2_bias)
    for part in range(2):
        here = slice(part * part_rows, (part + 1) * part_rows)
        out = dot(slots[MIXED, here, :].astype(bf16), wout[...])
        residual = tok[here, :].astype(f32) + out + row(out_bias)
        unit, _ = unit_of(residual)
        normed = (unit * gain_two + offset_two).astype(bf16)
        nrm[here, :] = normed
        nrm2_t[:, here] = normed.T
        slots[RES, here, :] = residual
        slots[ACC, here, :] = residual + row(fc2_bias)
        slots[GNT, here, :] = jnp.zeros((part_rows, D), f32)

    loads[3].wait()
    loads[4].wait()
    loads[5].wait()

    def feed(c, carry):
        units = pl.ds(pl.multiple_of(c * FF_CHUNK, FF_CHUNK), FF_CHUNK)
        w1 = wfc1[:, units]
        w2 = terms[chunk_rows(wfc2_at, c), :]
        pre = dot(nrm[...], w1) + fc1_bias[units].reshape(1, FF_CHUNK)
        phi = 0.5 * (1.0 + lax.erf(pre * 0.7071067811865476))
        slope = phi + pre * jnp.exp(-0.5 * pre * pre) * 0.3989422804014327
        activated = (pre * phi).astype(bf16)
        grad_pre = (dot_nt(cot[...], w2) * slope).astype(bf16)
        slots[ACC] += dot(activated, w2)
        slots[GNT] += dot_nt(grad_pre, w1)
        terms[chunk_rows(wfc2_at, c), :FF_CHUNK] = activated
        fb1_ref[0:1, units] = column_sum(grad_pre.astype(f32))
        put_24(c, dot(nrm2_t[...], grad_pre))
        feed_tick(c)
        return carry

    lax.fori_loop(0, FF // FF_CHUNK, feed, 0)

    def weight_fc2(c, carry):
        pieces = []
        for p in range(3):
            piece = 3 * c + p
            lanes = pl.ds(pl.multiple_of(lax.rem(piece, 2) * wide, wide), wide)
            pieces.append(dot_tn(terms[chunk_rows(wfc2_at, piece // 2), lanes], cot[...]))
        values = jnp.concatenate(pieces, axis=0)
        for low in range(8):
            there = bits_of(low)
            there["z0"], there["z1"] = lax.rem(c, 2), c // 2
            for order, lane, width in GROUPS:
                place = 16 * place_of(order, there)
                for j in range(6):
                    top = 96 * low + 16 * j
                    block = values[top : top + 16, lane : lane + width].astype(bf16)
                    at = pl.multiple_of((6 + j) * ITEM_ROWS + place, 16)
                    terms[pl.ds(at, 16), lane : lane + width] = block
        pl.when(c == 1)(functools.partial(tick, 6))
        return carry

    lax.fori_loop(0, 4, weight_fc2, 0)
    tick(7)

    vec_ref[...] = jnp.zeros(vec_ref.shape, f32)
    fb1_ref[1:8, :] = jnp.zeros((7, FF), f32)
    V_OB, V_LN2G, V_LN2B, V_FC2B = range(4)
    cs_ref[0] = jnp.zeros(cs_ref.shape[1:], f32)

    def add_vec(kind, values):
        vec_ref[kind : kind + 1, :] += column_sum(values)

    def second_back(t, carry):
        here = tile(t)
        unit, inverse = unit_of(slots[RES, here, :])
        tokp[here, :] = slots[ACC, here, :].astype(bf16)
        upstream = slots[GNT, here, :]
        grad_out = cot[here, :].astype(f32)
        add_vec(V_FC2B, grad_out)
        add_vec(V_LN2G, upstream * unit)
        add_vec(V_LN2B, upstream)
        scaled = upstream * gain_two
        grad = grad_out + inverse * (
            scaled
            - jnp.mean(scaled, axis=1, keepdims=True)
            - unit * jnp.mean(scaled * unit, axis=1, keepdims=True)
        )
        slots[RES, here, :] = grad
        low = grad.astype(bf16)
        nrm[here, :] = low
        add_vec(V_OB, low.astype(f32))
        return carry

    lax.fori_loop(0, 2, second_back, 0)
    tick(8)
    lax.fori_loop(2, row_tiles, second_back, 0)
    store_result = pltpu.make_async_copy(tokp, result_hbm.at[0], load_sem.at[0])
    store_result.start()
    tick(9)

    GQ = ACC

    def mixed_back(c, carry):
        cols = pl.ds(pl.multiple_of(c * wide, wide), wide)
        gm[:, cols] = dot_nt(nrm[...], wout[cols, :]).astype(bf16)
        mixed = slots[MIXED, :, cols].astype(bf16)
        wfc1[cols, :D] = dot_tn(mixed, nrm[...]).astype(bf16)
        return carry

    lax.fori_loop(0, D // wide, mixed_back, 0)
    def window(ref, first, count):
        block = first // 128 * 128
        shift = first - block
        wide_enough = 256 if shift + count > 128 else 128
        piece = ref[:, block : block + wide_enough]
        if shift:
            piece = pltpu.roll(piece, wide_enough - shift, 1)
        return piece[:, :128]

    small_order = GROUPS[0][0]
    for d in range(32):
        at = pl.multiple_of(16 * place_of(small_order, bits_of(d)), 16)
        small[pl.ds(at, 8), :] = window(vec_ref, 24 * d, 24)
        small[pl.ds(at + 8, 8), :] = window(fb1_ref, 96 * d, 96)

    def small_copy(stage):
        count = ITEM_ROWS >> stage
        return pltpu.make_async_remote_copy(
            src_ref=small.at[pl.ds(count, count)],
            dst_ref=small_in.at[pl.ds(LANDING[stage - 1], count)],
            send_sem=small_send.at[stage - 1],
            recv_sem=small_recv.at[stage - 1],
            device_id=across[small_order[stage - 1]],
            device_id_type=MESH,
        )

    def small_step(stage):
        small_copy(stage).wait()
        count = ITEM_ROWS >> stage
        came = small_in[LANDING[stage - 1] : LANDING[stage - 1] + count]
        small[:count] = small[:count] + came
        if stage < STAGES:
            small_copy(stage + 1).start()
            return
        out_small[:9, :] = small[:9, :]

    small_copy(1).start()

    def sums_copy(stage):
        return pltpu.make_async_remote_copy(
            src_ref=cs_ref.at[stage - 1],
            dst_ref=cs_in.at[stage - 1],
            send_sem=sums_send.at[stage - 1],
            recv_sem=sums_recv.at[stage - 1],
            device_id=across[small_order[stage - 1]],
            device_id_type=MESH,
        )

    def sums_step(stage):
        sums_copy(stage).wait()
        cs_ref[stage] = cs_ref[stage - 1] + cs_in[stage - 1]
        if stage < STAGES:
            sums_copy(stage + 1).start()

    tick(10)

    def backward_pair(part, hp):
        own = part == 0
        ref, key_at, value_at = (qkv, D, 2 * D) if own else (kvp, 0, D)
        kind = (F_OWN, F_A, F_B)[part]
        count = rows if own else part_rows
        first = 0 if own else (part - 1) * part_rows
        keys = pl.ds(first, count)
        col = aligned(hp * 128, 128)
        cols = pl.ds(col, 128)
        q = qkv[:, cols]
        q_t = q.T
        k = ref[keys, pl.ds(key_at + col, 128)]
        v = ref[keys, pl.ds(value_at + col, 128)]
        grad_in = gm[:, cols].astype(f32)
        scaled = grad_in * slots[kind, :, cols]
        weighted = scaled * slots[MIXED, :, cols]
        scaled = scaled.astype(bf16)
        scaled_t = scaled.T
        grad_q = None
        grad_k, grad_v = [], []
        for h in range(2):
            delta = jnp.sum(half(weighted, h), axis=1, keepdims=True)
            e = ering[hp, h, :, first : first + count]
            grad_probs = dot_nt(scaled, half(v, h))
            grad_scores = (e.astype(f32) * (grad_probs - delta)).astype(bf16)
            term = dot(grad_scores, half(k, h))
            grad_q = term if grad_q is None else grad_q + term
            grad_k.append(dot(q_t[64 * h : 64 * h + 64], grad_scores))
            grad_v.append(dot(scaled_t[64 * h : 64 * h + 64], e))
        grad_k = jnp.concatenate(grad_k, axis=0).T.astype(bf16)
        grad_v = jnp.concatenate(grad_v, axis=0).T.astype(bf16)
        ref[keys, pl.ds(key_at + col, 128)] = grad_k
        ref[keys, pl.ds(value_at + col, 128)] = grad_v
        if part == 1:
            slots[GQ, :, cols] = grad_q
        elif part == 2:
            slots[GQ, :, cols] += grad_q
        else:
            total_q = (slots[GQ, :, cols] + grad_q) * score_scale
            qkv[:, cols] = total_q.astype(bf16)

    store_result.wait()
    send_gn = []
    for part in (1, 2):
        first = (part - 1) * part_rows
        here = pl.ds(first, part_rows)

        def twin_step(i, carry):
            for p in range(TWIN_UNROLL):
                backward_pair(part, TWIN_UNROLL * i + p)

            @pl.when(i == PAIRS // TWIN_UNROLL // 2 - 1)
            def _():
                tick(2 * part + 9)

            return carry

        lax.fori_loop(0, PAIRS // TWIN_UNROLL, twin_step, 0)
        if part == 2:
            for hp in range(PAIRS):
                e_in(hp).start()

        def partial_out(c, carry):
            cols = pl.ds(pl.multiple_of(c * wide, wide), wide)
            tokp[here, cols] = dot_nt(kvp[here, :], wqkv[cols, D : 3 * D]).astype(bf16)
            return carry

        lax.fori_loop(0, D // wide, partial_out, 0)
        for c in range(3):
            cols = pl.ds(wide * c, wide)
            sem = 2 + 3 * (part - 1) + c
            send_gn.append(to_twin(sem, tokp.at[here, cols], gn_in.at[here, cols]))
        tick(2 * part + 10)
        send_gn[part - 1].start()
        small_step(part)

    def own_step(hp, carry):
        e_in(hp).wait()
        backward_pair(0, hp)
        col = pl.multiple_of(hp * 128, 128)
        grad_q = qkv[:, pl.ds(col, 128)]
        own = jnp.concatenate(
            [qkv[:, pl.ds(D + col, 128)], qkv[:, pl.ds(2 * D + col, 128)]], axis=1
        )
        other = jnp.concatenate(
            [kvp[:, pl.ds(col, 128)], kvp[:, pl.ds(D + col, 128)]], axis=1
        )
        sum_kv = column_sum(own.astype(f32) + other.astype(f32))
        cs_ref[0, 0:1, pl.ds(col, 128)] = column_sum(grad_q.astype(f32))
        cs_ref[0, 1:2, pl.ds(col, 128)] = sum_kv[:, :128]
        cs_ref[0, 2:3, pl.ds(col, 128)] = sum_kv[:, 128:]
        weight_kv = dot(unit_t[...], jnp.concatenate([own, other], axis=0))
        weight_q = dot(unit_t[:, :rows], grad_q)
        weight_o = wfc1[:, pl.ds(col, 128)].astype(f32)
        put_24(12 + hp, jnp.concatenate([weight_kv, weight_q, weight_o], axis=1))
        tick(15 + hp, 15, 20)
        for c in range(4):
            pl.when(hp == c)(send_gn[2 + c].start)
        for c in range(3):
            pl.when(hp == 2 * c + 1)(functools.partial(small_step, 3 + c))
        return carry

    lax.fori_loop(0, PAIRS, own_step, 0)

    def first_back_product(c, carry):
        cols = pl.ds(pl.multiple_of(c * wide, wide), wide)
        slots[GNT, :, cols] = dot_nt(qkv[...], wqkv[cols, :])
        return carry

    sums_copy(1).start()
    gain_one = row(ln1_gain)

    def first_back(t, carry):
        here = tile(t)
        unit, inverse = unit_of(tok[here, :].astype(f32))
        upstream = slots[GNT, here, :] + gn_in[here, :].astype(f32)
        scaled = upstream * gain_one
        grad = slots[RES, here, :] + inverse * (
            scaled
            - jnp.mean(scaled, axis=1, keepdims=True)
            - unit * jnp.mean(scaled * unit, axis=1, keepdims=True)
        )
        gm[here, :] = grad.astype(bf16)
        return carry

    store_gtok = pltpu.make_async_copy(gm, gtok_hbm.at[0], load_sem.at[2])
    last_start = STARTS[-1]
    product_at = last_start + 1
    tokens_at = product_at + D // wide

    def late_tick(number, carry):
        tick(number, last_start + 1, last_start + ENDS[-1])
        for i, since in enumerate(SUMS_AT):
            pl.when(number == last_start + since)(functools.partial(sums_step, 1 + i))

        @pl.when(number < tokens_at)
        def _():
            first_back_product(number - product_at, 0)

        @pl.when(number == tokens_at)
        def _():
            for copy in send_gn:
                copy.wait()

        @pl.when((number >= tokens_at) & (number < tokens_at + row_tiles))
        def _():
            first_back(number - tokens_at, 0)

        pl.when(number == tokens_at + row_tiles)(store_gtok.start)
        return carry

    lax.fori_loop(last_start + 1, last_start + ENDS[-1] + 1, late_tick, 0)

    me = seq * 2 + blk
    low_row = me * 24 // 16 * 16
    weights = wqkv[pl.ds(pl.multiple_of(low_row, 16), 32), :].astype(f32)
    weights = jnp.where(me * 24 == low_row, weights[:24], weights[8:])
    sums = cs_ref[STAGES]
    lanes = lax.broadcasted_iota(jnp.int32, (24, D), 1)
    mine = lanes == me * 24 + lax.broadcasted_iota(jnp.int32, (24, D), 0)

    def my_column(values):
        return jnp.sum(jnp.where(mine, values, 0.0), axis=1, keepdims=True)

    gain_mine, bias_mine = my_column(row(ln1_gain)), my_column(row(ln1_bias))
    gain_sum = jnp.zeros((24, 1), f32)
    bias_sum = jnp.zeros((24, 1), f32)
    for kind in range(3):
        cols = slice(kind * D, (kind + 1) * D)
        product = out_qkv[:, cols]
        total = sums[kind : kind + 1, :]
        gain_sum += jnp.sum(weights[:, cols] * product, axis=1, keepdims=True)
        bias_sum += jnp.sum(weights[:, cols] * total, axis=1, keepdims=True)
        out_qkv[:, cols] = gain_mine * product + bias_mine * total
    diagonal = lax.broadcasted_iota(jnp.int32, (24, 128), 0) == lax.broadcasted_iota(
        jnp.int32, (24, 128), 1
    )
    for kind, values in enumerate(
        (gain_sum, bias_sum, my_column(sums[0:1]), my_column(sums[2:3]))
    ):
        line = column_sum(jnp.where(diagonal, values, 0.0))
        out_small[9 + kind : 10 + kind, :] = line
    store_gtok.wait()


SMALL_ROWS = ((2, 9), (3, 10), (5, 11), (6, 12), (8, 0), (9, 1), (10, 2), (12, 8), (14, 3))
LARGE = (0, 1, 4, 7, 11, 13)


def hand_on(*refs):
    large, small, outs = refs[:6], refs[6], refs[7:22]
    for ref, at in zip(large, LARGE):
        outs[at][...] = ref[...]
    for at, line in SMALL_ROWS:
        outs[at][...] = small[line, : outs[at].shape[0]]


def block_body(
    tokens,
    lengths,
    padding,
    cotangent,
    ln1_gain,
    ln1_bias,
    w_qkv,
    q_bias,
    v_bias,
    w_out,
    out_bias,
    ln2_gain,
    ln2_bias,
    w_fc1,
    fc1_bias,
    w_fc2,
    fc2_bias,
):
    rows = tokens.shape[1]
    n_dev = lax.axis_size("seq") * lax.axis_size("blk")
    shape = jax.ShapeDtypeStruct
    any_spec = pl.BlockSpec(memory_space=pl.ANY)
    vmem = pl.BlockSpec(memory_space=pltpu.VMEM)
    smem = pl.BlockSpec(memory_space=pltpu.SMEM)
    part = D // n_dev
    line = shape((part,), f32)
    outs = pl.pallas_call(
        block_kernel,
        name="block",
        out_shape=(
            shape((1, rows, D), bf16),
            shape((1, rows, D), bf16),
            shape((part, 3 * D), f32),
            shape((part, D), f32),
            shape((part, FF), f32),
            shape((FF // n_dev, D), f32),
            shape((16, 128), f32),
            shape((PAIRS, 2, rows, rows), bf16),
        ),
        in_specs=[
            any_spec, smem, vmem, any_spec, vmem, vmem, any_spec, vmem, vmem,
            any_spec, vmem, vmem, vmem, any_spec, vmem, any_spec, vmem,
        ],
        out_specs=(any_spec,) * 2 + (vmem,) * 5 + (any_spec,),
        scratch_shapes=[
            pltpu.VMEM((D, 3 * D), bf16),
            pltpu.VMEM((D, D), bf16),
            pltpu.VMEM((D, FF), bf16),
            pltpu.VMEM((rows, D), bf16),
            pltpu.VMEM((rows, D), bf16),
            pltpu.VMEM((rows, D), bf16),
            pltpu.VMEM((rows, D), bf16),
            pltpu.VMEM((D, 2 * rows), bf16),
            pltpu.VMEM((D, rows), bf16),
            pltpu.VMEM((rows, 3 * D), bf16),
            pltpu.VMEM((rows, 2 * D), bf16),
            pltpu.VMEM((rows, D), bf16),
            pltpu.VMEM((rows, rows), f32),
            pltpu.VMEM((PAIRS, 2, rows, rows), bf16),
            pltpu.VMEM((7, rows, D), f32),
            pltpu.VMEM((ITEMS * ITEM_ROWS, ITEM_LANES), bf16),
            pltpu.VMEM((SLOTS * LANDING_ROWS, ITEM_LANES), bf16),
            pltpu.VMEM((rows, D), bf16),
            pltpu.VMEM((2, 8, rows), jnp.int32),
            pltpu.VMEM((8, D), f32),
            pltpu.VMEM((8, FF), f32),
            pltpu.VMEM((ITEM_ROWS, 128), f32),
            pltpu.VMEM((LANDING_ROWS, 128), f32),
            pltpu.VMEM((STAGES + 1, 8, D), f32),
            pltpu.VMEM((STAGES, 8, D), f32),
            pltpu.SemaphoreType.DMA((6,)),
            pltpu.SemaphoreType.DMA((PAIRS,)),
            pltpu.SemaphoreType.DMA((9,)),
            pltpu.SemaphoreType.DMA((9,)),
            pltpu.SemaphoreType.DMA((SLOTS * STAGES * len(GROUPS),)),
            pltpu.SemaphoreType.DMA((SLOTS * STAGES * len(GROUPS),)),
            pltpu.SemaphoreType.DMA((STAGES,)),
            pltpu.SemaphoreType.DMA((STAGES,)),
            pltpu.SemaphoreType.DMA((STAGES,)),
            pltpu.SemaphoreType.DMA((STAGES,)),
        ],
        compiler_params=pltpu.CompilerParams(
            collective_id=0, has_side_effects=True, vmem_limit_bytes=VMEM_LIMIT
        ),
        cost_estimate=pl.CostEstimate(
            flops=30 * 10**9, bytes_accessed=60 * 10**6, transcendentals=10**7
        ),
    )(
        tokens, lengths, padding, cotangent, ln1_gain, ln1_bias, w_qkv, q_bias, v_bias,
        w_out, out_bias, ln2_gain, ln2_bias, w_fc1, fc1_bias, w_fc2, fc2_bias,
    )
    final = (
        outs[0], outs[1], line, line, outs[2], line, line, outs[3], line, line, line, outs[4],
        shape((FF // n_dev,), f32), outs[5], line,
    )
    return pl.pallas_call(
        hand_on,
        name="hand_on",
        out_shape=tuple(shape(o.shape, o.dtype) for o in final),
        in_specs=[vmem] * 7,
        out_specs=(vmem,) * 15,
    )(*outs[:7])


VMEM_LIMIT = 63 * 2**20


def solution(mesh):
    in_specs = (
        P("seq", "blk", None),
        P("seq", None),
        P("seq", "blk"),
        P("seq", "blk", None),
        P(),
        P(),
        P(),
        P(),
        P(),
        P(),
        P(),
        P(),
        P(),
        P(),
        P(),
        P(),
        P(),
    )
    out_specs = (
        P("seq", "blk", None),
        P("seq", "blk", None),
        P(("seq", "blk")),
        P(("seq", "blk")),
        P(("seq", "blk"), None),
        P(("seq", "blk")),
        P(("seq", "blk")),
        P(("seq", "blk"), None),
        P(("seq", "blk")),
        P(("seq", "blk")),
        P(("seq", "blk")),
        P(("seq", "blk"), None),
        P(("seq", "blk")),
        P(("seq", "blk"), None),
        P(("seq", "blk")),
    )
    step = block_body if fits(mesh) else body
    return jax.shard_map(step, mesh=mesh, in_specs=in_specs, out_specs=out_specs, check_vma=False)
```
